128 devices in a mesh: dp: 8 (over x, core), tensor: 16 (over z, y).
Axes of the slice: x: 4, y: 4, z: 4, core: 2. Of those that a mesh axis runs over, the one named last changes fastest.
Arguments:
- hidden: bfloat16 [8192, 8192], P('dp', 'tensor'), may hold values from -6 to 6
- exited: int32 [128], P('dp'), may hold values from 0 to 1, as said below
- destination: int32 [128], P('dp'), may hold values from 0 to 7, as said below
- norm_gain: float32 [8192], replicated, may hold values from 0.25 to 1.75
- query_weight: bfloat16 [8192, 8192], P('dp', 'tensor'), may hold values from -0.0625 to 0.0625
- keyvalue_weight: bfloat16 [8192, 2048], P('dp', 'tensor'), may hold values from -0.0625 to 0.0625
- output_weight: bfloat16 [8192, 8192], P('tensor', 'dp'), may hold values from -0.0625 to 0.0625
Outputs:
- updated: bfloat16 [3072, 8192], P('dp', 'tensor')
The draws below stay inside these ranges and needn't reach their ends.
Inputs may be any that keep to these rules, and one draw needn't show every extreme that they name: In the 16 items of each data group at most 12 have exited = 0, and in some group exactly 12. `destination`: only read where exited = 0. Each data group is named by exactly 6 remaining items over all groups, and by at most 2 remaining items of one data group, a bound reached in every draw.
All inputs are finite; a program needn't handle non-finite values.
Results may differ from the reference program's by a relative error of at most 0.011.
Values may be sent and summed in bfloat16 or wider, within the bound.
A program may use at most 128 MiB of HBM per device.

```python
import jax
import jax.numpy as jnp
from jax import lax

D = 8192
H = 64
KV = 8
HD = 128
ITEM_LEN = 64
INCOMING_BATCH = 16
ITEMS = 128
SMAX = 12
RECV = 6
SLOT = 2
N_DP = 8
N_TENSOR = 16


def continuing_arrangement(key):
    heavy = jax.random.randint(jax.random.fold_in(key, 11), (), 0, N_DP)
    floor_share = SMAX // N_DP
    column_rank = jax.random.permutation(jax.random.fold_in(key, 12), N_DP)
    heavy_count = floor_share + (column_rank < SMAX % N_DP).astype(jnp.int32)
    pool_size = N_DP * floor_share
    column_keys = jax.random.split(jax.random.fold_in(key, 13), N_DP)
    column_perms = jax.vmap(lambda single: jax.random.permutation(single, pool_size))(column_keys)
    pool_row = jnp.arange(pool_size) // floor_share
    logit_scores = column_perms + jnp.where(pool_row == heavy, pool_size, 0)[None, :]
    ranks = jnp.argsort(jnp.argsort(logit_scores, axis=1), axis=1)
    picked = (ranks < (RECV - heavy_count)[:, None]).astype(jnp.int32)
    lighter_tallies = picked.reshape(N_DP, N_DP, floor_share).sum(axis=2).T
    row_ids = jnp.arange(N_DP)
    counts = jnp.where(row_ids[:, None] == heavy, heavy_count[None, :], lighter_tallies)
    slot_numbers = jnp.arange(INCOMING_BATCH)
    slot_dest = jnp.minimum(slot_numbers // SLOT, N_DP - 1)
    slot_within = slot_numbers % SLOT
    slot_valid = slot_numbers < N_DP * SLOT
    slot_live = slot_valid[None, :] & (slot_within[None, :] < counts[:, slot_dest])
    item_keys = jax.random.split(jax.random.fold_in(key, 14), N_DP)
    item_perms = jax.vmap(lambda single: jax.random.permutation(single, INCOMING_BATCH))(item_keys)
    alive = jnp.take_along_axis(slot_live, item_perms, axis=1)
    target = jnp.minimum(item_perms // SLOT, N_DP - 1)
    filler = jax.random.randint(jax.random.fold_in(key, 15), (N_DP, INCOMING_BATCH), 0, N_DP)
    chosen_dest = jnp.where(alive, target, filler)
    return ((1 - alive.astype(jnp.int32)).reshape(-1).astype(jnp.int32), chosen_dest.reshape(-1).astype(jnp.int32))


def draw_exited(key, part):
    return continuing_arrangement(key)[0]


def draw_destination(key, part):
    return continuing_arrangement(key)[1]


def shard_levels(key, dims, pieces, least, largest):
    factor_of = 1.0
    for axis_at, shards_of in pieces:
        steps = jax.random.uniform(jax.random.fold_in(jax.random.fold_in(key, 6), axis_at), (shards_of,), jnp.float32, least / len(pieces), largest / len(pieces))
        factor_of = factor_of * jnp.repeat(jnp.exp(steps), dims[axis_at] // shards_of).reshape((-1,) + (1,) * (len(dims) - 1 - axis_at))
    return factor_of


def normal_values(stream_key, shape, scale, reach, pieces=(), kind=jnp.bfloat16):
    drawn = scale * jax.random.normal(stream_key, shape, jnp.float32)
    if pieces:
        drawn = drawn * shard_levels(stream_key, shape, pieces, -0.22, 0.18)
    return jnp.clip(drawn, -reach, reach).astype(kind)


def setup_inputs(seed: int = 0) -> dict:
    key_of = jax.random.split(jax.random.key(seed), 8)
    return {
        "hidden": normal_values(key_of[0], (ITEMS * ITEM_LEN, D), 1.0, 6.0, ((0, 8), (1, 16))),
        "exited": draw_exited(jax.random.fold_in(key_of[7], 71), 0),
        "destination": draw_destination(jax.random.fold_in(key_of[7], 71), 0),
        "norm_gain": jnp.clip(1.0 + 0.15 * jax.random.normal(key_of[3], (D,), jnp.float32), 0.25, 1.75),
        "query_weight": normal_values(key_of[4], (D, D), D ** -0.5, 0.0625, ((0, 8), (1, 16))),
        "keyvalue_weight": normal_values(key_of[5], (D, 2 * KV * HD), D ** -0.5, 0.0625, ((0, 8), (1, 16))),
        "output_weight": normal_values(key_of[6], (D, D), D ** -0.5, 0.0625, ((0, 16), (1, 8))),
    }


EPSILON = 1e-05
THETA = 500000.0

def rotate(values, sequence_places):
    halfway = values.shape[-1] // 2
    freq_scale = THETA ** (-(jnp.arange(halfway, dtype=jnp.float32) * 2.0 / values.shape[-1]))
    rotary_phases = sequence_places[..., None] * freq_scale
    cosine = jnp.cos(rotary_phases)
    sine = jnp.sin(rotary_phases)
    first_half = values[..., :halfway]
    second_half = values[..., halfway:]
    return jnp.concatenate([first_half * cosine - second_half * sine, second_half * cosine + first_half * sine], axis=-1)

def reference(hidden, exited, destination, norm_gain, query_weight, keyvalue_weight, output_weight):
    item_ids = jnp.arange(ITEMS, dtype=jnp.int32)
    sort_keys = jnp.where(exited == 0, destination * ITEMS + item_ids, N_DP * ITEMS + item_ids)
    chosen = jnp.argsort(sort_keys)[:N_DP * RECV].astype(jnp.int32)
    block = jnp.take(hidden.reshape(ITEMS, ITEM_LEN, D), chosen, axis=0).reshape(N_DP * RECV * ITEM_LEN, D)
    row_count = block.shape[0]
    item_count = N_DP * RECV
    widened = block.astype(jnp.float32)
    scale_inv = lax.rsqrt(lax.optimization_barrier(jnp.mean(widened * widened, axis=1, keepdims=True)) + EPSILON)
    rescaled_hidden = (widened * scale_inv * norm_gain[None, :]).astype(jnp.bfloat16)
    sequence_places = jnp.arange(ITEM_LEN).astype(jnp.float32)
    query_accumulated = jnp.dot(rescaled_hidden, query_weight, preferred_element_type=jnp.float32)
    request_vectors = rotate(query_accumulated.reshape(item_count, ITEM_LEN, H, HD), sequence_places[:, None]).astype(jnp.bfloat16)
    keyvalue_sum = jnp.dot(rescaled_hidden, keyvalue_weight, preferred_element_type=jnp.float32)
    keyvalue_sum = keyvalue_sum.reshape(item_count, ITEM_LEN, KV, 2, HD)
    keys_part = rotate(keyvalue_sum[:, :, :, 0, :], sequence_places[:, None]).astype(jnp.bfloat16)
    values_part = keyvalue_sum[:, :, :, 1, :].astype(jnp.bfloat16)
    keys_wide = jnp.repeat(keys_part, H // KV, axis=2)
    values_wide = jnp.repeat(values_part, H // KV, axis=2)
    logit_scores = jnp.einsum('nlhd,nmhd->nhlm', request_vectors.astype(jnp.float32), keys_wide.astype(jnp.float32)) * HD ** (-0.5)
    causal = jnp.arange(ITEM_LEN)[:, None] >= jnp.arange(ITEM_LEN)[None, :]
    logit_scores = jnp.where(causal[None, None], logit_scores, -1e+30)
    highest = lax.optimization_barrier(jnp.max(logit_scores, axis=-1, keepdims=True))
    raised = jnp.exp(logit_scores - highest)
    probs = (raised / lax.optimization_barrier(jnp.sum(raised, axis=-1, keepdims=True))).astype(jnp.bfloat16)
    context = jnp.einsum('nhlm,nmhd->nlhd', probs.astype(jnp.float32), values_wide.astype(jnp.float32)).astype(jnp.bfloat16)
    context = context.reshape(row_count, D)
    group_width = D // N_TENSOR
    context_groups = context.reshape(row_count, N_TENSOR, group_width).transpose(1, 0, 2)
    weight_groups = output_weight.reshape(N_TENSOR, group_width, D)

    def add_group(total, pair):
        partial_term = jnp.dot(pair[0], pair[1], preferred_element_type=jnp.float32)
        rounded = lax.optimization_barrier(partial_term.astype(jnp.bfloat16))
        return (total + rounded.astype(jnp.float32), None)
    summed, unused = lax.scan(add_group, jnp.zeros((row_count, D), jnp.float32), (context_groups, weight_groups))
    return (widened + summed).astype(jnp.bfloat16)
```

```python
import jax
import jax.numpy as jnp
from jax import lax
from jax.sharding import PartitionSpec as P

HD = 128
ITEM_LEN = 64


EPSILON = 1e-05
THETA = 500000.0


def swapped(value, axis, stride):
    return lax.ppermute(value, axis, [(i, i ^ 1 << stride) for i in range(lax.axis_size(axis))])


def rotate(values, sequence_places):
    halfway = values.shape[-1] // 2
    freq_scale = THETA ** (-(jnp.arange(halfway, dtype=jnp.float32) * 2.0 / values.shape[-1]))
    rotary_phases = sequence_places[..., None] * freq_scale
    cosine = jnp.cos(rotary_phases)
    sine = jnp.sin(rotary_phases)
    first_half = values[..., :halfway]
    second_half = values[..., halfway:]
    return jnp.concatenate(
        [first_half * cosine - second_half * sine, second_half * cosine + first_half * sine],
        axis=-1,
    )


def attend(request_vectors, keys_part, values_part):
    logit_scores = jnp.einsum(
        "nlhd,nmd->nhlm", request_vectors, keys_part, preferred_element_type=jnp.float32
    )
    logit_scores = logit_scores * request_vectors.shape[-1] ** (-0.5)
    length = request_vectors.shape[1]
    causal = jnp.arange(length)[:, None] >= jnp.arange(length)[None, :]
    logit_scores = jnp.where(causal[None, None], logit_scores, -1e30)
    highest = jnp.max(logit_scores, axis=-1, keepdims=True)
    raised = jnp.exp(logit_scores - highest)
    probs = (raised / jnp.sum(raised, axis=-1, keepdims=True)).astype(jnp.bfloat16)
    return jnp.einsum(
        "nhlm,nmd->nlhd", probs, values_part, preferred_element_type=jnp.float32
    ).astype(jnp.bfloat16)


def attention_layer(block_rows, norm_gain, query_weight, keyvalue_weight, output_weight):
    row_count = block_rows.shape[0]
    gathered = lax.all_gather(block_rows, "tensor", axis=1, tiled=True)
    widened = gathered.astype(jnp.float32)
    scale_inv = lax.rsqrt(jnp.mean(widened * widened, axis=1, keepdims=True) + EPSILON)
    rescaled_hidden = (widened * scale_inv * norm_gain[None, :]).astype(jnp.bfloat16)
    query_accumulated = jnp.dot(
        rescaled_hidden,
        lax.all_gather(query_weight, "dp", axis=0, tiled=True),
        preferred_element_type=jnp.float32,
    )
    keyvalue_sum = jnp.dot(
        rescaled_hidden,
        lax.all_gather(keyvalue_weight, "dp", axis=0, tiled=True),
        preferred_element_type=jnp.float32,
    )
    sequence_places = (jnp.arange(row_count) % ITEM_LEN).astype(jnp.float32)
    head_count = query_weight.shape[1] // HD
    request_vectors = rotate(
        query_accumulated.reshape(row_count, head_count, HD), sequence_places[:, None]
    ).astype(jnp.bfloat16)
    parity = lax.axis_index("tensor") % 2
    rotated = rotate(keyvalue_sum, sequence_places).astype(jnp.bfloat16)
    own_part = jnp.where(parity == 0, rotated, keyvalue_sum.astype(jnp.bfloat16))
    partner = swapped(own_part, "tensor", 0)
    keys_part = jnp.where(parity == 0, own_part, partner)
    values_part = jnp.where(parity == 0, partner, own_part)
    item_count = row_count // ITEM_LEN
    context = attend(
        request_vectors.reshape(item_count, ITEM_LEN, head_count, HD),
        keys_part.reshape(item_count, ITEM_LEN, HD),
        values_part.reshape(item_count, ITEM_LEN, HD),
    )
    context = context.reshape(row_count, head_count * HD)
    terms = jnp.dot(
        context,
        lax.all_gather(output_weight, "dp", axis=1, tiled=True),
        preferred_element_type=jnp.float32,
    )
    summed = lax.psum_scatter(
        terms.astype(jnp.bfloat16), "tensor", scatter_dimension=1, tiled=True
    ).astype(jnp.float32)
    return (block_rows.astype(jnp.float32) + summed).astype(jnp.bfloat16)


def compact_received(received, received_flags, keep_count):
    flag_integers = received_flags.astype(jnp.int32)
    before = jnp.cumsum(flag_integers) - flag_integers
    picker = (jnp.arange(keep_count)[:, None] == before[None, :]) & (flag_integers[None, :] == 1)
    return jnp.dot(
        picker.astype(jnp.bfloat16), received, preferred_element_type=jnp.float32
    ).astype(jnp.bfloat16)


def shards(hidden, exited, destination, norm_gain, query_weight, keyvalue_weight, output_weight):
    group_number = lax.axis_size("dp")
    items_here = exited.shape[0]
    columns = hidden.shape[1]
    most_kept = 3 * items_here // 4
    taken = 3 * items_here // 8
    slot_cap = (most_kept + group_number - 1) // group_number
    capacity_sum = group_number * slot_cap
    staying = 1 - exited
    dest_onehot = (destination[:, None] == jnp.arange(group_number)[None, :]).astype(
        jnp.int32
    ) * staying[:, None]
    earlier = jnp.cumsum(dest_onehot, axis=0) - dest_onehot
    within = jnp.sum(earlier * dest_onehot, axis=1)
    slot_index = jnp.where(staying == 1, destination * slot_cap + within, -1)
    to_slot = jnp.arange(capacity_sum)[:, None] == slot_index[None, :]
    slot_flags = jnp.any(to_slot, axis=1).astype(jnp.bfloat16).reshape(group_number, slot_cap)
    item_rows = hidden.reshape(items_here, ITEM_LEN * columns)
    outgoing = jnp.dot(
        to_slot.astype(jnp.bfloat16), item_rows, preferred_element_type=jnp.float32
    ).astype(jnp.bfloat16)
    outgoing = outgoing.reshape(group_number, slot_cap, ITEM_LEN * columns)
    arrived, arrived_flags = (
        lax.all_to_all(outgoing, "dp", split_axis=0, concat_axis=0, tiled=True),
        lax.all_to_all(slot_flags, "dp", split_axis=0, concat_axis=0, tiled=True),
    )
    compact = compact_received(
        arrived.reshape(capacity_sum, ITEM_LEN * columns),
        arrived_flags.reshape(capacity_sum),
        taken,
    )
    return attention_layer(
        compact.reshape(taken * ITEM_LEN, columns),
        norm_gain,
        query_weight,
        keyvalue_weight,
        output_weight,
    )


def solution(mesh):
    placed = (
        P("dp", "tensor"),
        P("dp"),
        P("dp"),
        P(),
        P("dp", "tensor"),
        P("dp", "tensor"),
        P("tensor", "dp"),
    )
    return jax.shard_map(
        shards, mesh=mesh, in_specs=placed, out_specs=P("dp", "tensor"), check_vma=False
    )
```

```python
import functools

import jax
import jax.numpy as jnp
import numpy as np
from jax import lax
from jax.experimental import pallas as pl
from jax.experimental.pallas import tpu as pltpu
from jax.sharding import PartitionSpec as P

MESH = pl.DeviceIdType.MESH

HD = 128
ITEM_LEN = 64
HERE = 16
TAKEN = 6
ROWS = TAKEN * ITEM_LEN
WIDE = 512
DEPTH = 1024
EPSILON = 1e-05
THETA = 500000.0
BF = jnp.bfloat16
F32 = jnp.float32

PIECE = DEPTH // 4
HALF = ROWS // 2
QUARTER = ROWS // 4


def tables():
    j = np.arange(HD // 2, dtype=np.float64)
    freq = (THETA ** (-2.0 * j / HD)).astype(np.float32)
    phase = (np.arange(ITEM_LEN, dtype=np.float32)[:, None] * freq).astype(np.float64)
    cos, sin = np.cos(phase), np.sin(phase)
    return (
        np.concatenate([cos, cos], axis=1).astype(np.float32),
        np.concatenate([-sin, sin], axis=1).astype(np.float32),
    )


def kernel(
    exited, destination, hidden, gain, wq, wkv, wo, cos, sin, out,
    hid, outgoing, arrived, meta, meta_scalar, act, wbuf, obuf, acc, squares, qs, kvown, kvpart,
    ctx, part, r1, r2, s1, q1, q2,
    local_sem, meta_s, meta_r, route_s, route_r, x_s, x_r, ag_s, ag_r, rs_s, rs_r, kv_s, kv_r,
):
    me = lax.axis_index("dp")
    t = lax.axis_index("tensor")
    x, c = me // 2, me % 2
    z, y = t // 4, t % 4
    left = ((x + 3) % 4) * 2 + c
    right = ((x + 1) % 4) * 2 + c
    far = ((x + 2) % 4) * 2 + c
    zp, zm, zf = (z + 1) % 4, (z + 3) % 4, (z + 2) % 4
    yp, ym, yf = (y + 1) % 4, (y + 3) % 4, (y + 2) % 4

    def sibling(i):
        return i + 1 - 2 * c

    sib = sibling(me)

    started = []

    def put(src, dst, send, recv, device):
        copy = pltpu.make_async_remote_copy(
            src_ref=src, dst_ref=dst, send_sem=send, recv_sem=recv,
            device_id=device, device_id_type=MESH,
        )
        copy.start()
        started.append(copy)

    def got(dst, recv):
        pltpu.make_async_remote_copy(
            src_ref=dst, dst_ref=dst, send_sem=recv, recv_sem=recv,
            device_id=(sib, t), device_id_type=MESH,
        ).wait_recv()

    loads = [pltpu.make_async_copy(hidden, hid, local_sem.at[0])]
    loads.append(pltpu.make_async_copy(wq, wbuf.at[me, :, pl.ds(0, WIDE)], local_sem.at[1]))
    loads.append(pltpu.make_async_copy(wkv, wbuf.at[me, :, pl.ds(WIDE, HD)], local_sem.at[2]))
    for s in range(4):
        for h in range(2):
            loads.append(
                pltpu.make_async_copy(
                    wo.at[:, pl.ds(h * WIDE + s * HD, HD)],
                    obuf.at[s, me, :, pl.ds(h * HD, HD)],
                    local_sem.at[3 + 2 * s + h],
                )
            )
    for load in loads:
        load.start()

    barrier = pltpu.get_barrier_semaphore()
    peers = [((me + k) % 8, t) for k in range(1, 8)]
    peers += [(me, zp * 4 + y), (me, zm * 4 + y), (me, z * 4 + yp), (me, z * 4 + ym)]
    for peer in peers:
        pl.semaphore_signal(barrier, inc=1, device_id=peer, device_id_type=MESH)
    pl.semaphore_wait(barrier, len(peers))

    codes = [jnp.where(exited[k] == 0, destination[k], -1) for k in range(HERE)]
    lane = lax.broadcasted_iota(jnp.int32, (8, 128), 1)
    row = jnp.full((8, 128), -1, jnp.int32)
    for k in range(HERE):
        row = jnp.where(lane == k, codes[k], row)
    meta[me] = row
    for k in range(1, 8):
        put(meta.at[me], meta.at[me], meta_s.at[k], meta_r.at[k], ((me + k) % 8, t))

    loads[0].wait()
    for k in [4, 2, 6, 3, 5, 1, 7, 0]:
        dest = (me + k) % 8 if k else me
        seen = jnp.int32(0)
        first = jnp.int32(0)
        second = jnp.int32(0)
        for item in range(HERE):
            hit = codes[item] == dest
            first = jnp.where(hit & (seen == 0), item, first)
            second = jnp.where(hit & (seen == 1), item, second)
            seen = seen + jnp.where(hit, 1, 0)
        if k:
            outgoing[dest, 0] = hid[first]
            outgoing[dest, 1] = hid[second]
            put(outgoing.at[dest], arrived.at[me], route_s.at[k], route_r.at[k], (dest, t))
        else:
            arrived[me, 0] = hid[first]
            arrived[me, 1] = hid[second]
    for load in loads[1:]:
        load.wait()

    def weights(r, i, low=0, count=None):
        if r < 4:
            return wbuf.at[i, pl.ds(r * PIECE + low, count or PIECE), :]
        return obuf.at[r - 4, i, pl.ds(low, count or WIDE), :]

    def half_of(r):
        return PIECE // 2 if r < 4 else WIDE // 2

    def x_put(r, k, view, device):
        put(view, view, x_s.at[r, k], x_r.at[r, k], (device, t))

    def x_own_sibling(r):
        x_put(r, 4, weights(r, me), sib)

    def x_own(r):
        x_put(r, 0, weights(r, me), right)
        x_put(r, 1, weights(r, me), left)

    def x_near(r):
        n = half_of(r)
        got(weights(r, left), x_r.at[r, 0])
        x_put(r, 2, weights(r, left, 0, n), right)
        x_put(r, 5, weights(r, left), sib)
        got(weights(r, right), x_r.at[r, 1])
        x_put(r, 3, weights(r, right, n, n), left)
        x_put(r, 6, weights(r, right), sib)

    def x_far(r):
        n = half_of(r)
        got(weights(r, far, 0, n), x_r.at[r, 2])
        x_put(r, 7, weights(r, far, 0, n), sib)
        got(weights(r, far, n, n), x_r.at[r, 3])
        x_put(r, 8, weights(r, far, n, n), sib)

    def x_sibling(r):
        n = half_of(r)
        got(weights(r, sib), x_r.at[r, 4])
        got(weights(r, sibling(left)), x_r.at[r, 5])
        got(weights(r, sibling(right)), x_r.at[r, 6])
        got(weights(r, sibling(far), 0, n), x_r.at[r, 7])
        got(weights(r, sibling(far), n, n), x_r.at[r, 8])

    for r in range(8):
        x_own_sibling(r)

    for k in range(1, 8):
        got(meta.at[(me + 8 - k) % 8], meta_r.at[k])
    to_scalar = pltpu.make_async_copy(meta, meta_scalar, local_sem.at[11])
    to_scalar.start()
    to_scalar.wait()
    picks = [jnp.int32(0)] * TAKEN
    rank = jnp.int32(0)
    for j in range(8):
        count = jnp.int32(0)
        for item in range(HERE):
            count = count + jnp.where(meta_scalar[j, 0, item] == me, 1, 0)
        for s in range(2):
            valid = count > s
            for r in range(TAKEN):
                picks[r] = jnp.where(valid & (rank == r), 2 * j + s, picks[r])
            rank = rank + jnp.where(valid, 1, 0)

    for k in range(1, 8):
        got(arrived.at[(me + 8 - k) % 8], route_r.at[k])
    flat = arrived.reshape(16, ITEM_LEN, WIDE)
    for r in range(TAKEN):
        act[t, pl.ds(r * ITEM_LEN, ITEM_LEN), :] = flat[picks[r]]

    def line(half, phase):
        along_z = (half == 0) == (phase == 0)
        if along_z:
            return (z, zm, zp, zf), lambda a, b: a * 4 + b
        return (y, ym, yp, yf), lambda a, b: b * 4 + a

    def chunk(tt, half, low=0, count=HALF):
        return act.at[tt, pl.ds(half * HALF + low, count), :]

    def ag_put(half, k, view, device):
        put(view, view, ag_s.at[half, k], ag_r.at[half, k], (me, device))

    def other(half):
        return y if half == 0 else z

    def ag_send(half, phase, base, tt, near):
        (own, minus, plus, opposite), at = line(half, phase)
        place = other(half) if phase == 0 else near
        ag_put(half, base, chunk(tt, half), at(plus, place))
        ag_put(half, base + 1, chunk(tt, half), at(minus, place))

    def ag_near(half, phase, base, place):
        (own, minus, plus, opposite), at = line(half, phase)
        got(chunk(at(minus, place), half), ag_r.at[half, base])
        q = HALF // 2
        here = other(half) if phase == 0 else (z if half == 0 else y)
        ag_put(half, base + 2, chunk(at(minus, place), half, 0, q), at(plus, here))
        got(chunk(at(plus, place), half), ag_r.at[half, base + 1])
        ag_put(half, base + 3, chunk(at(plus, place), half, q, q), at(minus, here))

    def ag_far(half, phase, base, place):
        (own, minus, plus, opposite), at = line(half, phase)
        q = HALF // 2
        got(chunk(at(opposite, place), half, 0, q), ag_r.at[half, base + 2])
        got(chunk(at(opposite, place), half, q, q), ag_r.at[half, base + 3])

    def places(half):
        return (z, zm, zp, zf) if half == 0 else (y, ym, yp, yf)

    def first_at(half, a):
        return a * 4 + y if half == 0 else z * 4 + a

    def ag2_send(half, n):
        a = places(half)[n]
        ag_send(half, 1, 4 + 4 * n, first_at(half, a), places(half)[0])

    def ag2_near(half, n):
        ag_near(half, 1, 4 + 4 * n, places(half)[n])

    def ag2_far(half, n):
        ag_far(half, 1, 4 + 4 * n, places(half)[n])

    for half in range(2):
        ag_send(half, 0, 0, t, None)
    x_own(0)
    for half in range(2):
        ag2_send(half, 0)
    x_own(1)
    for half in range(2):
        ag_near(half, 0, 0, other(half))
        ag2_send(half, 1)
        ag2_send(half, 2)
    x_near(0)
    for half in range(2):
        ag_far(half, 0, 0, other(half))
        ag2_send(half, 3)
    for half in range(2):
        ag2_near(half, 0)
    x_far(0)
    x_own(2)
    x_near(1)
    for half in range(2):
        ag2_near(half, 1)
    for half in range(2):
        ag2_near(half, 2)
    x_far(1)
    x_own(3)
    x_near(2)
    for half in range(2):
        ag2_near(half, 3)
    for n in range(4):
        for half in range(2):
            ag2_far(half, n)

    acc[...] = jnp.zeros_like(acc)
    squares[...] = jnp.zeros_like(squares)

    def project(p):
        x_sibling(p)

        @pl.loop(0, 8)
        def _(i):
            tt = 2 * i + p // 2
            cols = pl.ds((p % 2) * PIECE, PIECE)
            rows = act[tt, :, cols].astype(F32)
            power = rows * rows
            squares[...] += power[:, :HD] + power[:, HD:]
            scaled = (rows * gain[tt, :, cols]).astype(BF)
            acc[...] += jnp.dot(
                scaled, wbuf[i, pl.ds(p * PIECE, PIECE), :], preferred_element_type=F32
            )

    project(0)
    x_far(2)
    x_own(4)
    x_near(3)
    project(1)
    project(2)
    x_far(3)
    x_own(5)
    x_near(4)
    project(3)

    def rotated(value):
        return value * cos[...] + pltpu.roll(value, HD // 2, 1) * sin[...]

    squares[:, :1] = lax.rsqrt(
        jnp.sum(squares[...], axis=1, keepdims=True) * (1.0 / (16 * WIDE)) + EPSILON
    )
    parity = t % 2

    @pl.loop(0, TAKEN)
    def _(n):
        rows = pl.ds(n * ITEM_LEN, ITEM_LEN)
        value = acc[rows, pl.ds(WIDE, HD)] * squares[rows, :1]
        kvown[rows, :] = jnp.where(parity == 0, rotated(value), value).astype(BF)

    put(kvown, kvpart, kv_s, kv_r, (me, t + 1 - 2 * parity))

    @pl.loop(0, TAKEN)
    def _(n):
        rows = pl.ds(n * ITEM_LEN, ITEM_LEN)
        inverse = squares[rows, :1]
        for h in range(4):
            value = acc[rows, pl.ds(h * HD, HD)] * inverse
            qs[n, pl.ds(h * ITEM_LEN, ITEM_LEN), :] = rotated(value).astype(BF)

    got(kvpart, kv_r)

    @pl.loop(0, TAKEN)
    def _(n):
        rows = pl.ds(n * ITEM_LEN, ITEM_LEN)
        mine, theirs = kvown[rows, :], kvpart[rows, :]
        keys = jnp.where(parity == 0, mine, theirs)
        values = jnp.where(parity == 0, theirs, mine)
        scores = lax.dot_general(
            qs[n], keys, (((1,), (1,)), ((), ())), preferred_element_type=F32
        ) * (HD ** -0.5)
        place = lax.broadcasted_iota(jnp.int32, scores.shape, 0) % ITEM_LEN
        scores = jnp.where(
            place >= lax.broadcasted_iota(jnp.int32, scores.shape, 1), scores, -1e30
        )
        raised = jnp.exp(scores - jnp.max(scores, axis=1, keepdims=True))
        probs = (raised * (1.0 / jnp.sum(raised, axis=1, keepdims=True))).astype(BF)
        context = jnp.dot(probs, values, preferred_element_type=F32).astype(BF)
        for h in range(4):
            ctx[rows, pl.ds(h * HD, HD)] = context[h * ITEM_LEN:(h + 1) * ITEM_LEN, :]

    def multiply(s):
        x_sibling(4 + s)

        @pl.loop(0, 4)
        def _(a):
            for b in range(2):
                term = jnp.dot(
                    ctx[...], obuf[s, 2 * a + b], preferred_element_type=F32
                ).astype(BF)
                part[s, a, 2 * b] = term[:, :HD]
                part[s, a, 2 * b + 1] = term[:, HD:]

    def rs_put(s, half, k, src, dst, device):
        put(src, dst, rs_s.at[s, half, k], rs_r.at[s, half, k], (me, device))

    A = (0, QUARTER)
    B = (QUARTER, QUARTER)

    def block(s, half, a, rows):
        low, count = rows
        span = pl.ds(half * HALF + low, count)
        if half == 0:
            return part.at[s, a, :, span, :]
        return part.at[s, :, a, span, :]

    def devices(half, phase):
        if (half == 0) == (phase == 0):
            return zp * 4 + y, zm * 4 + y
        return z * 4 + yp, z * 4 + ym

    def ends(half, phase):
        if (half == 0) == (phase == 0):
            return z, zm, zp, zf
        return y, ym, yp, yf

    def span(rows):
        return pl.ds(rows[0], rows[1])

    def send_first(s):
        for half in range(2):
            own, minus, plus, opposite = ends(half, 0)
            up, down = devices(half, 0)
            rs_put(s, half, 0, block(s, half, opposite, A), r1.at[s, half, 0], up)
            rs_put(s, half, 1, block(s, half, opposite, B), r1.at[s, half, 1], down)
            rs_put(s, half, 2, block(s, half, plus, B), r2.at[s, half, 0, :, span(B), :], up)
            rs_put(s, half, 3, block(s, half, minus, A), r2.at[s, half, 1, :, span(A), :], down)

    def add_first(s):
        for half in range(2):
            own, minus, plus, opposite = ends(half, 0)
            up, down = devices(half, 0)
            for side, (a, rows, device) in enumerate(((plus, A, up), (minus, B, down))):
                got(r1.at[s, half, side], rs_r.at[s, half, side])
                view = block(s, half, a, rows)
                view[...] = (view[...].astype(F32) + r1[s, half, side].astype(F32)).astype(BF)
                rs_put(s, half, 4 + side, view, r2.at[s, half, side, :, span(rows), :], device)

    def send_second(s):
        for half in range(2):
            own, minus, plus, opposite = ends(half, 0)
            got(r2.at[s, half, 0, :, span(B), :], rs_r.at[s, half, 2])
            got(r2.at[s, half, 1, :, span(A), :], rs_r.at[s, half, 3])
            got(r2.at[s, half, 0, :, span(A), :], rs_r.at[s, half, 4])
            got(r2.at[s, half, 1, :, span(B), :], rs_r.at[s, half, 5])
            view = block(s, half, own, (0, HALF))
            s1[s, half] = (
                view[...].astype(F32) + r2[s, half, 0].astype(F32) + r2[s, half, 1].astype(F32)
            ).astype(BF)
            own, minus, plus, opposite = ends(half, 1)
            up, down = devices(half, 1)
            to = lambda a, rows: s1.at[s, half, a, span(rows), :]
            rs_put(s, half, 6, to(opposite, A), q1.at[s, half, 0], up)
            rs_put(s, half, 7, to(opposite, B), q1.at[s, half, 1], down)
            rs_put(s, half, 8, to(plus, B), q2.at[s, half, 0, span(B), :], up)
            rs_put(s, half, 9, to(minus, A), q2.at[s, half, 1, span(A), :], down)

    def add_second(s):
        for half in range(2):
            own, minus, plus, opposite = ends(half, 1)
            up, down = devices(half, 1)
            for side, (a, rows, device) in enumerate(((plus, A, up), (minus, B, down))):
                got(q1.at[s, half, side], rs_r.at[s, half, 6 + side])
                view = s1.at[s, half, a, span(rows), :]
                view[...] = (view[...].astype(F32) + q1[s, half, side].astype(F32)).astype(BF)
                rs_put(s, half, 10 + side, view, q2.at[s, half, side, span(rows), :], device)

    def finish(s):
        for half in range(2):
            own, minus, plus, opposite = ends(half, 1)
            got(q2.at[s, half, 0, span(B), :], rs_r.at[s, half, 8])
            got(q2.at[s, half, 1, span(A), :], rs_r.at[s, half, 9])
            got(q2.at[s, half, 0, span(A), :], rs_r.at[s, half, 10])
            got(q2.at[s, half, 1, span(B), :], rs_r.at[s, half, 11])
            rows, cols = pl.ds(half * HALF, HALF), pl.ds(s * HD, HD)
            out[rows, cols] = (
                act[t, rows, cols].astype(F32)
                + s1[s, half, own].astype(F32)
                + q2[s, half, 0].astype(F32)
                + q2[s, half, 1].astype(F32)
            ).astype(BF)

    x_far(4)
    x_own(6)
    x_near(5)
    multiply(0)
    send_first(0)
    x_far(5)
    x_own(7)
    x_near(6)
    add_first(0)
    multiply(1)
    send_first(1)
    send_second(0)
    add_first(1)
    x_far(6)
    x_near(7)
    add_second(0)
    multiply(2)
    send_first(2)
    send_second(1)
    add_first(2)
    x_far(7)
    finish(0)
    add_second(1)
    multiply(3)
    send_first(3)
    send_second(2)
    add_first(3)
    finish(1)
    add_second(2)
    send_second(3)
    finish(2)
    add_second(3)
    finish(3)

    for copy in started:
        copy.wait_send()


def shards(hidden, exited, destination, norm_gain, query_weight, keyvalue_weight, output_weight):
    cos, sin = tables()
    smem = pl.BlockSpec(memory_space=pltpu.SMEM)
    vmem = pl.BlockSpec(memory_space=pltpu.VMEM)
    hbm = pl.BlockSpec(memory_space=pl.ANY)
    dma = pltpu.SemaphoreType.DMA
    return pl.pallas_call(
        kernel,
        out_shape=jax.ShapeDtypeStruct((ROWS, WIDE), BF),
        in_specs=[smem, smem, hbm, vmem, hbm, hbm, hbm, vmem, vmem],
        out_specs=vmem,
        scratch_shapes=[
            pltpu.VMEM((HERE, ITEM_LEN, WIDE), BF),
            pltpu.VMEM((8, 2, ITEM_LEN, WIDE), BF),
            pltpu.VMEM((8, 2, ITEM_LEN, WIDE), BF),
            pltpu.VMEM((8, 8, 128), jnp.int32),
            pltpu.SMEM((8, 8, 128), jnp.int32),
            pltpu.VMEM((16, ROWS, WIDE), BF),
            pltpu.VMEM((8, DEPTH, WIDE + HD), BF),
            pltpu.VMEM((4, 8, WIDE, 2 * HD), BF),
            pltpu.VMEM((ROWS, WIDE + HD), F32),
            pltpu.VMEM((ROWS, HD), F32),
            pltpu.VMEM((TAKEN, 4 * ITEM_LEN, HD), BF),
            pltpu.VMEM((ROWS, HD), BF),
            pltpu.VMEM((ROWS, HD), BF),
            pltpu.VMEM((ROWS, WIDE), BF),
            pltpu.VMEM((4, 4, 4, ROWS, HD), BF),
            pltpu.VMEM((4, 2, 2, 4, QUARTER, HD), BF),
            pltpu.VMEM((4, 2, 2, 4, HALF, HD), BF),
            pltpu.VMEM((4, 2, 4, HALF, HD), BF),
            pltpu.VMEM((4, 2, 2, QUARTER, HD), BF),
            pltpu.VMEM((4, 2, 2, HALF, HD), BF),
            dma((12,)),
            dma((8,)),
            dma((8,)),
            dma((8,)),
            dma((8,)),
            dma((8, 9)),
            dma((8, 9)),
            dma((2, 20)),
            dma((2, 20)),
            dma((4, 2, 12)),
            dma((4, 2, 12)),
            dma(()),
            dma(()),
        ],
        compiler_params=pltpu.CompilerParams(
            collective_id=0, has_side_effects=True, vmem_limit_bytes=60 * 1024 * 1024
        ),
        cost_estimate=pl.CostEstimate(
            flops=2 * ROWS * 16 * WIDE * (2 * WIDE + HD),
            bytes_accessed=8 * 1024 * 1024,
            transcendentals=ROWS * 4 * ITEM_LEN,
        ),
    )(
        exited,
        destination,
        hidden.reshape(HERE, ITEM_LEN, WIDE),
        norm_gain.reshape(16, 1, WIDE),
        query_weight,
        keyvalue_weight,
        output_weight,
        jnp.asarray(cos),
        jnp.asarray(sin),
    )


def solution(mesh):
    placed = (
        P("dp", "tensor"),
        P("dp"),
        P("dp"),
        P(),
        P("dp", "tensor"),
        P("dp", "tensor"),
        P("tensor", "dp"),
    )
    return jax.shard_map(
        shards, mesh=mesh, in_specs=placed, out_specs=P("dp", "tensor"), check_vma=False
    )
```

```python
import functools

import jax
import jax.numpy as jnp
import numpy as np
from jax import lax
from jax.experimental import pallas as pl
from jax.experimental.pallas import tpu as pltpu
from jax.sharding import PartitionSpec as P

MESH = pl.DeviceIdType.MESH

HD = 128
ITEM_LEN = 64
HERE = 16
TAKEN = 6
ROWS = TAKEN * ITEM_LEN
WIDE = 512
DEPTH = 1024
EPSILON = 1e-05
THETA = 500000.0
BF = jnp.bfloat16
F32 = jnp.float32

PIECE = DEPTH // 4
HALF = ROWS // 2
QUARTER = ROWS // 4


def tables():
    j = np.arange(HD // 2, dtype=np.float64)
    freq = (THETA ** (-2.0 * j / HD)).astype(np.float32)
    phase = (np.arange(ITEM_LEN, dtype=np.float32)[:, None] * freq).astype(np.float64)
    cos, sin = np.cos(phase), np.sin(phase)
    return (
        np.concatenate([cos, cos], axis=1).astype(np.float32),
        np.concatenate([-sin, sin], axis=1).astype(np.float32),
    )


def kernel(
    exited, destination, hidden, gain_in, wq, wkv, wo, cos_in, sin_in, result,
    gain, cos, sin, out,
    hid, outgoing, arrived, meta, meta_scalar, act, scaled, wbuf, obuf, acc, squares, qs, kvown, kvpart,
    ctx, part, r1, r2, s1, q1, q2,
    local_sem, out_sem, meta_s, meta_r, route_s, route_r, x_s, x_r, ag_s, ag_r, rs_s, rs_r, kv_s, kv_r,
):
    me = lax.axis_index("dp")
    t = lax.axis_index("tensor")
    x, c = me // 2, me % 2
    z, y = t // 4, t % 4
    left = ((x + 3) % 4) * 2 + c
    right = ((x + 1) % 4) * 2 + c
    far = ((x + 2) % 4) * 2 + c
    zp, zm, zf = (z + 1) % 4, (z + 3) % 4, (z + 2) % 4
    yp, ym, yf = (y + 1) % 4, (y + 3) % 4, (y + 2) % 4

    def sibling(i):
        return i + 1 - 2 * c

    sib = sibling(me)

    started = []

    def put(src, dst, send, recv, device):
        copy = pltpu.make_async_remote_copy(
            src_ref=src, dst_ref=dst, send_sem=send, recv_sem=recv,
            device_id=device, device_id_type=MESH,
        )
        copy.start()
        started.append(copy)

    def got(dst, recv):
        pltpu.make_async_remote_copy(
            src_ref=dst, dst_ref=dst, send_sem=recv, recv_sem=recv,
            device_id=(sib, t), device_id_type=MESH,
        ).wait_recv()

    loads = [pltpu.make_async_copy(hidden, hid, local_sem.at[0])]
    loads.append(pltpu.make_async_copy(wq, wbuf.at[me, :, pl.ds(0, WIDE)], local_sem.at[1]))
    loads.append(pltpu.make_async_copy(wkv, wbuf.at[me, :, pl.ds(WIDE, HD)], local_sem.at[2]))
    for s in range(4):
        for h in range(2):
            loads.append(
                pltpu.make_async_copy(
                    wo.at[:, pl.ds(h * WIDE + s * HD, HD)],
                    obuf.at[s, me, :, pl.ds(h * HD, HD)],
                    local_sem.at[3 + 2 * s + h],
                )
            )
    loads.append(pltpu.make_async_copy(gain_in, gain, local_sem.at[12]))
    loads.append(pltpu.make_async_copy(cos_in, cos, local_sem.at[13]))
    loads.append(pltpu.make_async_copy(sin_in, sin, local_sem.at[14]))
    for load in loads:
        load.start()

    barrier = pltpu.get_barrier_semaphore()
    peers = [((me + k) % 8, t) for k in range(1, 8)]
    peers += [(me, zp * 4 + y), (me, zm * 4 + y), (me, z * 4 + yp), (me, z * 4 + ym)]
    for peer in peers:
        pl.semaphore_signal(barrier, inc=1, device_id=peer, device_id_type=MESH)
    pl.semaphore_wait(barrier, len(peers))

    def weights(r, i, low=0, count=None):
        if r < 4:
            return wbuf.at[i, pl.ds(r * PIECE + low, count or PIECE), :]
        return obuf.at[r - 4, i, pl.ds(low, count or WIDE), :]

    def half_of(r):
        return PIECE // 2 if r < 4 else WIDE // 2

    def x_put(r, k, view, device):
        put(view, view, x_s.at[r, k], x_r.at[r, k], (device, t))

    def x_own_sibling(r):
        x_put(r, 6, weights(r, me), sib)

    def x_own(r, which):
        n = half_of(r)
        x_put(r, 2 * which, weights(r, me, which * n, n), right)
        x_put(r, 2 * which + 1, weights(r, me, n - which * n, n), left)

    def x_hand_on(r):
        n = half_of(r)
        got(weights(r, left, 0, n), x_r.at[r, 0])
        x_put(r, 4, weights(r, left, 0, n), right)
        got(weights(r, right, n, n), x_r.at[r, 1])
        x_put(r, 5, weights(r, right, n, n), left)

    def x_near(r, *after):
        n = half_of(r)
        got(weights(r, left, n, n), x_r.at[r, 2])
        got(weights(r, right, 0, n), x_r.at[r, 3])
        for piece in after:
            x_own(*piece)
        x_put(r, 7, weights(r, left), sib)
        x_put(r, 8, weights(r, right), sib)

    def x_far(r, *after):
        n = half_of(r)
        got(weights(r, far, 0, n), x_r.at[r, 4])
        got(weights(r, far, n, n), x_r.at[r, 5])
        for piece in after:
            x_own(*piece)
        x_put(r, 9, weights(r, far, 0, n), sib)
        x_put(r, 10, weights(r, far, n, n), sib)

    def x_sibling(r):
        n = half_of(r)
        got(weights(r, sib), x_r.at[r, 6])
        got(weights(r, sibling(left)), x_r.at[r, 7])
        got(weights(r, sibling(right)), x_r.at[r, 8])
        got(weights(r, sibling(far), 0, n), x_r.at[r, 9])
        got(weights(r, sibling(far), n, n), x_r.at[r, 10])

    loads[1].wait()
    loads[2].wait()
    x_own(0, 0)
    for r in range(4):
        x_own_sibling(r)

    codes = [jnp.where(exited[k] == 0, destination[k], -1) for k in range(HERE)]
    lane = lax.broadcasted_iota(jnp.int32, (8, 128), 1)
    row = jnp.full((8, 128), -1, jnp.int32)
    for k in range(HERE):
        row = jnp.where(lane == k, codes[k], row)
    meta[me] = row
    for k in range(1, 8):
        put(meta.at[me], meta.at[me], meta_s.at[k], meta_r.at[k], ((me + k) % 8, t))

    loads[0].wait()
    for k in [4, 2, 6, 3, 5, 1, 7, 0]:
        dest = (me + k) % 8 if k else me
        seen = jnp.int32(0)
        first = jnp.int32(0)
        second = jnp.int32(0)
        for item in range(HERE):
            hit = codes[item] == dest
            first = jnp.where(hit & (seen == 0), item, first)
            second = jnp.where(hit & (seen == 1), item, second)
            seen = seen + jnp.where(hit, 1, 0)
        if k:
            outgoing[dest, 0] = hid[first]
            outgoing[dest, 1] = hid[second]
            put(outgoing.at[dest], arrived.at[me], route_s.at[k], route_r.at[k], (dest, t))
        else:
            arrived[me, 0] = hid[first]
            arrived[me, 1] = hid[second]
    for load in loads[3:11]:
        load.wait()
    for r in range(4, 8):
        x_own_sibling(r)

    for k in range(1, 8):
        got(meta.at[(me + 8 - k) % 8], meta_r.at[k])
    to_scalar = pltpu.make_async_copy(meta, meta_scalar, local_sem.at[11])
    to_scalar.start()
    to_scalar.wait()
    picks = [jnp.int32(0)] * TAKEN
    rank = jnp.int32(0)
    for j in range(8):
        count = jnp.int32(0)
        for item in range(HERE):
            count = count + jnp.where(meta_scalar[j, 0, item] == me, 1, 0)
        for s in range(2):
            valid = count > s
            for r in range(TAKEN):
                picks[r] = jnp.where(valid & (rank == r), 2 * j + s, picks[r])
            rank = rank + jnp.where(valid, 1, 0)

    for k in range(1, 8):
        got(arrived.at[(me + 8 - k) % 8], route_r.at[k])
    flat = arrived.reshape(16, ITEM_LEN, WIDE)
    for r in range(TAKEN):
        act[t, pl.ds(r * ITEM_LEN, ITEM_LEN), :] = flat[picks[r]]

    def line(half, phase):
        along_z = (half == 0) == (phase == 0)
        if along_z:
            return (z, zm, zp, zf), lambda a, b: a * 4 + b
        return (y, ym, yp, yf), lambda a, b: b * 4 + a

    def chunk(tt, half, low=0, count=HALF):
        return act.at[tt, pl.ds(half * HALF + low, count), :]

    def ag_put(half, k, view, device):
        put(view, view, ag_s.at[half, k], ag_r.at[half, k], (me, device))

    def other(half):
        return y if half == 0 else z

    def ag_send(half, phase, base, tt, near):
        (own, minus, plus, opposite), at = line(half, phase)
        place = other(half) if phase == 0 else near
        ag_put(half, base, chunk(tt, half), at(plus, place))
        ag_put(half, base + 1, chunk(tt, half), at(minus, place))

    def ag_near(half, phase, base, place):
        (own, minus, plus, opposite), at = line(half, phase)
        got(chunk(at(minus, place), half), ag_r.at[half, base])
        q = HALF // 2
        here = other(half) if phase == 0 else (z if half == 0 else y)
        ag_put(half, base + 2, chunk(at(minus, place), half, 0, q), at(plus, here))
        got(chunk(at(plus, place), half), ag_r.at[half, base + 1])
        ag_put(half, base + 3, chunk(at(plus, place), half, q, q), at(minus, here))

    def ag_far(half, phase, base, place):
        (own, minus, plus, opposite), at = line(half, phase)
        q = HALF // 2
        got(chunk(at(opposite, place), half, 0, q), ag_r.at[half, base + 2])
        got(chunk(at(opposite, place), half, q, q), ag_r.at[half, base + 3])

    def places(half):
        return (z, zm, zp, zf) if half == 0 else (y, ym, yp, yf)

    def first_at(half, a):
        return a * 4 + y if half == 0 else z * 4 + a

    def ag2_send(half, n):
        a = places(half)[n]
        ag_send(half, 1, 4 + 4 * n, first_at(half, a), places(half)[0])

    def ag2_near(half, n):
        ag_near(half, 1, 4 + 4 * n, places(half)[n])

    def ag2_far(half, n):
        ag_far(half, 1, 4 + 4 * n, places(half)[n])

    def rotated(value):
        return value * cos[...] + pltpu.roll(value, HD // 2, 1) * sin[...]

    parity = t % 2

    def project(p, low, count):
        @pl.loop(0, 8, step=2)
        def _(i):
            term = None
            for j in range(2):
                product = jnp.dot(
                    scaled[2 * (i + j) + p // 2, :, pl.ds((p % 2) * PIECE, PIECE)],
                    wbuf[i + j, pl.ds(p * PIECE, PIECE), pl.ds(low, count)],
                    preferred_element_type=F32,
                )
                term = product if term is None else term + product
            acc[:, pl.ds(low, count)] += term

    def multiply(s):
        x_sibling(4 + s)

        @pl.loop(0, 4)
        def _(a):
            for b in range(2):
                term = jnp.dot(
                    ctx[...], obuf[s, 2 * a + b], preferred_element_type=F32
                ).astype(BF)
                part[s, a, 2 * b] = term[:, :HD]
                part[s, a, 2 * b + 1] = term[:, HD:]

    def rs_put(s, half, k, src, dst, device):
        put(src, dst, rs_s.at[s, half, k], rs_r.at[s, half, k], (me, device))

    A = (0, QUARTER)
    B = (QUARTER, QUARTER)

    def block(s, half, a, rows):
        low, count = rows
        span = pl.ds(half * HALF + low, count)
        if half == 0:
            return part.at[s, a, :, span, :]
        return part.at[s, :, a, span, :]

    def devices(half, phase):
        if (half == 0) == (phase == 0):
            return zp * 4 + y, zm * 4 + y
        return z * 4 + yp, z * 4 + ym

    def ends(half, phase):
        if (half == 0) == (phase == 0):
            return z, zm, zp, zf
        return y, ym, yp, yf

    def span(rows):
        return pl.ds(rows[0], rows[1])

    def send_first(s):
        for half in range(2):
            own, minus, plus, opposite = ends(half, 0)
            up, down = devices(half, 0)
            rs_put(s, half, 0, block(s, half, opposite, A), r1.at[s, half, 0], up)
            rs_put(s, half, 1, block(s, half, opposite, B), r1.at[s, half, 1], down)
            rs_put(s, half, 2, block(s, half, plus, B), r2.at[s, half, 0, :, span(B), :], up)
            rs_put(s, half, 3, block(s, half, minus, A), r2.at[s, half, 1, :, span(A), :], down)

    def add_first(s, half):
        own, minus, plus, opposite = ends(half, 0)
        up, down = devices(half, 0)
        for side, (a, rows, device) in enumerate(((plus, A, up), (minus, B, down))):
            got(r1.at[s, half, side], rs_r.at[s, half, side])
            view = block(s, half, a, rows)
            view[...] = (view[...].astype(F32) + r1[s, half, side].astype(F32)).astype(BF)
            rs_put(s, half, 4 + side, view, r2.at[s, half, side, :, span(rows), :], device)

    def send_second(s, half):
        own, minus, plus, opposite = ends(half, 0)
        got(r2.at[s, half, 0, :, span(B), :], rs_r.at[s, half, 2])
        got(r2.at[s, half, 1, :, span(A), :], rs_r.at[s, half, 3])
        got(r2.at[s, half, 0, :, span(A), :], rs_r.at[s, half, 4])
        got(r2.at[s, half, 1, :, span(B), :], rs_r.at[s, half, 5])
        view = block(s, half, own, (0, HALF))
        s1[s, half] = (
            view[...].astype(F32) + r2[s, half, 0].astype(F32) + r2[s, half, 1].astype(F32)
        ).astype(BF)
        own, minus, plus, opposite = ends(half, 1)
        up, down = devices(half, 1)
        to = lambda a, rows: s1.at[s, half, a, span(rows), :]
        rs_put(s, half, 6, to(opposite, A), q1.at[s, half, 0], up)
        rs_put(s, half, 7, to(opposite, B), q1.at[s, half, 1], down)
        rs_put(s, half, 8, to(plus, B), q2.at[s, half, 0, span(B), :], up)
        rs_put(s, half, 9, to(minus, A), q2.at[s, half, 1, span(A), :], down)

    def add_second(s, half):
        own, minus, plus, opposite = ends(half, 1)
        up, down = devices(half, 1)
        for side, (a, rows, device) in enumerate(((plus, A, up), (minus, B, down))):
            got(q1.at[s, half, side], rs_r.at[s, half, 6 + side])
            view = s1.at[s, half, a, span(rows), :]
            view[...] = (view[...].astype(F32) + q1[s, half, side].astype(F32)).astype(BF)
            rs_put(s, half, 10 + side, view, q2.at[s, half, side, span(rows), :], device)

    writes = []

    def finish(s, half):
        own, minus, plus, opposite = ends(half, 1)
        got(q2.at[s, half, 0, span(B), :], rs_r.at[s, half, 8])
        got(q2.at[s, half, 1, span(A), :], rs_r.at[s, half, 9])
        got(q2.at[s, half, 0, span(A), :], rs_r.at[s, half, 10])
        got(q2.at[s, half, 1, span(B), :], rs_r.at[s, half, 11])
        rows, cols = pl.ds(half * HALF, HALF), pl.ds(s * HD, HD)
        out[rows, cols] = (
            act[t, rows, cols].astype(F32)
            + s1[s, half, own].astype(F32)
            + q2[s, half, 0].astype(F32)
            + q2[s, half, 1].astype(F32)
        ).astype(BF)
        write = pltpu.make_async_copy(out.at[rows, cols], result.at[rows, cols], out_sem.at[s, half])
        write.start()
        writes.append(write)

    x_own(0, 1)
    ag_send(0, 0, 0, t, None)
    ag_send(1, 0, 0, t, None)
    ag2_send(0, 0)
    ag2_send(1, 0)
    x_hand_on(0)
    x_near(0, (1, 0))
    ag_near(0, 0, 0, other(0))
    ag2_send(0, 1)
    ag2_send(0, 2)
    ag_near(1, 0, 0, other(1))
    ag2_send(1, 1)
    ag2_send(1, 2)
    x_far(0, (1, 1))
    ag2_near(1, 0)
    ag2_near(0, 0)
    x_sibling(0)
    x_hand_on(1)
    ag_far(0, 0, 0, other(0))
    ag2_send(0, 3)
    ag2_near(0, 1)
    x_near(1, (2, 0))
    ag2_near(1, 1)
    ag2_near(0, 2)
    x_far(1, (2, 1))
    ag2_near(1, 2)
    ag_far(1, 0, 0, other(1))
    ag2_send(1, 3)
    x_sibling(1)
    x_hand_on(2)
    ag2_far(1, 0)
    ag2_far(0, 0)
    ag2_far(1, 1)
    x_near(2, (3, 0))
    ag2_far(1, 2)
    ag2_near(0, 3)
    ag2_far(0, 1)
    x_far(2, (3, 1))
    ag2_near(1, 3)
    ag2_far(0, 2)
    x_sibling(2)
    x_hand_on(3)
    ag2_far(0, 3)
    ag2_far(1, 3)
    loads[11].wait()
    acc[...] = jnp.zeros_like(acc)
    squares[...] = jnp.zeros_like(squares)

    @pl.loop(0, 16)
    def _(tt):
        rows = act[tt].astype(F32)
        power = rows * rows
        squares[...] += (power[:, :HD] + power[:, HD:2 * HD]) + (
            power[:, 2 * HD:3 * HD] + power[:, 3 * HD:]
        )
        scaled[tt] = (rows * gain[tt]).astype(BF)

    squares[:, :1] = lax.rsqrt(
        jnp.sum(squares[...], axis=1, keepdims=True) * (1.0 / (16 * WIDE)) + EPSILON
    )
    x_near(3, (4, 0))
    project(0, 0, WIDE + HD)
    project(1, 0, WIDE + HD)
    x_far(3, (4, 1))
    project(2, 0, WIDE + HD)
    x_hand_on(4)
    x_sibling(3)
    project(3, WIDE, HD)
    loads[12].wait()
    loads[13].wait()

    @pl.loop(0, TAKEN, unroll=True)
    def _(n):
        rows = pl.ds(n * ITEM_LEN, ITEM_LEN)
        value = acc[rows, pl.ds(WIDE, HD)] * squares[rows, :1]
        kvown[rows, :] = jnp.where(parity == 0, rotated(value), value).astype(BF)

    put(kvown, kvpart, kv_s, kv_r, (me, t + 1 - 2 * parity))
    project(3, 0, WIDE)

    @pl.loop(0, TAKEN, unroll=True)
    def _(n):
        rows = pl.ds(n * ITEM_LEN, ITEM_LEN)
        inverse = squares[rows, :1]
        for h in range(4):
            value = acc[rows, pl.ds(h * HD, HD)] * inverse
            qs[n, pl.ds(h * ITEM_LEN, ITEM_LEN), :] = rotated(value).astype(BF)

    x_near(4, (5, 0))
    got(kvpart, kv_r)

    @pl.loop(0, TAKEN, unroll=True)
    def _(n):
        rows = pl.ds(n * ITEM_LEN, ITEM_LEN)
        mine, theirs = kvown[rows, :], kvpart[rows, :]
        keys = jnp.where(parity == 0, mine, theirs)
        values = jnp.where(parity == 0, theirs, mine)
        scores = lax.dot_general(
            qs[n], keys, (((1,), (1,)), ((), ())), preferred_element_type=F32
        ) * (HD ** -0.5)
        place = lax.broadcasted_iota(jnp.int32, scores.shape, 0) % ITEM_LEN
        scores = jnp.where(
            place >= lax.broadcasted_iota(jnp.int32, scores.shape, 1), scores, -1e30
        )
        raised = jnp.exp(scores - jnp.max(scores, axis=1, keepdims=True))
        probs = (raised * (1.0 / jnp.sum(raised, axis=1, keepdims=True))).astype(BF)
        context = jnp.dot(probs, values, preferred_element_type=F32).astype(BF)
        for h in range(4):
            ctx[rows, pl.ds(h * HD, HD)] = context[h * ITEM_LEN:(h + 1) * ITEM_LEN, :]

    x_far(4, (5, 1))
    x_hand_on(5)
    multiply(0)
    send_first(0)
    x_near(5, (6, 0))
    x_far(5, (6, 1))
    add_first(0, 0)
    add_first(0, 1)
    multiply(1)
    send_first(1)
    x_hand_on(6)
    send_second(0, 0)
    send_second(0, 1)
    x_near(6, (7, 0))
    add_first(1, 0)
    add_first(1, 1)
    x_far(6, (7, 1))
    add_second(0, 1)
    add_second(0, 0)
    multiply(2)
    send_first(2)
    x_hand_on(7)
    send_second(1, 0)
    send_second(1, 1)
    x_near(7)
    finish(0, 0)
    finish(0, 1)
    add_first(2, 0)
    add_first(2, 1)
    x_far(7)
    add_second(1, 1)
    add_second(1, 0)
    multiply(3)
    send_first(3)
    send_second(2, 0)
    send_second(2, 1)
    finish(1, 0)
    finish(1, 1)
    add_first(3, 0)
    add_first(3, 1)
    add_second(2, 1)
    add_second(2, 0)
    send_second(3, 0)
    send_second(3, 1)
    finish(2, 0)
    finish(2, 1)
    add_second(3, 0)
    add_second(3, 1)
    finish(3, 0)
    finish(3, 1)

    for copy in started:
        copy.wait_send()
    for write in writes:
        write.wait()


def shards(hidden, exited, destination, norm_gain, query_weight, keyvalue_weight, output_weight):
    cos, sin = tables()
    smem = pl.BlockSpec(memory_space=pltpu.SMEM)
    hbm = pl.BlockSpec(memory_space=pl.ANY)
    dma = pltpu.SemaphoreType.DMA
    return pl.pallas_call(
        kernel,
        out_shape=jax.ShapeDtypeStruct((ROWS, WIDE), BF),
        in_specs=[smem, smem, hbm, hbm, hbm, hbm, hbm, hbm, hbm],
        out_specs=hbm,
        scratch_shapes=[
            pltpu.VMEM((16, 1, WIDE), F32),
            pltpu.VMEM((ITEM_LEN, HD), F32),
            pltpu.VMEM((ITEM_LEN, HD), F32),
            pltpu.VMEM((ROWS, WIDE), BF),
            pltpu.VMEM((HERE, ITEM_LEN, WIDE), BF),
            pltpu.VMEM((8, 2, ITEM_LEN, WIDE), BF),
            pltpu.VMEM((8, 2, ITEM_LEN, WIDE), BF),
            pltpu.VMEM((8, 8, 128), jnp.int32),
            pltpu.SMEM((8, 8, 128), jnp.int32),
            pltpu.VMEM((16, ROWS, WIDE), BF),
            pltpu.VMEM((16, ROWS, WIDE), BF),
            pltpu.VMEM((8, DEPTH, WIDE + HD), BF),
            pltpu.VMEM((4, 8, WIDE, 2 * HD), BF),
            pltpu.VMEM((ROWS, WIDE + HD), F32),
            pltpu.VMEM((ROWS, HD), F32),
            pltpu.VMEM((TAKEN, 4 * ITEM_LEN, HD), BF),
            pltpu.VMEM((ROWS, HD), BF),
            pltpu.VMEM((ROWS, HD), BF),
            pltpu.VMEM((ROWS, WIDE), BF),
            pltpu.VMEM((4, 4, 4, ROWS, HD), BF),
            pltpu.VMEM((4, 2, 2, 4, QUARTER, HD), BF),
            pltpu.VMEM((4, 2, 2, 4, HALF, HD), BF),
            pltpu.VMEM((4, 2, 4, HALF, HD), BF),
            pltpu.VMEM((4, 2, 2, QUARTER, HD), BF),
            pltpu.VMEM((4, 2, 2, HALF, HD), BF),
            dma((15,)),
            dma((4, 2)),
            dma((8,)),
            dma((8,)),
            dma((8,)),
            dma((8,)),
            dma((8, 11)),
            dma((8, 11)),
            dma((2, 20)),
            dma((2, 20)),
            dma((4, 2, 12)),
            dma((4, 2, 12)),
            dma(()),
            dma(()),
        ],
        compiler_params=pltpu.CompilerParams(
            collective_id=0, has_side_effects=True, vmem_limit_bytes=60 * 1024 * 1024
        ),
        cost_estimate=pl.CostEstimate(
            flops=2 * ROWS * 16 * WIDE * (2 * WIDE + HD),
            bytes_accessed=8 * 1024 * 1024,
            transcendentals=ROWS * 4 * ITEM_LEN,
        ),
    )(
        exited,
        destination,
        hidden.reshape(HERE, ITEM_LEN, WIDE),
        norm_gain.reshape(16, 1, WIDE),
        query_weight,
        keyvalue_weight,
        output_weight,
        jnp.asarray(cos),
        jnp.asarray(sin),
    )


def solution(mesh):
    placed = (
        P("dp", "tensor"),
        P("dp"),
        P("dp"),
        P(),
        P("dp", "tensor"),
        P("dp", "tensor"),
        P("tensor", "dp"),
    )
    return jax.shard_map(
        shards, mesh=mesh, in_specs=placed, out_specs=P("dp", "tensor"), check_vma=False
    )
```

```python
import functools

import jax
import jax.numpy as jnp
import numpy as np
from jax import lax
from jax.experimental import pallas as pl
from jax.experimental.pallas import tpu as pltpu
from jax.sharding import PartitionSpec as P

MESH = pl.DeviceIdType.MESH

HD = 128
ITEM_LEN = 64
HERE = 16
TAKEN = 6
ROWS = TAKEN * ITEM_LEN
WIDE = 512
DEPTH = 1024
EPSILON = 1e-05
THETA = 500000.0
BF = jnp.bfloat16
F32 = jnp.float32

PIECE = DEPTH // 4
HALF = ROWS // 2
QUARTER = ROWS // 4


def tables():
    j = np.arange(HD // 2, dtype=np.float64)
    freq = (THETA ** (-2.0 * j / HD)).astype(np.float32)
    phase = (np.arange(ITEM_LEN, dtype=np.float32)[:, None] * freq).astype(np.float64)
    cos, sin = np.cos(phase), np.sin(phase)
    return (
        np.concatenate([cos, cos], axis=1).astype(np.float32),
        np.concatenate([-sin, sin], axis=1).astype(np.float32),
    )


def kernel(
    exited, destination, hidden, gain_in, wq, wkv, wo, cos_in, sin_in, result,
    gain, cos, sin, out,
    hid, outgoing, arrived, meta, meta_scalar, act, scaled, wbuf, obuf, acc, squares, qs, kvown, kvpart,
    ctx, part, r1, r2, s1, q1, q2,
    local_sem, out_sem, meta_s, meta_r, route_s, route_r, x_s, x_r, ag_s, ag_r, rs_s, rs_r, kv_s, kv_r,
):
    me = lax.axis_index("dp")
    t = lax.axis_index("tensor")
    x, c = me // 2, me % 2
    z, y = t // 4, t % 4
    left = ((x + 3) % 4) * 2 + c
    right = ((x + 1) % 4) * 2 + c
    far = ((x + 2) % 4) * 2 + c
    zp, zm, zf = (z + 1) % 4, (z + 3) % 4, (z + 2) % 4
    yp, ym, yf = (y + 1) % 4, (y + 3) % 4, (y + 2) % 4

    def sibling(i):
        return i + 1 - 2 * c

    sib = sibling(me)

    def put(src, dst, send, recv, device):
        copy = pltpu.make_async_remote_copy(
            src_ref=src, dst_ref=dst, send_sem=send, recv_sem=recv,
            device_id=device, device_id_type=MESH,
        )
        copy.start()

    def got(dst, recv):
        pltpu.make_async_remote_copy(
            src_ref=dst, dst_ref=dst, send_sem=recv, recv_sem=recv,
            device_id=(sib, t), device_id_type=MESH,
        ).wait_recv()

    def sent(src, send):
        pltpu.make_async_remote_copy(
            src_ref=src, dst_ref=src, send_sem=send, recv_sem=send,
            device_id=(sib, t), device_id_type=MESH,
        ).wait_send()

    def loaded(dst, sem):
        pltpu.make_async_copy(dst, dst, sem).wait()

    loads = [pltpu.make_async_copy(hidden, hid, local_sem.at[0])]
    loads.append(pltpu.make_async_copy(wq, wbuf.at[me, :, pl.ds(0, WIDE)], local_sem.at[1]))
    loads.append(pltpu.make_async_copy(wkv, wbuf.at[me, :, pl.ds(WIDE, HD)], local_sem.at[1]))
    for s in range(4):
        for h in range(2):
            loads.append(
                pltpu.make_async_copy(
                    wo.at[:, pl.ds(h * WIDE + s * HD, HD)],
                    obuf.at[s, me, :, pl.ds(h * HD, HD)],
                    local_sem.at[2],
                )
            )
    loads.append(pltpu.make_async_copy(gain_in, gain, local_sem.at[3]))
    loads.append(pltpu.make_async_copy(cos_in, cos, local_sem.at[4]))
    loads.append(pltpu.make_async_copy(sin_in, sin, local_sem.at[5]))
    for load in loads:
        load.start()

    barrier = pltpu.get_barrier_semaphore()
    peers = [((me + k) % 8, t) for k in range(1, 8)]
    peers += [(me, zp * 4 + y), (me, zm * 4 + y), (me, z * 4 + yp), (me, z * 4 + ym)]
    for peer in peers:
        pl.semaphore_signal(barrier, inc=1, device_id=peer, device_id_type=MESH)
    pl.semaphore_wait(barrier, len(peers))

    def weights(r, i, low=0, count=None):
        if r < 4:
            return wbuf.at[i, pl.ds(r * PIECE + low, count or PIECE), :]
        return obuf.at[r - 4, i, pl.ds(low, count or WIDE), :]

    def half_of(r):
        return PIECE // 2 if r < 4 else WIDE // 2

    def x_put(r, k, view, device):
        put(view, view, x_s.at[r], x_r.at[r, k], (device, t))

    def shares(r, count):
        if r < 4:
            return wbuf.at[pl.ds(0, count), pl.ds(r * PIECE, PIECE), :]
        return obuf.at[r - 4, pl.ds(0, count)]

    def x_own_sibling(r):
        x_put(r, 3, weights(r, me), sib)

    def x_own(r, which):
        n = half_of(r)
        x_put(r, which, weights(r, me, which * n, n), right)
        x_put(r, which, weights(r, me, n - which * n, n), left)

    def x_hand_on(r):
        n = half_of(r)
        got(shares(r, 1), x_r.at[r, 0])
        x_put(r, 2, weights(r, left, 0, n), right)
        x_put(r, 2, weights(r, right, n, n), left)

    def x_near(r, *after):
        got(shares(r, 1), x_r.at[r, 1])
        for piece in after:
            x_own(*piece)
        x_put(r, 3, weights(r, left), sib)
        x_put(r, 3, weights(r, right), sib)

    def x_far(r, *after):
        got(shares(r, 1), x_r.at[r, 2])
        for piece in after:
            x_own(*piece)
        x_put(r, 3, weights(r, far), sib)

    def x_sibling(r):
        got(shares(r, 4), x_r.at[r, 3])

    loaded(wbuf.at[me], local_sem.at[1])
    x_own(0, 0)
    for r in range(4):
        x_own_sibling(r)

    codes = [jnp.where(exited[k] == 0, destination[k], -1) for k in range(HERE)]
    lane = lax.broadcasted_iota(jnp.int32, (8, 128), 1)
    row = jnp.full((8, 128), -1, jnp.int32)
    for k in range(HERE):
        row = jnp.where(lane == k, codes[k], row)
    meta[me] = row
    for k in range(1, 8):
        put(meta.at[me], meta.at[me], meta_s, meta_r, ((me + k) % 8, t))

    loads[0].wait()
    for k in [4, 2, 6, 3, 5, 1, 7, 0]:
        dest = (me + k) % 8 if k else me
        seen = jnp.int32(0)
        first = jnp.int32(0)
        second = jnp.int32(0)
        for item in range(HERE):
            hit = codes[item] == dest
            first = jnp.where(hit & (seen == 0), item, first)
            second = jnp.where(hit & (seen == 1), item, second)
            seen = seen + jnp.where(hit, 1, 0)
        if k:
            outgoing[dest, 0] = hid[first]
            outgoing[dest, 1] = hid[second]
            put(outgoing.at[dest], arrived.at[me], route_s, route_r, (dest, t))
        else:
            arrived[me, 0] = hid[first]
            arrived[me, 1] = hid[second]
    loaded(obuf.at[pl.ds(0, 4), me], local_sem.at[2])
    x_own(0, 1)
    for r in range(4, 8):
        x_own_sibling(r)

    got(meta.at[pl.ds(0, 7)], meta_r)
    to_scalar = pltpu.make_async_copy(meta, meta_scalar, local_sem.at[6])
    to_scalar.start()
    to_scalar.wait()
    picks = [jnp.int32(0)] * TAKEN
    rank = jnp.int32(0)
    for j in range(8):
        count = jnp.int32(0)
        for item in range(HERE):
            count = count + jnp.where(meta_scalar[j, 0, item] == me, 1, 0)
        for s in range(2):
            valid = count > s
            for r in range(TAKEN):
                picks[r] = jnp.where(valid & (rank == r), 2 * j + s, picks[r])
            rank = rank + jnp.where(valid, 1, 0)

    got(arrived.at[pl.ds(0, 7)], route_r)
    flat = arrived.reshape(16, ITEM_LEN, WIDE)
    for r in range(TAKEN):
        act[t, pl.ds(r * ITEM_LEN, ITEM_LEN), :] = flat[picks[r]]

    def line(half, phase):
        along_z = (half == 0) == (phase == 0)
        if along_z:
            return (z, zm, zp, zf), lambda a, b: a * 4 + b
        return (y, ym, yp, yf), lambda a, b: b * 4 + a

    def chunk(tt, half, low=0, count=HALF):
        return act.at[tt, pl.ds(half * HALF + low, count), :]

    def ag_put(half, k, view, device):
        put(view, view, ag_s.at[half], ag_r.at[half, k], (me, device))

    def other(half):
        return y if half == 0 else z

    def ag_send(half, phase, slot, tt, near):
        (own, minus, plus, opposite), at = line(half, phase)
        place = other(half) if phase == 0 else near
        ag_put(half, slot, chunk(tt, half), at(plus, place))
        ag_put(half, slot, chunk(tt, half), at(minus, place))

    def ag_near(half, phase, slot, far_slot, place):
        (own, minus, plus, opposite), at = line(half, phase)
        got(act.at[pl.ds(0, 2), pl.ds(half * HALF, HALF), :], ag_r.at[half, slot])
        q = HALF // 2
        here = other(half) if phase == 0 else (z if half == 0 else y)
        ag_put(half, far_slot, chunk(at(minus, place), half, 0, q), at(plus, here))
        ag_put(half, far_slot, chunk(at(plus, place), half, q, q), at(minus, here))

    def places(half):
        return (z, zm, zp, zf) if half == 0 else (y, ym, yp, yf)

    def first_at(half, a):
        return a * 4 + y if half == 0 else z * 4 + a

    def ag2_send(half, n):
        a = places(half)[n]
        ag_send(half, 1, 2 + n, first_at(half, a), places(half)[0])

    def ag2_near(half, n):
        ag_near(half, 1, 2 + n, 6, places(half)[n])

    def rotated(value):
        return value * cos[...] + pltpu.roll(value, HD // 2, 1) * sin[...]

    parity = t % 2

    def project(p, low, count):
        @pl.loop(0, 8, step=8)
        def _(i):
            term = None
            for j in range(8):
                product = jnp.dot(
                    scaled[2 * (i + j) + p // 2, :, pl.ds((p % 2) * PIECE, PIECE)],
                    wbuf[i + j, pl.ds(p * PIECE, PIECE), pl.ds(low, count)],
                    preferred_element_type=F32,
                )
                term = product if term is None else term + product
            acc[:, pl.ds(low, count)] += term

    def multiply(s):
        x_sibling(4 + s)

        @pl.loop(0, 4, unroll=True)
        def _(a):
            for b in range(2):
                term = jnp.dot(
                    ctx[...], obuf[s, 2 * a + b], preferred_element_type=F32
                ).astype(BF)
                part[s, a, 2 * b] = term[:, :HD]
                part[s, a, 2 * b + 1] = term[:, HD:]

    def rs_put(s, half, k, src, dst, device):
        put(src, dst, rs_s.at[s, half], rs_r.at[s, half, k], (me, device))

    A = (0, QUARTER)
    B = (QUARTER, QUARTER)

    def block(s, half, a, rows):
        low, count = rows
        span = pl.ds(half * HALF + low, count)
        if half == 0:
            return part.at[s, a, :, span, :]
        return part.at[s, :, a, span, :]

    def devices(half, phase):
        if (half == 0) == (phase == 0):
            return zp * 4 + y, zm * 4 + y
        return z * 4 + yp, z * 4 + ym

    def ends(half, phase):
        if (half == 0) == (phase == 0):
            return z, zm, zp, zf
        return y, ym, yp, yf

    def span(rows):
        return pl.ds(rows[0], rows[1])

    def send_first(s):
        for half in range(2):
            own, minus, plus, opposite = ends(half, 0)
            up, down = devices(half, 0)
            rs_put(s, half, 0, block(s, half, opposite, A), r1.at[s, half, 0], up)
            rs_put(s, half, 0, block(s, half, opposite, B), r1.at[s, half, 1], down)
            rs_put(s, half, 1, block(s, half, plus, B), r2.at[s, half, 0, :, span(B), :], up)
            rs_put(s, half, 1, block(s, half, minus, A), r2.at[s, half, 1, :, span(A), :], down)

    def add_first(s, half):
        own, minus, plus, opposite = ends(half, 0)
        up, down = devices(half, 0)
        got(r1.at[s, half], rs_r.at[s, half, 0])
        for side, (a, rows, device) in enumerate(((plus, A, up), (minus, B, down))):
            view = block(s, half, a, rows)
            view[...] = (view[...].astype(F32) + r1[s, half, side].astype(F32)).astype(BF)
            rs_put(s, half, 1, view, r2.at[s, half, side, :, span(rows), :], device)

    def send_second(s, half):
        own, minus, plus, opposite = ends(half, 0)
        got(r2.at[s, half], rs_r.at[s, half, 1])
        view = block(s, half, own, (0, HALF))
        s1[s, half] = (
            view[...].astype(F32) + r2[s, half, 0].astype(F32) + r2[s, half, 1].astype(F32)
        ).astype(BF)
        own, minus, plus, opposite = ends(half, 1)
        up, down = devices(half, 1)
        to = lambda a, rows: s1.at[s, half, a, span(rows), :]
        rs_put(s, half, 2, to(opposite, A), q1.at[s, half, 0], up)
        rs_put(s, half, 2, to(opposite, B), q1.at[s, half, 1], down)
        rs_put(s, half, 3, to(plus, B), q2.at[s, half, 0, span(B), :], up)
        rs_put(s, half, 3, to(minus, A), q2.at[s, half, 1, span(A), :], down)

    def add_second(s, half):
        own, minus, plus, opposite = ends(half, 1)
        up, down = devices(half, 1)
        got(q1.at[s, half], rs_r.at[s, half, 2])
        for side, (a, rows, device) in enumerate(((plus, A, up), (minus, B, down))):
            view = s1.at[s, half, a, span(rows), :]
            view[...] = (view[...].astype(F32) + q1[s, half, side].astype(F32)).astype(BF)
            rs_put(s, half, 3, view, q2.at[s, half, side, span(rows), :], device)

    def finish(s, half):
        own, minus, plus, opposite = ends(half, 1)
        got(q2.at[s, half], rs_r.at[s, half, 3])
        rows, cols = pl.ds(half * HALF, HALF), pl.ds(s * HD, HD)
        out[rows, cols] = (
            act[t, rows, cols].astype(F32)
            + s1[s, half, own].astype(F32)
            + q2[s, half, 0].astype(F32)
            + q2[s, half, 1].astype(F32)
        ).astype(BF)
        pltpu.make_async_copy(out.at[rows, cols], result.at[rows, cols], out_sem).start()

    ag_send(0, 0, 0, t, None)
    ag_send(1, 0, 0, t, None)
    ag2_send(0, 0)
    ag2_send(1, 0)
    x_hand_on(0)
    x_near(0, (1, 0))
    ag_near(0, 0, 0, 1, other(0))
    ag2_send(0, 1)
    ag2_send(0, 2)
    x_far(0, (1, 1))
    ag_near(1, 0, 0, 1, other(1))
    ag2_send(1, 1)
    ag2_send(1, 2)
    x_sibling(0)
    x_hand_on(1)
    ag2_near(1, 0)
    ag2_near(0, 0)
    got(act.at[0, pl.ds(0 * HALF, HALF), :], ag_r.at[0, 1])
    ag2_send(0, 3)
    x_near(1, (2, 0))
    ag2_near(0, 1)
    ag2_near(1, 1)
    x_far(1, (2, 1))
    ag2_near(0, 2)
    x_sibling(1)
    x_hand_on(2)
    ag2_near(1, 2)
    got(act.at[0, pl.ds(1 * HALF, HALF), :], ag_r.at[1, 1])
    ag2_send(1, 3)
    x_near(2, (3, 0))
    ag2_near(0, 3)
    x_far(2, (3, 1))
    x_sibling(2)
    x_hand_on(3)
    ag2_near(1, 3)
    got(act.at[pl.ds(0, 4), pl.ds(0 * HALF, HALF), :], ag_r.at[0, 6])
    x_near(3, (4, 0))
    got(act.at[pl.ds(0, 4), pl.ds(1 * HALF, HALF), :], ag_r.at[1, 6])
    loaded(gain, local_sem.at[3])
    acc[...] = jnp.zeros_like(acc)
    squares[...] = jnp.zeros_like(squares)

    @pl.loop(0, 16)
    def _(tt):
        rows = act[tt].astype(F32)
        power = rows * rows
        squares[...] += (power[:, :HD] + power[:, HD:2 * HD]) + (
            power[:, 2 * HD:3 * HD] + power[:, 3 * HD:]
        )
        scaled[tt] = (rows * gain[tt]).astype(BF)

    squares[:, :1] = lax.rsqrt(
        jnp.sum(squares[...], axis=1, keepdims=True) * (1.0 / (16 * WIDE)) + EPSILON
    )
    project(0, 0, WIDE + HD)
    x_far(3, (4, 1))
    project(1, 0, WIDE + HD)
    project(2, 0, WIDE + HD)
    x_hand_on(4)
    x_sibling(3)
    project(3, WIDE, HD)
    loaded(cos, local_sem.at[4])
    loaded(sin, local_sem.at[5])

    @pl.loop(0, TAKEN, unroll=True)
    def _(n):
        rows = pl.ds(n * ITEM_LEN, ITEM_LEN)
        value = acc[rows, pl.ds(WIDE, HD)] * squares[rows, :1]
        kvown[rows, :] = jnp.where(parity == 0, rotated(value), value).astype(BF)

    put(kvown.at[pl.ds(0 * HALF, HALF), :], kvpart.at[pl.ds(0 * HALF, HALF), :], kv_s, kv_r.at[0], (me, t + 1 - 2 * parity))
    put(kvown.at[pl.ds(1 * HALF, HALF), :], kvpart.at[pl.ds(1 * HALF, HALF), :], kv_s, kv_r.at[1], (me, t + 1 - 2 * parity))
    project(3, 0, WIDE)

    @pl.loop(0, TAKEN, unroll=True)
    def _(n):
        rows = pl.ds(n * ITEM_LEN, ITEM_LEN)
        inverse = squares[rows, :1]
        for h in range(4):
            value = acc[rows, pl.ds(h * HD, HD)] * inverse
            qs[n, pl.ds(h * ITEM_LEN, ITEM_LEN), :] = rotated(value).astype(BF)

    x_near(4, (5, 0))
    got(kvpart.at[pl.ds(0 * HALF, HALF), :], kv_r.at[0])

    @pl.loop(0, 3, unroll=True)
    def _(n):
        rows = pl.ds(n * ITEM_LEN, ITEM_LEN)
        mine, theirs = kvown[rows, :], kvpart[rows, :]
        keys = jnp.where(parity == 0, mine, theirs)
        values = jnp.where(parity == 0, theirs, mine)
        scores = lax.dot_general(
            qs[n], keys, (((1,), (1,)), ((), ())), preferred_element_type=F32
        ) * (HD ** -0.5)
        place = lax.broadcasted_iota(jnp.int32, scores.shape, 0) % ITEM_LEN
        scores = jnp.where(
            place >= lax.broadcasted_iota(jnp.int32, scores.shape, 1), scores, -1e30
        )
        raised = jnp.exp(scores - jnp.max(scores, axis=1, keepdims=True))
        probs = (raised * (1.0 / jnp.sum(raised, axis=1, keepdims=True))).astype(BF)
        context = jnp.dot(probs, values, preferred_element_type=F32).astype(BF)
        for h in range(4):
            ctx[rows, pl.ds(h * HD, HD)] = context[h * ITEM_LEN:(h + 1) * ITEM_LEN, :]

    got(kvpart.at[pl.ds(1 * HALF, HALF), :], kv_r.at[1])

    @pl.loop(3, 6, unroll=True)
    def _(n):
        rows = pl.ds(n * ITEM_LEN, ITEM_LEN)
        mine, theirs = kvown[rows, :], kvpart[rows, :]
        keys = jnp.where(parity == 0, mine, theirs)
        values = jnp.where(parity == 0, theirs, mine)
        scores = lax.dot_general(
            qs[n], keys, (((1,), (1,)), ((), ())), preferred_element_type=F32
        ) * (HD ** -0.5)
        place = lax.broadcasted_iota(jnp.int32, scores.shape, 0) % ITEM_LEN
        scores = jnp.where(
            place >= lax.broadcasted_iota(jnp.int32, scores.shape, 1), scores, -1e30
        )
        raised = jnp.exp(scores - jnp.max(scores, axis=1, keepdims=True))
        probs = (raised * (1.0 / jnp.sum(raised, axis=1, keepdims=True))).astype(BF)
        context = jnp.dot(probs, values, preferred_element_type=F32).astype(BF)
        for h in range(4):
            ctx[rows, pl.ds(h * HD, HD)] = context[h * ITEM_LEN:(h + 1) * ITEM_LEN, :]

    x_far(4, (5, 1))
    x_hand_on(5)
    multiply(0)
    send_first(0)
    x_near(5, (6, 0))
    add_first(0, 0)
    add_first(0, 1)
    x_far(5, (6, 1))
    multiply(1)
    send_first(1)
    x_hand_on(6)
    send_second(0, 0)
    send_second(0, 1)
    x_near(6, (7, 0))
    add_first(1, 0)
    add_first(1, 1)
    x_far(6, (7, 1))
    add_second(0, 1)
    add_second(0, 0)
    multiply(2)
    send_first(2)
    x_hand_on(7)
    send_second(1, 0)
    send_second(1, 1)
    finish(0, 0)
    finish(0, 1)
    x_near(7)
    add_first(2, 0)
    add_first(2, 1)
    x_far(7)
    add_second(1, 1)
    add_second(1, 0)
    multiply(3)
    send_first(3)
    send_second(2, 0)
    send_second(2, 1)
    finish(1, 0)
    finish(1, 1)
    add_first(3, 0)
    add_first(3, 1)
    add_second(2, 1)
    add_second(2, 0)
    send_second(3, 0)
    send_second(3, 1)
    finish(2, 1)
    finish(2, 0)
    add_second(3, 0)
    add_second(3, 1)
    finish(3, 0)
    finish(3, 1)

    sent(meta.at[pl.ds(0, 7)], meta_s)
    sent(outgoing.at[pl.ds(0, 7)], route_s)
    for r in range(8):
        sent(shares(r, 7), x_s.at[r])
    for half in range(2):
        sent(act.at[pl.ds(0, 15), pl.ds(half * HALF, HALF), :], ag_s.at[half])
    sent(kvown, kv_s)
    terms = part.reshape(64, ROWS, HD)
    for s in range(4):
        for half in range(2):
            sent(terms.at[pl.ds(16 * s, 15), pl.ds(0, HALF), :], rs_s.at[s, half])
    loaded(out, out_sem)


def shards(hidden, exited, destination, norm_gain, query_weight, keyvalue_weight, output_weight):
    cos, sin = tables()
    smem = pl.BlockSpec(memory_space=pltpu.SMEM)
    hbm = pl.BlockSpec(memory_space=pl.ANY)
    dma = pltpu.SemaphoreType.DMA
    return pl.pallas_call(
        kernel,
        out_shape=jax.ShapeDtypeStruct((ROWS, WIDE), BF),
        in_specs=[smem, smem, hbm, hbm, hbm, hbm, hbm, hbm, hbm],
        out_specs=hbm,
        scratch_shapes=[
            pltpu.VMEM((16, 1, WIDE), F32),
            pltpu.VMEM((ITEM_LEN, HD), F32),
            pltpu.VMEM((ITEM_LEN, HD), F32),
            pltpu.VMEM((ROWS, WIDE), BF),
            pltpu.VMEM((HERE, ITEM_LEN, WIDE), BF),
            pltpu.VMEM((8, 2, ITEM_LEN, WIDE), BF),
            pltpu.VMEM((8, 2, ITEM_LEN, WIDE), BF),
            pltpu.VMEM((8, 8, 128), jnp.int32),
            pltpu.SMEM((8, 8, 128), jnp.int32),
            pltpu.VMEM((16, ROWS, WIDE), BF),
            pltpu.VMEM((16, ROWS, WIDE), BF),
            pltpu.VMEM((8, DEPTH, WIDE + HD), BF),
            pltpu.VMEM((4, 8, WIDE, 2 * HD), BF),
            pltpu.VMEM((ROWS, WIDE + HD), F32),
            pltpu.VMEM((ROWS, HD), F32),
            pltpu.VMEM((TAKEN, 4 * ITEM_LEN, HD), BF),
            pltpu.VMEM((ROWS, HD), BF),
            pltpu.VMEM((ROWS, HD), BF),
            pltpu.VMEM((ROWS, WIDE), BF),
            pltpu.VMEM((4, 4, 4, ROWS, HD), BF),
            pltpu.VMEM((4, 2, 2, 4, QUARTER, HD), BF),
            pltpu.VMEM((4, 2, 2, 4, HALF, HD), BF),
            pltpu.VMEM((4, 2, 4, HALF, HD), BF),
            pltpu.VMEM((4, 2, 2, QUARTER, HD), BF),
            pltpu.VMEM((4, 2, 2, HALF, HD), BF),
            dma((7,)),
            dma(()),
            dma(()),
            dma(()),
            dma(()),
            dma(()),
            dma((8,)),
            dma((8, 4)),
            dma((2,)),
            dma((2, 7)),
            dma((4, 2)),
            dma((4, 2, 4)),
            dma(()),
            dma((2,)),
        ],
        compiler_params=pltpu.CompilerParams(
            collective_id=0, has_side_effects=True, vmem_limit_bytes=60 * 1024 * 1024
        ),
        cost_estimate=pl.CostEstimate(
            flops=2 * ROWS * 16 * WIDE * (2 * WIDE + HD),
            bytes_accessed=8 * 1024 * 1024,
            transcendentals=ROWS * 4 * ITEM_LEN,
        ),
    )(
        exited,
        destination,
        hidden.reshape(HERE, ITEM_LEN, WIDE),
        norm_gain.reshape(16, 1, WIDE),
        query_weight,
        keyvalue_weight,
        output_weight,
        jnp.asarray(cos),
        jnp.asarray(sin),
    )


def solution(mesh):
    placed = (
        P("dp", "tensor"),
        P("dp"),
        P("dp"),
        P(),
        P("dp", "tensor"),
        P("dp", "tensor"),
        P("tensor", "dp"),
    )
    return jax.shard_map(
        shards, mesh=mesh, in_specs=placed, out_specs=P("dp", "tensor"), check_vma=False
    )
```

```python
import functools

import jax
import jax.numpy as jnp
import numpy as np
from jax import lax
from jax.experimental import pallas as pl
from jax.experimental.pallas import tpu as pltpu
from jax.sharding import PartitionSpec as P

MESH = pl.DeviceIdType.MESH

HD = 128
ITEM_LEN = 64
HERE = 16
TAKEN = 6
ROWS = TAKEN * ITEM_LEN
WIDE = 512
DEPTH = 1024
EPSILON = 1e-05
THETA = 500000.0
BF = jnp.bfloat16
F32 = jnp.float32

PIECE = DEPTH // 4
HALF = ROWS // 2
QUARTER = ROWS // 4
DIRECT = (3,)


def tables():
    j = np.arange(HD // 2, dtype=np.float64)
    freq = (THETA ** (-2.0 * j / HD)).astype(np.float32)
    phase = (np.arange(ITEM_LEN, dtype=np.float32)[:, None] * freq).astype(np.float64)
    cos, sin = np.cos(phase), np.sin(phase)
    return (
        np.concatenate([cos, cos], axis=1).astype(np.float32),
        np.concatenate([-sin, sin], axis=1).astype(np.float32),
    )


def kernel(
    exited, destination, hidden, gain_in, wq, wkv, wo, cos_in, sin_in, result,
    gain, cos, sin, out,
    hid, outgoing, arrived, meta, meta_scalar, act, scaled, wbuf, obuf, acc, squares, qs, kvown, kvpart,
    ctx, part, r1, r2, s1, q1, q2,
    local_sem, out_sem, meta_s, meta_r, route_s, route_r, x_s, x_r, ag_s, ag_r, rs_s, rs_r, kv_s, kv_r,
):
    me = lax.axis_index("dp")
    t = lax.axis_index("tensor")
    x, c = me // 2, me % 2
    z, y = t // 4, t % 4
    left = ((x + 3) % 4) * 2 + c
    right = ((x + 1) % 4) * 2 + c
    far = ((x + 2) % 4) * 2 + c
    zp, zm, zf = (z + 1) % 4, (z + 3) % 4, (z + 2) % 4
    yp, ym, yf = (y + 1) % 4, (y + 3) % 4, (y + 2) % 4

    def sibling(i):
        return i + 1 - 2 * c

    sib = sibling(me)

    def put(src, dst, send, recv, device):
        copy = pltpu.make_async_remote_copy(
            src_ref=src, dst_ref=dst, send_sem=send, recv_sem=recv,
            device_id=device, device_id_type=MESH,
        )
        copy.start()

    def got(dst, recv):
        pltpu.make_async_remote_copy(
            src_ref=dst, dst_ref=dst, send_sem=recv, recv_sem=recv,
            device_id=(sib, t), device_id_type=MESH,
        ).wait_recv()

    def sent(src, send):
        pltpu.make_async_remote_copy(
            src_ref=src, dst_ref=src, send_sem=send, recv_sem=send,
            device_id=(sib, t), device_id_type=MESH,
        ).wait_send()

    def loaded(dst, sem):
        pltpu.make_async_copy(dst, dst, sem).wait()

    loads = [pltpu.make_async_copy(hidden, hid, local_sem.at[0])]
    loads.append(pltpu.make_async_copy(wq, wbuf.at[me, :, pl.ds(0, WIDE)], local_sem.at[1]))
    loads.append(pltpu.make_async_copy(wkv, wbuf.at[me, :, pl.ds(WIDE, HD)], local_sem.at[1]))
    for s in range(4):
        for h in range(2):
            loads.append(
                pltpu.make_async_copy(
                    wo.at[:, pl.ds(h * WIDE + s * HD, HD)],
                    obuf.at[s, me, :, pl.ds(h * HD, HD)],
                    local_sem.at[2],
                )
            )
    loads.append(pltpu.make_async_copy(gain_in, gain, local_sem.at[3]))
    loads.append(pltpu.make_async_copy(cos_in, cos, local_sem.at[4]))
    loads.append(pltpu.make_async_copy(sin_in, sin, local_sem.at[5]))
    for load in loads:
        load.start()

    barrier = pltpu.get_barrier_semaphore()
    peers = [((me + k) % 8, t) for k in (4, 3, 5, 2, 6, 1, 7)]
    peers += [(me, zf * 4 + y), (me, z * 4 + yf)]
    peers += [(me, zp * 4 + y), (me, zm * 4 + y), (me, z * 4 + yp), (me, z * 4 + ym)]
    for peer in peers:
        pl.semaphore_signal(barrier, inc=1, device_id=peer, device_id_type=MESH)
    pl.semaphore_wait(barrier, len(peers))

    def weights(r, i, low=0, count=None):
        if r < 4:
            return wbuf.at[i, pl.ds(r * PIECE + low, count or PIECE), :]
        return obuf.at[r - 4, i, pl.ds(low, count or WIDE), :]

    def half_of(r):
        return PIECE // 2 if r < 4 else WIDE // 2

    def x_put(r, k, view, device):
        put(view, view, x_s.at[r], x_r.at[r, k], (device, t))

    def shares(r, count):
        if r < 4:
            return wbuf.at[pl.ds(0, count), pl.ds(r * PIECE, PIECE), :]
        return obuf.at[r - 4, pl.ds(0, count)]

    def x_own_sibling(r):
        x_put(r, 3, weights(r, me), sib)

    def x_own(r, which):
        n = half_of(r)
        x_put(r, which, weights(r, me, which * n, n), right)
        x_put(r, which, weights(r, me, n - which * n, n), left)

    def x_hand_on(r):
        n = half_of(r)
        got(shares(r, 1), x_r.at[r, 0])
        x_put(r, 2, weights(r, left, 0, n), right)
        x_put(r, 2, weights(r, right, n, n), left)

    def x_near(r, *after):
        got(shares(r, 1), x_r.at[r, 1])
        for piece in after:
            x_own(*piece)
        x_put(r, 3, weights(r, left), sib)
        x_put(r, 3, weights(r, right), sib)

    def x_far(r, *after):
        got(shares(r, 1), x_r.at[r, 2])
        for piece in after:
            x_own(*piece)
        x_put(r, 4, weights(r, far), sib)

    def x_sibling_near(r):
        got(shares(r, 3), x_r.at[r, 3])

    def x_sibling_far(r):
        got(shares(r, 1), x_r.at[r, 4])

    def x_sibling(r):
        x_sibling_near(r)
        x_sibling_far(r)

    loaded(wbuf.at[me], local_sem.at[1])
    x_own(0, 0)
    for r in range(4):
        x_own_sibling(r)

    codes = [jnp.where(exited[k] == 0, destination[k], -1) for k in range(HERE)]
    lane = lax.broadcasted_iota(jnp.int32, (8, 128), 1)
    row = jnp.full((8, 128), -1, jnp.int32)
    for k in range(HERE):
        row = jnp.where(lane == k, codes[k], row)
    meta[me] = row
    for k in range(1, 8):
        put(meta.at[me], meta.at[me], meta_s, meta_r, ((me + k) % 8, t))

    loads[0].wait()
    for k in [4, 2, 6, 3, 5, 1, 7, 0]:
        dest = (me + k) % 8 if k else me
        seen = jnp.int32(0)
        first = jnp.int32(0)
        second = jnp.int32(0)
        for item in range(HERE):
            hit = codes[item] == dest
            first = jnp.where(hit & (seen == 0), item, first)
            second = jnp.where(hit & (seen == 1), item, second)
            seen = seen + jnp.where(hit, 1, 0)
        if k:
            outgoing[dest, 0] = hid[first]
            outgoing[dest, 1] = hid[second]
            put(outgoing.at[dest], arrived.at[me], route_s, route_r, (dest, t))
        else:
            arrived[me, 0] = hid[first]
            arrived[me, 1] = hid[second]
    loaded(obuf.at[pl.ds(0, 4), me], local_sem.at[2])
    x_own(0, 1)
    for r in range(4, 8):
        x_own_sibling(r)

    got(meta.at[pl.ds(0, 7)], meta_r)
    to_scalar = pltpu.make_async_copy(meta, meta_scalar, local_sem.at[6])
    to_scalar.start()
    to_scalar.wait()
    picks = [jnp.int32(0)] * TAKEN
    rank = jnp.int32(0)
    for j in range(8):
        count = jnp.int32(0)
        for item in range(HERE):
            count = count + jnp.where(meta_scalar[j, 0, item] == me, 1, 0)
        for s in range(2):
            valid = count > s
            for r in range(TAKEN):
                picks[r] = jnp.where(valid & (rank == r), 2 * j + s, picks[r])
            rank = rank + jnp.where(valid, 1, 0)

    got(arrived.at[pl.ds(0, 7)], route_r)
    flat = arrived.reshape(16, ITEM_LEN, WIDE)
    for r in range(TAKEN):
        act[t, pl.ds(r * ITEM_LEN, ITEM_LEN), :] = flat[picks[r]]

    def line(half, phase):
        along_z = (half == 0) == (phase == 0)
        if along_z:
            return (z, zm, zp, zf), lambda a, b: a * 4 + b
        return (y, ym, yp, yf), lambda a, b: b * 4 + a

    def chunk(tt, half, low=0, count=HALF):
        return act.at[tt, pl.ds(half * HALF + low, count), :]

    def ag_put(half, k, view, device):
        put(view, view, ag_s.at[half], ag_r.at[half, k], (me, device))

    def other(half):
        return y if half == 0 else z

    def ag_send(half, phase, slot, tt, near):
        (own, minus, plus, opposite), at = line(half, phase)
        place = other(half) if phase == 0 else near
        ag_put(half, slot, chunk(tt, half), at(plus, place))
        ag_put(half, slot, chunk(tt, half), at(minus, place))

    def ag_near(half, phase, slot, far_slot, place):
        (own, minus, plus, opposite), at = line(half, phase)
        got(act.at[pl.ds(0, 2), pl.ds(half * HALF, HALF), :], ag_r.at[half, slot])
        q = HALF // 2
        here = other(half) if phase == 0 else (z if half == 0 else y)
        ag_put(half, far_slot, chunk(at(minus, place), half, 0, q), at(plus, here))
        ag_put(half, far_slot, chunk(at(plus, place), half, q, q), at(minus, here))

    def places(half):
        return (z, zm, zp, zf) if half == 0 else (y, ym, yp, yf)

    def first_at(half, a):
        return a * 4 + y if half == 0 else z * 4 + a

    def ag2_send(half, n):
        a = places(half)[n]
        ag_send(half, 1, 2 + n, first_at(half, a), places(half)[0])

    def ag2_near(half, n):
        ag_near(half, 1, 2 + n, 6, places(half)[n])

    def rotated(value):
        return value * cos[...] + pltpu.roll(value, HD // 2, 1) * sin[...]

    parity = t % 2

    near_chips, far_chips = [x, (x + 3) % 4, (x + 1) % 4], [(x + 2) % 4]
    near_shards = [2 * chip + b for chip in near_chips for b in range(2)]
    far_shards = [2 * chip + b for chip in far_chips for b in range(2)]

    def project(p, low, count, shards):
        term = None
        for i in shards:
            product = jnp.dot(
                scaled[2 * i + p // 2, :, pl.ds((p % 2) * PIECE, PIECE)],
                wbuf[i, pl.ds(p * PIECE, PIECE), pl.ds(low, count)],
                preferred_element_type=F32,
            )
            term = product if term is None else term + product
        acc[:, pl.ds(low, count)] += term

    def multiply(s, chips):
        for chip in chips:
            for b in range(2):
                term = jnp.dot(
                    ctx[...], obuf[s, 2 * chip + b], preferred_element_type=F32
                ).astype(BF)
                part[s, chip, 2 * b] = term[:, :HD]
                part[s, chip, 2 * b + 1] = term[:, HD:]

    def rs_put(s, half, k, src, dst, device):
        put(src, dst, rs_s.at[s, half], rs_r.at[s, half, k], (me, device))

    A = (0, QUARTER)
    B = (QUARTER, QUARTER)

    def block(s, half, a, rows):
        low, count = rows
        span = pl.ds(half * HALF + low, count)
        if half == 0:
            return part.at[s, a, :, span, :]
        return part.at[s, :, a, span, :]

    def devices(half, phase):
        if (half == 0) == (phase == 0):
            return zp * 4 + y, zm * 4 + y
        return z * 4 + yp, z * 4 + ym

    def ends(half, phase):
        if (half == 0) == (phase == 0):
            return z, zm, zp, zf
        return y, ym, yp, yf

    def span(rows):
        return pl.ds(rows[0], rows[1])

    def send_first(s):
        for half in range(2):
            own, minus, plus, opposite = ends(half, 0)
            up, down = devices(half, 0)
            rs_put(s, half, 0, block(s, half, opposite, A), r1.at[s, half, 0], up)
            rs_put(s, half, 0, block(s, half, opposite, B), r1.at[s, half, 1], down)
            rs_put(s, half, 1, block(s, half, plus, B), r2.at[s, half, 0, :, span(B), :], up)
            rs_put(s, half, 1, block(s, half, minus, A), r2.at[s, half, 1, :, span(A), :], down)

    def add_first(s, half):
        own, minus, plus, opposite = ends(half, 0)
        up, down = devices(half, 0)
        got(r1.at[s, half], rs_r.at[s, half, 0])
        for side, (a, rows, device) in enumerate(((plus, A, up), (minus, B, down))):
            view = block(s, half, a, rows)
            view[...] = (view[...].astype(F32) + r1[s, half, side].astype(F32)).astype(BF)
            rs_put(s, half, 1, view, r2.at[s, half, side, :, span(rows), :], device)

    def send_second(s, half):
        own, minus, plus, opposite = ends(half, 0)
        got(r2.at[s, half], rs_r.at[s, half, 1])
        view = block(s, half, own, (0, HALF))
        s1[s, half] = (
            view[...].astype(F32) + r2[s, half, 0].astype(F32) + r2[s, half, 1].astype(F32)
        ).astype(BF)
        own, minus, plus, opposite = ends(half, 1)
        up, down = devices(half, 1)
        to = lambda a, rows: s1.at[s, half, a, span(rows), :]
        if s in DIRECT:
            across = zf * 4 + y if half else z * 4 + yf
            rs_put(s, half, 2, to(opposite, A), q1.at[s, half, 0], across)
            rs_put(s, half, 2, to(opposite, B), q1.at[s, half, 1], across)
            rs_put(s, half, 3, to(plus, (0, HALF)), q2.at[s, half, 0], up)
            rs_put(s, half, 3, to(minus, (0, HALF)), q2.at[s, half, 1], down)
            return
        rs_put(s, half, 2, to(opposite, A), q1.at[s, half, 0], up)
        rs_put(s, half, 2, to(opposite, B), q1.at[s, half, 1], down)
        rs_put(s, half, 3, to(plus, B), q2.at[s, half, 0, span(B), :], up)
        rs_put(s, half, 3, to(minus, A), q2.at[s, half, 1, span(A), :], down)

    def add_second(s, half):
        own, minus, plus, opposite = ends(half, 1)
        up, down = devices(half, 1)
        got(q1.at[s, half], rs_r.at[s, half, 2])
        for side, (a, rows, device) in enumerate(((plus, A, up), (minus, B, down))):
            view = s1.at[s, half, a, span(rows), :]
            view[...] = (view[...].astype(F32) + q1[s, half, side].astype(F32)).astype(BF)
            rs_put(s, half, 3, view, q2.at[s, half, side, span(rows), :], device)

    def finish(s, half):
        own, minus, plus, opposite = ends(half, 1)
        got(q2.at[s, half], rs_r.at[s, half, 3])
        rows, cols = pl.ds(half * HALF, HALF), pl.ds(s * HD, HD)
        total = (
            act[t, rows, cols].astype(F32)
            + s1[s, half, own].astype(F32)
            + q2[s, half, 0].astype(F32)
            + q2[s, half, 1].astype(F32)
        )
        if s in DIRECT:
            got(q1.at[s, half], rs_r.at[s, half, 2])
            total = total + q1[s, half].reshape(HALF, HD).astype(F32)
        out[rows, cols] = total.astype(BF)
        pltpu.make_async_copy(out.at[rows, cols], result.at[rows, cols], out_sem).start()

    ag_send(0, 0, 0, t, None)
    ag_send(1, 0, 0, t, None)
    ag2_send(0, 0)
    ag2_send(1, 0)
    x_hand_on(0)
    x_near(0, (1, 0))
    x_far(0, (1, 1))
    ag_near(0, 0, 0, 1, other(0))
    ag2_send(0, 1)
    ag2_send(0, 2)
    ag_near(1, 0, 0, 1, other(1))
    ag2_send(1, 1)
    ag2_send(1, 2)
    x_sibling(0)
    x_hand_on(1)
    ag2_near(1, 0)
    ag2_near(0, 0)
    got(act.at[0, pl.ds(0 * HALF, HALF), :], ag_r.at[0, 1])
    ag2_send(0, 3)
    x_near(1, (2, 0))
    ag2_near(0, 1)
    x_far(1, (2, 1))
    ag2_near(1, 1)
    ag2_near(0, 2)
    x_sibling(1)
    x_hand_on(2)
    ag2_near(1, 2)
    got(act.at[0, pl.ds(1 * HALF, HALF), :], ag_r.at[1, 1])
    ag2_send(1, 3)
    x_near(2, (3, 0))
    x_far(2, (3, 1))
    ag2_near(0, 3)
    x_sibling(2)
    x_hand_on(3)
    ag2_near(1, 3)
    got(act.at[pl.ds(0, 4), pl.ds(0 * HALF, HALF), :], ag_r.at[0, 6])
    x_near(3, (4, 0))
    got(act.at[pl.ds(0, 4), pl.ds(1 * HALF, HALF), :], ag_r.at[1, 6])
    loaded(gain, local_sem.at[3])
    acc[...] = jnp.zeros_like(acc)
    squares[...] = jnp.zeros_like(squares)

    @pl.loop(0, 16)
    def _(tt):
        rows = act[tt].astype(F32)
        power = rows * rows
        squares[...] += (power[:, :HD] + power[:, HD:2 * HD]) + (
            power[:, 2 * HD:3 * HD] + power[:, 3 * HD:]
        )
        scaled[tt] = (rows * gain[tt]).astype(BF)

    squares[:, :1] = lax.rsqrt(
        jnp.sum(squares[...], axis=1, keepdims=True) * (1.0 / (16 * WIDE)) + EPSILON
    )
    x_far(3, (4, 1))
    project(0, 0, WIDE + HD, range(8))
    project(1, 0, WIDE + HD, range(8))
    x_hand_on(4)
    project(2, 0, WIDE + HD, range(8))
    x_sibling_near(3)
    project(3, 0, WIDE + HD, near_shards)
    x_near(4, (5, 0))
    x_sibling_far(3)
    project(3, WIDE, HD, far_shards)
    loaded(cos, local_sem.at[4])
    loaded(sin, local_sem.at[5])

    @pl.loop(0, TAKEN, unroll=True)
    def _(n):
        rows = pl.ds(n * ITEM_LEN, ITEM_LEN)
        value = acc[rows, pl.ds(WIDE, HD)] * squares[rows, :1]
        kvown[rows, :] = jnp.where(parity == 0, rotated(value), value).astype(BF)

    put(kvown.at[pl.ds(0 * HALF, HALF), :], kvpart.at[pl.ds(0 * HALF, HALF), :], kv_s, kv_r.at[0], (me, t + 1 - 2 * parity))
    put(kvown.at[pl.ds(1 * HALF, HALF), :], kvpart.at[pl.ds(1 * HALF, HALF), :], kv_s, kv_r.at[1], (me, t + 1 - 2 * parity))
    project(3, 0, WIDE, far_shards)

    @pl.loop(0, TAKEN, unroll=True)
    def _(n):
        rows = pl.ds(n * ITEM_LEN, ITEM_LEN)
        inverse = squares[rows, :1]
        for h in range(4):
            value = acc[rows, pl.ds(h * HD, HD)] * inverse
            qs[n, pl.ds(h * ITEM_LEN, ITEM_LEN), :] = rotated(value).astype(BF)

    x_far(4, (5, 1))
    got(kvpart.at[pl.ds(0 * HALF, HALF), :], kv_r.at[0])

    @pl.loop(0, 3, unroll=True)
    def _(n):
        rows = pl.ds(n * ITEM_LEN, ITEM_LEN)
        mine, theirs = kvown[rows, :], kvpart[rows, :]
        keys = jnp.where(parity == 0, mine, theirs)
        values = jnp.where(parity == 0, theirs, mine)
        scores = lax.dot_general(
            qs[n], keys, (((1,), (1,)), ((), ())), preferred_element_type=F32
        ) * (HD ** -0.5)
        place = lax.broadcasted_iota(jnp.int32, scores.shape, 0) % ITEM_LEN
        scores = jnp.where(
            place >= lax.broadcasted_iota(jnp.int32, scores.shape, 1), scores, -1e30
        )
        raised = jnp.exp(scores - jnp.max(scores, axis=1, keepdims=True))
        probs = (raised * (1.0 / jnp.sum(raised, axis=1, keepdims=True))).astype(BF)
        context = jnp.dot(probs, values, preferred_element_type=F32).astype(BF)
        for h in range(4):
            ctx[rows, pl.ds(h * HD, HD)] = context[h * ITEM_LEN:(h + 1) * ITEM_LEN, :]

    got(kvpart.at[pl.ds(1 * HALF, HALF), :], kv_r.at[1])

    @pl.loop(3, 6, unroll=True)
    def _(n):
        rows = pl.ds(n * ITEM_LEN, ITEM_LEN)
        mine, theirs = kvown[rows, :], kvpart[rows, :]
        keys = jnp.where(parity == 0, mine, theirs)
        values = jnp.where(parity == 0, theirs, mine)
        scores = lax.dot_general(
            qs[n], keys, (((1,), (1,)), ((), ())), preferred_element_type=F32
        ) * (HD ** -0.5)
        place = lax.broadcasted_iota(jnp.int32, scores.shape, 0) % ITEM_LEN
        scores = jnp.where(
            place >= lax.broadcasted_iota(jnp.int32, scores.shape, 1), scores, -1e30
        )
        raised = jnp.exp(scores - jnp.max(scores, axis=1, keepdims=True))
        probs = (raised * (1.0 / jnp.sum(raised, axis=1, keepdims=True))).astype(BF)
        context = jnp.dot(probs, values, preferred_element_type=F32).astype(BF)
        for h in range(4):
            ctx[rows, pl.ds(h * HD, HD)] = context[h * ITEM_LEN:(h + 1) * ITEM_LEN, :]

    x_hand_on(5)
    x_sibling_near(4)
    multiply(0, near_chips)
    x_sibling_far(4)
    multiply(0, far_chips)
    send_first(0)
    x_near(5, (6, 0))
    x_far(5, (6, 1))
    add_first(0, 0)
    add_first(0, 1)
    x_sibling_near(5)
    multiply(1, near_chips)
    x_sibling_far(5)
    multiply(1, far_chips)
    send_first(1)
    x_hand_on(6)
    send_second(0, 0)
    send_second(0, 1)
    x_near(6, (7, 0))
    add_first(1, 0)
    add_first(1, 1)
    x_far(6, (7, 1))
    x_sibling_near(6)
    multiply(2, near_chips)
    add_second(0, 1)
    add_second(0, 0)
    x_sibling_far(6)
    multiply(2, far_chips)
    send_first(2)
    x_hand_on(7)
    send_second(1, 0)
    send_second(1, 1)
    finish(0, 0)
    finish(0, 1)
    x_near(7)
    add_first(2, 0)
    add_first(2, 1)
    x_far(7)
    x_sibling_near(7)
    multiply(3, near_chips)
    add_second(1, 1)
    add_second(1, 0)
    x_sibling_far(7)
    multiply(3, far_chips)
    send_first(3)
    send_second(2, 0)
    send_second(2, 1)
    finish(1, 0)
    finish(1, 1)
    add_first(3, 0)
    add_first(3, 1)
    add_second(2, 1)
    add_second(2, 0)
    send_second(3, 0)
    send_second(3, 1)
    finish(2, 0)
    finish(2, 1)
    finish(3, 0)
    finish(3, 1)

    sent(meta.at[pl.ds(0, 7)], meta_s)
    sent(outgoing.at[pl.ds(0, 7)], route_s)
    for r in range(8):
        sent(shares(r, 7), x_s.at[r])
    for half in range(2):
        sent(act.at[pl.ds(0, 15), pl.ds(half * HALF, HALF), :], ag_s.at[half])
    sent(kvown, kv_s)
    terms = part.reshape(64, ROWS, HD)
    for s in range(4):
        for half in range(2):
            sent(terms.at[pl.ds(16 * s, 15), pl.ds(0, HALF), :], rs_s.at[s, half])
    loaded(out, out_sem)


def shards(hidden, exited, destination, norm_gain, query_weight, keyvalue_weight, output_weight):
    cos, sin = tables()
    smem = pl.BlockSpec(memory_space=pltpu.SMEM)
    hbm = pl.BlockSpec(memory_space=pl.ANY)
    dma = pltpu.SemaphoreType.DMA
    return pl.pallas_call(
        kernel,
        out_shape=jax.ShapeDtypeStruct((ROWS, WIDE), BF),
        in_specs=[smem, smem, hbm, hbm, hbm, hbm, hbm, hbm, hbm],
        out_specs=hbm,
        scratch_shapes=[
            pltpu.VMEM((16, 1, WIDE), F32),
            pltpu.VMEM((ITEM_LEN, HD), F32),
            pltpu.VMEM((ITEM_LEN, HD), F32),
            pltpu.VMEM((ROWS, WIDE), BF),
            pltpu.VMEM((HERE, ITEM_LEN, WIDE), BF),
            pltpu.VMEM((8, 2, ITEM_LEN, WIDE), BF),
            pltpu.VMEM((8, 2, ITEM_LEN, WIDE), BF),
            pltpu.VMEM((8, 8, 128), jnp.int32),
            pltpu.SMEM((8, 8, 128), jnp.int32),
            pltpu.VMEM((16, ROWS, WIDE), BF),
            pltpu.VMEM((16, ROWS, WIDE), BF),
            pltpu.VMEM((8, DEPTH, WIDE + HD), BF),
            pltpu.VMEM((4, 8, WIDE, 2 * HD), BF),
            pltpu.VMEM((ROWS, WIDE + HD), F32),
            pltpu.VMEM((ROWS, HD), F32),
            pltpu.VMEM((TAKEN, 4 * ITEM_LEN, HD), BF),
            pltpu.VMEM((ROWS, HD), BF),
            pltpu.VMEM((ROWS, HD), BF),
            pltpu.VMEM((ROWS, WIDE), BF),
            pltpu.VMEM((4, 4, 4, ROWS, HD), BF),
            pltpu.VMEM((4, 2, 2, 4, QUARTER, HD), BF),
            pltpu.VMEM((4, 2, 2, 4, HALF, HD), BF),
            pltpu.VMEM((4, 2, 4, HALF, HD), BF),
            pltpu.VMEM((4, 2, 2, QUARTER, HD), BF),
            pltpu.VMEM((4, 2, 2, HALF, HD), BF),
            dma((7,)),
            dma(()),
            dma(()),
            dma(()),
            dma(()),
            dma(()),
            dma((8,)),
            dma((8, 5)),
            dma((2,)),
            dma((2, 7)),
            dma((4, 2)),
            dma((4, 2, 4)),
            dma(()),
            dma((2,)),
        ],
        compiler_params=pltpu.CompilerParams(
            collective_id=0, has_side_effects=True, vmem_limit_bytes=60 * 1024 * 1024
        ),
        cost_estimate=pl.CostEstimate(
            flops=2 * ROWS * 16 * WIDE * (2 * WIDE + HD),
            bytes_accessed=8 * 1024 * 1024,
            transcendentals=ROWS * 4 * ITEM_LEN,
        ),
    )(
        exited,
        destination,
        hidden.reshape(HERE, ITEM_LEN, WIDE),
        norm_gain.reshape(16, 1, WIDE),
        query_weight,
        keyvalue_weight,
        output_weight,
        jnp.asarray(cos),
        jnp.asarray(sin),
    )


def solution(mesh):
    placed = (
        P("dp", "tensor"),
        P("dp"),
        P("dp"),
        P(),
        P("dp", "tensor"),
        P("dp", "tensor"),
        P("tensor", "dp"),
    )
    return jax.shard_map(
        shards, mesh=mesh, in_specs=placed, out_specs=P("dp", "tensor"), check_vma=False
    )
```

```python
import functools

import jax
import jax.numpy as jnp
import numpy as np
from jax import lax
from jax.experimental import pallas as pl
from jax.experimental.pallas import tpu as pltpu
from jax.sharding import PartitionSpec as P

MESH = pl.DeviceIdType.MESH

HD = 128
ITEM_LEN = 64
HERE = 16
TAKEN = 6
ROWS = TAKEN * ITEM_LEN
WIDE = 512
DEPTH = 1024
EPSILON = 1e-05
THETA = 500000.0
BF = jnp.bfloat16
F32 = jnp.float32

PIECE = DEPTH // 4
HALF = ROWS // 2
QUARTER = ROWS // 4
DIRECT = (3,)


def tables():
    j = np.arange(HD // 2, dtype=np.float64)
    freq = (THETA ** (-2.0 * j / HD)).astype(np.float32)
    phase = (np.arange(ITEM_LEN, dtype=np.float32)[:, None] * freq).astype(np.float64)
    cos, sin = np.cos(phase), np.sin(phase)
    return (
        np.concatenate([cos, cos], axis=1).astype(np.float32),
        np.concatenate([-sin, sin], axis=1).astype(np.float32),
    )


def kernel(
    exited_in, destination_in, hidden, gain_in, wq, wkv, wo, cos_in, sin_in, result,
    exited, destination, gain, cos, sin, out,
    hid, outgoing, arrived, meta, meta_scalar, act, scaled, wbuf, obuf, acc, squares, qs, kvown, kvpart,
    ctx, part, r1, r2, s1, q1, q2,
    local_sem, out_sem, meta_s, meta_r, route_s, route_r, x_s, x_r, ag_s, ag_r, rs_s, rs_r, kv_s, kv_r,
):
    me = lax.axis_index("dp")
    t = lax.axis_index("tensor")
    x, c = me // 2, me % 2
    z, y = t // 4, t % 4
    left = ((x + 3) % 4) * 2 + c
    right = ((x + 1) % 4) * 2 + c
    far = ((x + 2) % 4) * 2 + c
    zp, zm, zf = (z + 1) % 4, (z + 3) % 4, (z + 2) % 4
    yp, ym, yf = (y + 1) % 4, (y + 3) % 4, (y + 2) % 4

    def sibling(i):
        return i + 1 - 2 * c

    sib = sibling(me)

    def put(src, dst, send, recv, device):
        copy = pltpu.make_async_remote_copy(
            src_ref=src, dst_ref=dst, send_sem=send, recv_sem=recv,
            device_id=device, device_id_type=MESH,
        )
        copy.start()

    def got(dst, recv):
        pltpu.make_async_remote_copy(
            src_ref=dst, dst_ref=dst, send_sem=recv, recv_sem=recv,
            device_id=(sib, t), device_id_type=MESH,
        ).wait_recv()

    def sent(src, send):
        pltpu.make_async_remote_copy(
            src_ref=src, dst_ref=src, send_sem=send, recv_sem=send,
            device_id=(sib, t), device_id_type=MESH,
        ).wait_send()

    def loaded(dst, sem):
        pltpu.make_async_copy(dst, dst, sem).wait()

    barrier = pltpu.get_barrier_semaphore()
    peers = [((me + k) % 8, t) for k in (4, 3, 5, 2, 6, 1, 7)]
    peers += [(me, zf * 4 + y), (me, z * 4 + yf)]
    peers += [(me, zp * 4 + y), (me, zm * 4 + y), (me, z * 4 + yp), (me, z * 4 + ym)]
    for peer in peers:
        pl.semaphore_signal(barrier, inc=1, device_id=peer, device_id_type=MESH)

    flags = [
        pltpu.make_async_copy(exited_in, exited, local_sem.at[7]),
        pltpu.make_async_copy(destination_in, destination, local_sem.at[8]),
    ]
    for flag in flags:
        flag.start()
    loads = [pltpu.make_async_copy(hidden, hid, local_sem.at[0])]
    loads.append(pltpu.make_async_copy(wq, wbuf.at[me, :, pl.ds(0, WIDE)], local_sem.at[1]))
    loads.append(pltpu.make_async_copy(wkv, wbuf.at[me, :, pl.ds(WIDE, HD)], local_sem.at[1]))
    for s in range(4):
        for h in range(2):
            loads.append(
                pltpu.make_async_copy(
                    wo.at[:, pl.ds(h * WIDE + s * HD, HD)],
                    obuf.at[s, me, :, pl.ds(h * HD, HD)],
                    local_sem.at[2],
                )
            )
    loads.append(pltpu.make_async_copy(gain_in, gain, local_sem.at[3]))
    loads.append(pltpu.make_async_copy(cos_in, cos, local_sem.at[4]))
    loads.append(pltpu.make_async_copy(sin_in, sin, local_sem.at[5]))
    for load in loads:
        load.start()

    def weights(r, i, low=0, count=None):
        if r < 4:
            return wbuf.at[i, pl.ds(r * PIECE + low, count or PIECE), :]
        return obuf.at[r - 4, i, pl.ds(low, count or WIDE), :]

    def half_of(r):
        return PIECE // 2 if r < 4 else WIDE // 2

    def x_put(r, k, view, device):
        put(view, view, x_s.at[r], x_r.at[r, k], (device, t))

    def shares(r, count):
        if r < 4:
            return wbuf.at[pl.ds(0, count), pl.ds(r * PIECE, PIECE), :]
        return obuf.at[r - 4, pl.ds(0, count)]

    def x_own_sibling(r):
        x_put(r, 3, weights(r, me), sib)

    def x_own(r, which):
        n = half_of(r)
        x_put(r, which, weights(r, me, which * n, n), right)
        x_put(r, which, weights(r, me, n - which * n, n), left)

    def x_hand_on(r):
        n = half_of(r)
        got(shares(r, 1), x_r.at[r, 0])
        x_put(r, 2, weights(r, left, 0, n), right)
        x_put(r, 2, weights(r, right, n, n), left)

    def x_near(r, *after):
        got(shares(r, 1), x_r.at[r, 1])
        for piece in after:
            x_own(*piece)
        x_put(r, 3, weights(r, left), sib)
        x_put(r, 3, weights(r, right), sib)

    def x_far(r, *after):
        got(shares(r, 1), x_r.at[r, 2])
        for piece in after:
            x_own(*piece)
        x_put(r, 4, weights(r, far), sib)

    def x_sibling_near(r):
        got(shares(r, 3), x_r.at[r, 3])

    def x_sibling_far(r):
        got(shares(r, 1), x_r.at[r, 4])

    def x_sibling(r):
        x_sibling_near(r)
        x_sibling_far(r)

    for flag in flags:
        flag.wait()
    codes = [jnp.where(exited[k] == 0, destination[k], -1) for k in range(HERE)]
    lane = lax.broadcasted_iota(jnp.int32, (8, 128), 1)
    row = jnp.full((8, 128), -1, jnp.int32)
    for k in range(HERE):
        row = jnp.where(lane == k, codes[k], row)
    meta[me] = row
    loads[0].wait()
    for k in range(8):
        dest = (me + k) % 8 if k else me
        seen = jnp.int32(0)
        first = jnp.int32(0)
        second = jnp.int32(0)
        for item in range(HERE):
            hit = codes[item] == dest
            first = jnp.where(hit & (seen == 0), item, first)
            second = jnp.where(hit & (seen == 1), item, second)
            seen = seen + jnp.where(hit, 1, 0)
        if k:
            outgoing[dest, 0] = hid[first]
            outgoing[dest, 1] = hid[second]
        else:
            arrived[me, 0] = hid[first]
            arrived[me, 1] = hid[second]
    loaded(wbuf.at[me], local_sem.at[1])
    pl.semaphore_wait(barrier, len(peers))

    for k in range(1, 8):
        put(meta.at[me], meta.at[me], meta_s, meta_r, ((me + k) % 8, t))
    for k in (4, 2, 6, 3, 5, 1, 7):
        put(outgoing.at[(me + k) % 8], arrived.at[me], route_s, route_r, ((me + k) % 8, t))
    x_own(0, 0)
    x_own(0, 1)
    for r in range(4):
        x_own_sibling(r)
    loaded(obuf.at[pl.ds(0, 4), me], local_sem.at[2])
    for r in range(4, 8):
        x_own_sibling(r)

    got(meta.at[pl.ds(0, 7)], meta_r)
    to_scalar = pltpu.make_async_copy(meta, meta_scalar, local_sem.at[6])
    to_scalar.start()
    to_scalar.wait()
    picks = [jnp.int32(0)] * TAKEN
    rank = jnp.int32(0)
    for j in range(8):
        count = jnp.int32(0)
        for item in range(HERE):
            count = count + jnp.where(meta_scalar[j, 0, item] == me, 1, 0)
        for s in range(2):
            valid = count > s
            for r in range(TAKEN):
                picks[r] = jnp.where(valid & (rank == r), 2 * j + s, picks[r])
            rank = rank + jnp.where(valid, 1, 0)

    got(arrived.at[pl.ds(0, 7)], route_r)
    flat = arrived.reshape(16, ITEM_LEN, WIDE)
    for r in range(TAKEN):
        act[t, pl.ds(r * ITEM_LEN, ITEM_LEN), :] = flat[picks[r]]

    def line(half, phase):
        along_z = (half == 0) == (phase == 0)
        if along_z:
            return (z, zm, zp, zf), lambda a, b: a * 4 + b
        return (y, ym, yp, yf), lambda a, b: b * 4 + a

    def chunk(tt, half, low=0, count=HALF):
        return act.at[tt, pl.ds(half * HALF + low, count), :]

    def ag_put(half, k, view, device):
        put(view, view, ag_s.at[half], ag_r.at[half, k], (me, device))

    def other(half):
        return y if half == 0 else z

    def ag_send(half, phase, slot, tt, near):
        (own, minus, plus, opposite), at = line(half, phase)
        place = other(half) if phase == 0 else near
        ag_put(half, slot, chunk(tt, half), at(plus, place))
        ag_put(half, slot, chunk(tt, half), at(minus, place))

    def ag_near(half, phase, slot, far_slot, place):
        (own, minus, plus, opposite), at = line(half, phase)
        got(act.at[pl.ds(0, 2), pl.ds(half * HALF, HALF), :], ag_r.at[half, slot])
        q = HALF // 2
        here = other(half) if phase == 0 else (z if half == 0 else y)
        ag_put(half, far_slot, chunk(at(minus, place), half, 0, q), at(plus, here))
        ag_put(half, far_slot, chunk(at(plus, place), half, q, q), at(minus, here))

    def places(half):
        return (z, zm, zp, zf) if half == 0 else (y, ym, yp, yf)

    def first_at(half, a):
        return a * 4 + y if half == 0 else z * 4 + a

    def ag2_send(half, n):
        a = places(half)[n]
        ag_send(half, 1, 2 + n, first_at(half, a), places(half)[0])

    def ag2_near(half, n):
        ag_near(half, 1, 2 + n, 6, places(half)[n])

    def rotated(value):
        return value * cos[...] + pltpu.roll(value, HD // 2, 1) * sin[...]

    parity = t % 2

    near_chips, far_chips = [x, (x + 3) % 4, (x + 1) % 4], [(x + 2) % 4]
    near_shards = [2 * chip + b for chip in near_chips for b in range(2)]
    far_shards = [2 * chip + b for chip in far_chips for b in range(2)]

    def project(p, low, count, shards):
        term = None
        for i in shards:
            product = jnp.dot(
                scaled[2 * i + p // 2, :, pl.ds((p % 2) * PIECE, PIECE)],
                wbuf[i, pl.ds(p * PIECE, PIECE), pl.ds(low, count)],
                preferred_element_type=F32,
            )
            term = product if term is None else term + product
        acc[:, pl.ds(low, count)] += term

    def multiply(s, chips):
        for chip in chips:
            for b in range(2):
                term = jnp.dot(
                    ctx[...], obuf[s, 2 * chip + b], preferred_element_type=F32
                ).astype(BF)
                part[s, chip, 2 * b] = term[:, :HD]
                part[s, chip, 2 * b + 1] = term[:, HD:]

    def rs_put(s, half, k, src, dst, device):
        put(src, dst, rs_s.at[s, half], rs_r.at[s, half, k], (me, device))

    A = (0, QUARTER)
    B = (QUARTER, QUARTER)

    def block(s, half, a, rows):
        low, count = rows
        span = pl.ds(half * HALF + low, count)
        if half == 0:
            return part.at[s, a, :, span, :]
        return part.at[s, :, a, span, :]

    def devices(half, phase):
        if (half == 0) == (phase == 0):
            return zp * 4 + y, zm * 4 + y
        return z * 4 + yp, z * 4 + ym

    def ends(half, phase):
        if (half == 0) == (phase == 0):
            return z, zm, zp, zf
        return y, ym, yp, yf

    def span(rows):
        return pl.ds(rows[0], rows[1])

    def send_first(s):
        for half in range(2):
            own, minus, plus, opposite = ends(half, 0)
            up, down = devices(half, 0)
            rs_put(s, half, 0, block(s, half, opposite, A), r1.at[s, half, 0], up)
            rs_put(s, half, 0, block(s, half, opposite, B), r1.at[s, half, 1], down)
            rs_put(s, half, 1, block(s, half, plus, B), r2.at[s, half, 0, :, span(B), :], up)
            rs_put(s, half, 1, block(s, half, minus, A), r2.at[s, half, 1, :, span(A), :], down)

    def add_first(s, half):
        own, minus, plus, opposite = ends(half, 0)
        up, down = devices(half, 0)
        got(r1.at[s, half], rs_r.at[s, half, 0])
        for side, (a, rows, device) in enumerate(((plus, A, up), (minus, B, down))):
            view = block(s, half, a, rows)
            view[...] = (view[...].astype(F32) + r1[s, half, side].astype(F32)).astype(BF)
            rs_put(s, half, 1, view, r2.at[s, half, side, :, span(rows), :], device)

    def send_second(s, half):
        own, minus, plus, opposite = ends(half, 0)
        got(r2.at[s, half], rs_r.at[s, half, 1])
        view = block(s, half, own, (0, HALF))
        s1[s, half] = (
            view[...].astype(F32) + r2[s, half, 0].astype(F32) + r2[s, half, 1].astype(F32)
        ).astype(BF)
        own, minus, plus, opposite = ends(half, 1)
        up, down = devices(half, 1)
        to = lambda a, rows: s1.at[s, half, a, span(rows), :]
        if s in DIRECT:
            across = zf * 4 + y if half else z * 4 + yf
            rs_put(s, half, 2, to(opposite, A), q1.at[s, half, 0], across)
            rs_put(s, half, 2, to(opposite, B), q1.at[s, half, 1], across)
            rs_put(s, half, 3, to(plus, (0, HALF)), q2.at[s, half, 0], up)
            rs_put(s, half, 3, to(minus, (0, HALF)), q2.at[s, half, 1], down)
            return
        rs_put(s, half, 2, to(opposite, A), q1.at[s, half, 0], up)
        rs_put(s, half, 2, to(opposite, B), q1.at[s, half, 1], down)
        rs_put(s, half, 3, to(plus, B), q2.at[s, half, 0, span(B), :], up)
        rs_put(s, half, 3, to(minus, A), q2.at[s, half, 1, span(A), :], down)

    def add_second(s, half):
        own, minus, plus, opposite = ends(half, 1)
        up, down = devices(half, 1)
        got(q1.at[s, half], rs_r.at[s, half, 2])
        for side, (a, rows, device) in enumerate(((plus, A, up), (minus, B, down))):
            view = s1.at[s, half, a, span(rows), :]
            view[...] = (view[...].astype(F32) + q1[s, half, side].astype(F32)).astype(BF)
            rs_put(s, half, 3, view, q2.at[s, half, side, span(rows), :], device)

    def finish(s, half):
        own, minus, plus, opposite = ends(half, 1)
        got(q2.at[s, half], rs_r.at[s, half, 3])
        rows, cols = pl.ds(half * HALF, HALF), pl.ds(s * HD, HD)
        total = (
            act[t, rows, cols].astype(F32)
            + s1[s, half, own].astype(F32)
            + q2[s, half, 0].astype(F32)
            + q2[s, half, 1].astype(F32)
        )
        if s in DIRECT:
            got(q1.at[s, half], rs_r.at[s, half, 2])
            total = total + q1[s, half].reshape(HALF, HD).astype(F32)
        out[rows, cols] = total.astype(BF)
        pltpu.make_async_copy(out.at[rows, cols], result.at[rows, cols], out_sem).start()

    ag_send(0, 0, 0, t, None)
    ag_send(1, 0, 0, t, None)
    ag2_send(0, 0)
    ag2_send(1, 0)
    x_hand_on(0)
    x_near(0, (1, 0))
    ag_near(0, 0, 0, 1, other(0))
    ag2_send(0, 1)
    ag2_send(0, 2)
    ag_near(1, 0, 0, 1, other(1))
    ag2_send(1, 1)
    ag2_send(1, 2)
    x_far(0, (1, 1))
    ag2_near(1, 0)
    ag2_near(0, 0)
    x_sibling(0)
    got(act.at[0, pl.ds(0 * HALF, HALF), :], ag_r.at[0, 1])
    ag2_send(0, 3)
    x_hand_on(1)
    ag2_near(0, 1)
    x_near(1, (2, 0))
    ag2_near(1, 1)
    ag2_near(0, 2)
    x_far(1, (2, 1))
    ag2_near(1, 2)
    got(act.at[0, pl.ds(1 * HALF, HALF), :], ag_r.at[1, 1])
    ag2_send(1, 3)
    x_sibling(1)
    x_hand_on(2)
    x_near(2, (3, 0))
    ag2_near(0, 3)
    x_far(2, (3, 1))
    ag2_near(1, 3)
    x_sibling(2)
    got(act.at[pl.ds(0, 4), pl.ds(0 * HALF, HALF), :], ag_r.at[0, 6])
    x_hand_on(3)
    got(act.at[pl.ds(0, 4), pl.ds(1 * HALF, HALF), :], ag_r.at[1, 6])
    loaded(gain, local_sem.at[3])
    acc[...] = jnp.zeros_like(acc)
    squares[...] = jnp.zeros_like(squares)

    @pl.loop(0, 16)
    def _(tt):
        rows = act[tt].astype(F32)
        power = rows * rows
        squares[...] += (power[:, :HD] + power[:, HD:2 * HD]) + (
            power[:, 2 * HD:3 * HD] + power[:, 3 * HD:]
        )
        scaled[tt] = (rows * gain[tt]).astype(BF)

    squares[:, :1] = lax.rsqrt(
        jnp.sum(squares[...], axis=1, keepdims=True) * (1.0 / (16 * WIDE)) + EPSILON
    )
    x_near(3, (4, 0))
    project(0, 0, WIDE + HD, range(8))
    project(1, 0, WIDE + HD, range(8))
    x_far(3, (4, 1))
    project(2, 0, WIDE + HD, range(8))
    x_sibling_near(3)
    project(3, 0, WIDE + HD, near_shards)
    x_hand_on(4)
    x_sibling_far(3)
    project(3, WIDE, HD, far_shards)
    loaded(cos, local_sem.at[4])
    loaded(sin, local_sem.at[5])

    @pl.loop(0, TAKEN, unroll=True)
    def _(n):
        rows = pl.ds(n * ITEM_LEN, ITEM_LEN)
        value = acc[rows, pl.ds(WIDE, HD)] * squares[rows, :1]
        kvown[rows, :] = jnp.where(parity == 0, rotated(value), value).astype(BF)

    put(kvown.at[pl.ds(0 * HALF, HALF), :], kvpart.at[pl.ds(0 * HALF, HALF), :], kv_s, kv_r.at[0], (me, t + 1 - 2 * parity))
    put(kvown.at[pl.ds(1 * HALF, HALF), :], kvpart.at[pl.ds(1 * HALF, HALF), :], kv_s, kv_r.at[1], (me, t + 1 - 2 * parity))
    project(3, 0, WIDE, far_shards)

    @pl.loop(0, TAKEN, unroll=True)
    def _(n):
        rows = pl.ds(n * ITEM_LEN, ITEM_LEN)
        inverse = squares[rows, :1]
        for h in range(4):
            value = acc[rows, pl.ds(h * HD, HD)] * inverse
            qs[n, pl.ds(h * ITEM_LEN, ITEM_LEN), :] = rotated(value).astype(BF)

    x_near(4, (5, 0))
    got(kvpart.at[pl.ds(0 * HALF, HALF), :], kv_r.at[0])

    @pl.loop(0, 3, unroll=True)
    def _(n):
        rows = pl.ds(n * ITEM_LEN, ITEM_LEN)
        mine, theirs = kvown[rows, :], kvpart[rows, :]
        keys = jnp.where(parity == 0, mine, theirs)
        values = jnp.where(parity == 0, theirs, mine)
        scores = lax.dot_general(
            qs[n], keys, (((1,), (1,)), ((), ())), preferred_element_type=F32
        ) * (HD ** -0.5)
        place = lax.broadcasted_iota(jnp.int32, scores.shape, 0) % ITEM_LEN
        scores = jnp.where(
            place >= lax.broadcasted_iota(jnp.int32, scores.shape, 1), scores, -1e30
        )
        raised = jnp.exp(scores - jnp.max(scores, axis=1, keepdims=True))
        probs = (raised * (1.0 / jnp.sum(raised, axis=1, keepdims=True))).astype(BF)
        context = jnp.dot(probs, values, preferred_element_type=F32).astype(BF)
        for h in range(4):
            ctx[rows, pl.ds(h * HD, HD)] = context[h * ITEM_LEN:(h + 1) * ITEM_LEN, :]

    got(kvpart.at[pl.ds(1 * HALF, HALF), :], kv_r.at[1])

    @pl.loop(3, 6, unroll=True)
    def _(n):
        rows = pl.ds(n * ITEM_LEN, ITEM_LEN)
        mine, theirs = kvown[rows, :], kvpart[rows, :]
        keys = jnp.where(parity == 0, mine, theirs)
        values = jnp.where(parity == 0, theirs, mine)
        scores = lax.dot_general(
            qs[n], keys, (((1,), (1,)), ((), ())), preferred_element_type=F32
        ) * (HD ** -0.5)
        place = lax.broadcasted_iota(jnp.int32, scores.shape, 0) % ITEM_LEN
        scores = jnp.where(
            place >= lax.broadcasted_iota(jnp.int32, scores.shape, 1), scores, -1e30
        )
        raised = jnp.exp(scores - jnp.max(scores, axis=1, keepdims=True))
        probs = (raised * (1.0 / jnp.sum(raised, axis=1, keepdims=True))).astype(BF)
        context = jnp.dot(probs, values, preferred_element_type=F32).astype(BF)
        for h in range(4):
            ctx[rows, pl.ds(h * HD, HD)] = context[h * ITEM_LEN:(h + 1) * ITEM_LEN, :]

    x_far(4, (5, 1))
    x_sibling_near(4)
    multiply(0, near_chips)
    x_sibling_far(4)
    multiply(0, far_chips)
    send_first(0)
    x_hand_on(5)
    x_near(5, (6, 0))
    add_first(0, 0)
    add_first(0, 1)
    x_far(5, (6, 1))
    x_sibling_near(5)
    multiply(1, near_chips)
    x_sibling_far(5)
    multiply(1, far_chips)
    send_first(1)
    x_hand_on(6)
    send_second(0, 0)
    send_second(0, 1)
    x_near(6, (7, 0))
    add_first(1, 0)
    add_first(1, 1)
    x_far(6, (7, 1))
    x_sibling_near(6)
    multiply(2, near_chips)
    add_second(0, 1)
    add_second(0, 0)
    x_sibling_far(6)
    multiply(2, far_chips)
    send_first(2)
    x_hand_on(7)
    send_second(1, 0)
    send_second(1, 1)
    finish(0, 0)
    finish(0, 1)
    x_near(7)
    add_first(2, 0)
    add_first(2, 1)
    x_far(7)
    x_sibling_near(7)
    multiply(3, near_chips)
    add_second(1, 1)
    add_second(1, 0)
    x_sibling_far(7)
    multiply(3, far_chips)
    send_first(3)
    send_second(2, 0)
    send_second(2, 1)
    finish(1, 0)
    finish(1, 1)
    add_first(3, 0)
    add_first(3, 1)
    add_second(2, 1)
    add_second(2, 0)
    send_second(3, 0)
    send_second(3, 1)
    finish(2, 0)
    finish(2, 1)
    finish(3, 0)
    finish(3, 1)

    sent(meta.at[pl.ds(0, 7)], meta_s)
    sent(outgoing.at[pl.ds(0, 7)], route_s)
    for r in range(8):
        sent(shares(r, 7), x_s.at[r])
    for half in range(2):
        sent(act.at[pl.ds(0, 15), pl.ds(half * HALF, HALF), :], ag_s.at[half])
    sent(kvown, kv_s)
    terms = part.reshape(64, ROWS, HD)
    for s in range(4):
        for half in range(2):
            sent(terms.at[pl.ds(16 * s, 15), pl.ds(0, HALF), :], rs_s.at[s, half])
    loaded(out, out_sem)


def shards(hidden, exited, destination, norm_gain, query_weight, keyvalue_weight, output_weight):
    cos, sin = tables()
    hbm = pl.BlockSpec(memory_space=pl.ANY)
    dma = pltpu.SemaphoreType.DMA
    return pl.pallas_call(
        kernel,
        out_shape=jax.ShapeDtypeStruct((ROWS, WIDE), BF),
        in_specs=[hbm, hbm, hbm, hbm, hbm, hbm, hbm, hbm, hbm],
        out_specs=hbm,
        scratch_shapes=[
            pltpu.SMEM((HERE,), jnp.int32),
            pltpu.SMEM((HERE,), jnp.int32),
            pltpu.VMEM((16, 1, WIDE), F32),
            pltpu.VMEM((ITEM_LEN, HD), F32),
            pltpu.VMEM((ITEM_LEN, HD), F32),
            pltpu.VMEM((ROWS, WIDE), BF),
            pltpu.VMEM((HERE, ITEM_LEN, WIDE), BF),
            pltpu.VMEM((8, 2, ITEM_LEN, WIDE), BF),
            pltpu.VMEM((8, 2, ITEM_LEN, WIDE), BF),
            pltpu.VMEM((8, 8, 128), jnp.int32),
            pltpu.SMEM((8, 8, 128), jnp.int32),
            pltpu.VMEM((16, ROWS, WIDE), BF),
            pltpu.VMEM((16, ROWS, WIDE), BF),
            pltpu.VMEM((8, DEPTH, WIDE + HD), BF),
            pltpu.VMEM((4, 8, WIDE, 2 * HD), BF),
            pltpu.VMEM((ROWS, WIDE + HD), F32),
            pltpu.VMEM((ROWS, HD), F32),
            pltpu.VMEM((TAKEN, 4 * ITEM_LEN, HD), BF),
            pltpu.VMEM((ROWS, HD), BF),
            pltpu.VMEM((ROWS, HD), BF),
            pltpu.VMEM((ROWS, WIDE), BF),
            pltpu.VMEM((4, 4, 4, ROWS, HD), BF),
            pltpu.VMEM((4, 2, 2, 4, QUARTER, HD), BF),
            pltpu.VMEM((4, 2, 2, 4, HALF, HD), BF),
            pltpu.VMEM((4, 2, 4, HALF, HD), BF),
            pltpu.VMEM((4, 2, 2, QUARTER, HD), BF),
            pltpu.VMEM((4, 2, 2, HALF, HD), BF),
            dma((9,)),
            dma(()),
            dma(()),
            dma(()),
            dma(()),
            dma(()),
            dma((8,)),
            dma((8, 5)),
            dma((2,)),
            dma((2, 7)),
            dma((4, 2)),
            dma((4, 2, 4)),
            dma(()),
            dma((2,)),
        ],
        compiler_params=pltpu.CompilerParams(
            collective_id=0, has_side_effects=True, vmem_limit_bytes=60 * 1024 * 1024
        ),
        cost_estimate=pl.CostEstimate(
            flops=2 * ROWS * 16 * WIDE * (2 * WIDE + HD),
            bytes_accessed=8 * 1024 * 1024,
            transcendentals=ROWS * 4 * ITEM_LEN,
        ),
    )(
        exited,
        destination,
        hidden.reshape(HERE, ITEM_LEN, WIDE),
        norm_gain.reshape(16, 1, WIDE),
        query_weight,
        keyvalue_weight,
        output_weight,
        jnp.asarray(cos),
        jnp.asarray(sin),
    )


def solution(mesh):
    placed = (
        P("dp", "tensor"),
        P("dp"),
        P("dp"),
        P(),
        P("dp", "tensor"),
        P("dp", "tensor"),
        P("tensor", "dp"),
    )
    return jax.shard_map(
        shards, mesh=mesh, in_specs=placed, out_specs=P("dp", "tensor"), check_vma=False
    )
```

```python
import functools

import jax
import jax.numpy as jnp
import numpy as np
from jax import lax
from jax.experimental import pallas as pl
from jax.experimental.pallas import tpu as pltpu
from jax.sharding import PartitionSpec as P

MESH = pl.DeviceIdType.MESH

HD = 128
ITEM_LEN = 64
HERE = 16
TAKEN = 6
ROWS = TAKEN * ITEM_LEN
WIDE = 512
DEPTH = 1024
EPSILON = 1e-05
THETA = 500000.0
BF = jnp.bfloat16
F32 = jnp.float32

PIECE = DEPTH // 4
HALF = ROWS // 2
QUARTER = ROWS // 4
DIRECT = (3,)


def tables():
    j = np.arange(HD // 2, dtype=np.float64)
    freq = (THETA ** (-2.0 * j / HD)).astype(np.float32)
    phase = (np.arange(ITEM_LEN, dtype=np.float32)[:, None] * freq).astype(np.float64)
    cos, sin = np.cos(phase), np.sin(phase)
    return (
        np.concatenate([cos, cos], axis=1).astype(np.float32),
        np.concatenate([-sin, sin], axis=1).astype(np.float32),
    )


def kernel(
    exited_in, destination_in, hidden, gain_in, wq, wkv, wo, cos_in, sin_in, result,
    exited, destination, gain, cos, sin, out,
    hid, outgoing, arrived, meta, meta_scalar, act, scaled, wbuf, obuf, acc, squares, qs, kvown, kvpart,
    ctx, part, r1, r2, s1, q1, q2,
    local_sem, out_sem, meta_s, meta_r, route_s, route_r, x_s, x_r, ag_s, ag_r, rs_s, rs_r, kv_s, kv_r,
):
    me = lax.axis_index("dp")
    t = lax.axis_index("tensor")
    x, c = me // 2, me % 2
    z, y = t // 4, t % 4
    left = ((x + 3) % 4) * 2 + c
    right = ((x + 1) % 4) * 2 + c
    far = ((x + 2) % 4) * 2 + c
    zp, zm, zf = (z + 1) % 4, (z + 3) % 4, (z + 2) % 4
    yp, ym, yf = (y + 1) % 4, (y + 3) % 4, (y + 2) % 4

    def sibling(i):
        return i + 1 - 2 * c

    sib = sibling(me)

    def put(src, dst, send, recv, device):
        copy = pltpu.make_async_remote_copy(
            src_ref=src, dst_ref=dst, send_sem=send, recv_sem=recv,
            device_id=device, device_id_type=MESH,
        )
        copy.start()

    def got(dst, recv):
        pltpu.make_async_remote_copy(
            src_ref=dst, dst_ref=dst, send_sem=recv, recv_sem=recv,
            device_id=(sib, t), device_id_type=MESH,
        ).wait_recv()

    def sent(src, send):
        pltpu.make_async_remote_copy(
            src_ref=src, dst_ref=src, send_sem=send, recv_sem=send,
            device_id=(sib, t), device_id_type=MESH,
        ).wait_send()

    def loaded(dst, sem):
        pltpu.make_async_copy(dst, dst, sem).wait()

    barrier = pltpu.get_barrier_semaphore()
    peers = [((me + k) % 8, t) for k in (4, 3, 5, 2, 6, 1, 7)]
    peers += [(me, zf * 4 + y), (me, z * 4 + yf)]
    peers += [(me, zp * 4 + y), (me, zm * 4 + y), (me, z * 4 + yp), (me, z * 4 + ym)]
    for peer in peers:
        pl.semaphore_signal(barrier, inc=1, device_id=peer, device_id_type=MESH)

    flags = [
        pltpu.make_async_copy(exited_in, exited, local_sem.at[7]),
        pltpu.make_async_copy(destination_in, destination, local_sem.at[8]),
    ]
    for flag in flags:
        flag.start()
    loads = [pltpu.make_async_copy(hidden, hid, local_sem.at[0])]
    loads.append(pltpu.make_async_copy(wq, wbuf.at[me, :, pl.ds(0, WIDE)], local_sem.at[1]))
    loads.append(pltpu.make_async_copy(wkv, wbuf.at[me, :, pl.ds(WIDE, HD)], local_sem.at[1]))
    for s in range(4):
        for h in range(2):
            loads.append(
                pltpu.make_async_copy(
                    wo.at[:, pl.ds(h * WIDE + s * HD, HD)],
                    obuf.at[s, me, :, pl.ds(h * HD, HD)],
                    local_sem.at[2],
                )
            )
    loads.append(pltpu.make_async_copy(gain_in, gain, local_sem.at[3]))
    loads.append(pltpu.make_async_copy(cos_in, cos, local_sem.at[4]))
    loads.append(pltpu.make_async_copy(sin_in, sin, local_sem.at[5]))
    for load in loads:
        load.start()

    def weights(r, i, low=0, count=None):
        if r < 4:
            return wbuf.at[i, pl.ds(r * PIECE + low, count or PIECE), :]
        return obuf.at[r - 4, i, pl.ds(low, count or WIDE), :]

    def half_of(r):
        return PIECE // 2 if r < 4 else WIDE // 2

    def x_put(r, k, view, device):
        put(view, view, x_s.at[r], x_r.at[r, k], (device, t))

    def shares(r, count):
        if r < 4:
            return wbuf.at[pl.ds(0, count), pl.ds(r * PIECE, PIECE), :]
        return obuf.at[r - 4, pl.ds(0, count)]

    def x_own_sibling(r):
        x_put(r, 3, weights(r, me), sib)

    def x_own(r, which):
        n = half_of(r)
        x_put(r, which, weights(r, me, which * n, n), right)
        x_put(r, which, weights(r, me, n - which * n, n), left)

    def x_hand_on(r):
        n = half_of(r)
        got(shares(r, 1), x_r.at[r, 0])
        x_put(r, 2, weights(r, left, 0, n), right)
        x_put(r, 2, weights(r, right, n, n), left)

    def x_near(r, *after):
        got(shares(r, 1), x_r.at[r, 1])
        for piece in after:
            x_own(*piece)
        x_put(r, 3, weights(r, left), sib)
        x_put(r, 3, weights(r, right), sib)

    def x_far(r, *after):
        got(shares(r, 1), x_r.at[r, 2])
        for piece in after:
            x_own(*piece)
        x_put(r, 4, weights(r, far), sib)

    def x_sibling_near(r):
        got(shares(r, 3), x_r.at[r, 3])

    def x_sibling_far(r):
        got(shares(r, 1), x_r.at[r, 4])

    def x_sibling(r):
        x_sibling_near(r)
        x_sibling_far(r)

    for flag in flags:
        flag.wait()
    codes = [jnp.where(exited[k] == 0, destination[k], -1) for k in range(HERE)]
    lane = lax.broadcasted_iota(jnp.int32, (8, 128), 1)
    row = jnp.full((8, 128), -1, jnp.int32)
    for k in range(HERE):
        row = jnp.where(lane == k, codes[k], row)
    meta[me] = row
    loads[0].wait()
    for k in range(8):
        dest = (me + k) % 8 if k else me
        seen = jnp.int32(0)
        first = jnp.int32(0)
        second = jnp.int32(0)
        for item in range(HERE):
            hit = codes[item] == dest
            first = jnp.where(hit & (seen == 0), item, first)
            second = jnp.where(hit & (seen == 1), item, second)
            seen = seen + jnp.where(hit, 1, 0)
        if k:
            outgoing[dest, 0] = hid[first]
            outgoing[dest, 1] = hid[second]
        else:
            arrived[me, 0] = hid[first]
            arrived[me, 1] = hid[second]
    loaded(wbuf.at[me], local_sem.at[1])
    pl.semaphore_wait(barrier, len(peers))

    for k in range(1, 8):
        put(meta.at[me], meta.at[me], meta_s, meta_r, ((me + k) % 8, t))
    for k in (4, 2, 6, 3, 5, 1, 7):
        put(outgoing.at[(me + k) % 8], arrived.at[me], route_s, route_r, ((me + k) % 8, t))
    x_own(0, 0)
    x_own(0, 1)
    for r in range(4):
        x_own_sibling(r)
    loaded(obuf.at[pl.ds(0, 4), me], local_sem.at[2])
    for r in range(4, 8):
        x_own_sibling(r)

    got(meta.at[pl.ds(0, 7)], meta_r)
    to_scalar = pltpu.make_async_copy(meta, meta_scalar, local_sem.at[6])
    to_scalar.start()
    to_scalar.wait()
    picks = [jnp.int32(0)] * TAKEN
    rank = jnp.int32(0)
    for j in range(8):
        count = jnp.int32(0)
        for item in range(HERE):
            count = count + jnp.where(meta_scalar[j, 0, item] == me, 1, 0)
        for s in range(2):
            valid = count > s
            for r in range(TAKEN):
                picks[r] = jnp.where(valid & (rank == r), 2 * j + s, picks[r])
            rank = rank + jnp.where(valid, 1, 0)

    got(arrived.at[pl.ds(0, 7)], route_r)
    flat = arrived.reshape(16, ITEM_LEN, WIDE)
    for r in range(TAKEN):
        act[t, pl.ds(r * ITEM_LEN, ITEM_LEN), :] = flat[picks[r]]

    def line(half, phase):
        along_z = (half == 0) == (phase == 0)
        if along_z:
            return (z, zm, zp, zf), lambda a, b: a * 4 + b
        return (y, ym, yp, yf), lambda a, b: b * 4 + a

    def chunk(tt, half, low=0, count=HALF):
        return act.at[tt, pl.ds(half * HALF + low, count), :]

    def ag_put(half, k, view, device):
        put(view, view, ag_s.at[half], ag_r.at[half, k], (me, device))

    def other(half):
        return y if half == 0 else z

    def ag_send(half, phase, slot, tt, near):
        (own, minus, plus, opposite), at = line(half, phase)
        place = other(half) if phase == 0 else near
        ag_put(half, slot, chunk(tt, half), at(plus, place))
        ag_put(half, slot, chunk(tt, half), at(minus, place))

    def ag_near(half, phase, slot, far_slot, place):
        (own, minus, plus, opposite), at = line(half, phase)
        got(act.at[pl.ds(0, 2), pl.ds(half * HALF, HALF), :], ag_r.at[half, slot])
        q = HALF // 2
        here = other(half) if phase == 0 else (z if half == 0 else y)
        ag_put(half, far_slot, chunk(at(minus, place), half, 0, q), at(plus, here))
        ag_put(half, far_slot, chunk(at(plus, place), half, q, q), at(minus, here))

    def places(half):
        return (z, zm, zp, zf) if half == 0 else (y, ym, yp, yf)

    def first_at(half, a):
        return a * 4 + y if half == 0 else z * 4 + a

    def ag2_send(half, n):
        a = places(half)[n]
        ag_send(half, 1, 2 + n, first_at(half, a), places(half)[0])

    def ag2_near(half, n):
        ag_near(half, 1, 2 + n, 6, places(half)[n])

    def rotated(value):
        return value * cos[...] + pltpu.roll(value, HD // 2, 1) * sin[...]

    parity = t % 2

    near_chips, far_chips = [x, (x + 3) % 4, (x + 1) % 4], [(x + 2) % 4]
    near_shards = [2 * chip + b for chip in near_chips for b in range(2)]
    far_shards = [2 * chip + b for chip in far_chips for b in range(2)]

    def project(p, low, count, shards):
        term = None
        for i in shards:
            product = jnp.dot(
                scaled[2 * i + p // 2, :, pl.ds((p % 2) * PIECE, PIECE)],
                wbuf[i, pl.ds(p * PIECE, PIECE), pl.ds(low, count)],
                preferred_element_type=F32,
            )
            term = product if term is None else term + product
        acc[:, pl.ds(low, count)] += term

    def multiply(s, chips):
        for chip in chips:
            for b in range(2):
                term = jnp.dot(
                    ctx[...], obuf[s, 2 * chip + b], preferred_element_type=F32
                ).astype(BF)
                part[s, chip, 2 * b] = term[:, :HD]
                part[s, chip, 2 * b + 1] = term[:, HD:]

    def rs_put(s, half, k, src, dst, device):
        put(src, dst, rs_s.at[s, half], rs_r.at[s, half, k], (me, device))

    A = (0, QUARTER)
    B = (QUARTER, QUARTER)

    def block(s, half, a, rows):
        low, count = rows
        span = pl.ds(half * HALF + low, count)
        if half == 0:
            return part.at[s, a, :, span, :]
        return part.at[s, :, a, span, :]

    def devices(half, phase):
        if (half == 0) == (phase == 0):
            return zp * 4 + y, zm * 4 + y
        return z * 4 + yp, z * 4 + ym

    def ends(half, phase):
        if (half == 0) == (phase == 0):
            return z, zm, zp, zf
        return y, ym, yp, yf

    def span(rows):
        return pl.ds(rows[0], rows[1])

    def send_first(s):
        for half in range(2):
            own, minus, plus, opposite = ends(half, 0)
            up, down = devices(half, 0)
            rs_put(s, half, 0, block(s, half, opposite, A), r1.at[s, half, 0], up)
            rs_put(s, half, 0, block(s, half, opposite, B), r1.at[s, half, 1], down)
            rs_put(s, half, 1, block(s, half, plus, B), r2.at[s, half, 0, :, span(B), :], up)
            rs_put(s, half, 1, block(s, half, minus, A), r2.at[s, half, 1, :, span(A), :], down)

    def add_first(s, half):
        own, minus, plus, opposite = ends(half, 0)
        up, down = devices(half, 0)
        got(r1.at[s, half], rs_r.at[s, half, 0])
        for side, (a, rows, device) in enumerate(((plus, A, up), (minus, B, down))):
            view = block(s, half, a, rows)
            view[...] = (view[...].astype(F32) + r1[s, half, side].astype(F32)).astype(BF)
            rs_put(s, half, 1, view, r2.at[s, half, side, :, span(rows), :], device)

    def send_second(s, half):
        own, minus, plus, opposite = ends(half, 0)
        got(r2.at[s, half], rs_r.at[s, half, 1])
        view = block(s, half, own, (0, HALF))
        s1[s, half] = (
            view[...].astype(F32) + r2[s, half, 0].astype(F32) + r2[s, half, 1].astype(F32)
        ).astype(BF)
        own, minus, plus, opposite = ends(half, 1)
        up, down = devices(half, 1)
        to = lambda a, rows: s1.at[s, half, a, span(rows), :]
        if s in DIRECT:
            across = zf * 4 + y if half else z * 4 + yf
            rs_put(s, half, 2, to(opposite, A), q1.at[s, half, 0], across)
            rs_put(s, half, 2, to(opposite, B), q1.at[s, half, 1], across)
            rs_put(s, half, 3, to(plus, (0, HALF)), q2.at[s, half, 0], up)
            rs_put(s, half, 3, to(minus, (0, HALF)), q2.at[s, half, 1], down)
            return
        rs_put(s, half, 2, to(opposite, A), q1.at[s, half, 0], up)
        rs_put(s, half, 2, to(opposite, B), q1.at[s, half, 1], down)
        rs_put(s, half, 3, to(plus, B), q2.at[s, half, 0, span(B), :], up)
        rs_put(s, half, 3, to(minus, A), q2.at[s, half, 1, span(A), :], down)

    def add_second(s, half):
        own, minus, plus, opposite = ends(half, 1)
        up, down = devices(half, 1)
        got(q1.at[s, half], rs_r.at[s, half, 2])
        for side, (a, rows, device) in enumerate(((plus, A, up), (minus, B, down))):
            view = s1.at[s, half, a, span(rows), :]
            view[...] = (view[...].astype(F32) + q1[s, half, side].astype(F32)).astype(BF)
            rs_put(s, half, 3, view, q2.at[s, half, side, span(rows), :], device)

    def finish(s, half):
        own, minus, plus, opposite = ends(half, 1)
        got(q2.at[s, half], rs_r.at[s, half, 3])
        rows, cols = pl.ds(half * HALF, HALF), pl.ds(s * HD, HD)
        total = (
            act[t, rows, cols].astype(F32)
            + s1[s, half, own].astype(F32)
            + q2[s, half, 0].astype(F32)
            + q2[s, half, 1].astype(F32)
        )
        if s in DIRECT:
            got(q1.at[s, half], rs_r.at[s, half, 2])
            total = total + q1[s, half].reshape(HALF, HD).astype(F32)
        out[rows, cols] = total.astype(BF)
        pltpu.make_async_copy(out.at[rows, cols], result.at[rows, cols], out_sem).start()

    ag_send(0, 0, 0, t, None)
    ag_send(1, 0, 0, t, None)
    ag2_send(0, 0)
    ag2_send(1, 0)
    x_hand_on(0)
    x_near(0, (1, 0))
    ag_near(0, 0, 0, 1, other(0))
    ag2_send(0, 1)
    ag2_send(0, 2)
    ag_near(1, 0, 0, 1, other(1))
    ag2_send(1, 1)
    ag2_send(1, 2)
    x_far(0, (1, 1))
    ag2_near(1, 0)
    ag2_near(0, 0)
    x_sibling(0)
    got(act.at[0, pl.ds(0 * HALF, HALF), :], ag_r.at[0, 1])
    ag2_send(0, 3)
    x_hand_on(1)
    ag2_near(0, 1)
    x_near(1, (2, 0))
    ag2_near(1, 1)
    ag2_near(0, 2)
    x_far(1, (2, 1))
    ag2_near(1, 2)
    got(act.at[0, pl.ds(1 * HALF, HALF), :], ag_r.at[1, 1])
    ag2_send(1, 3)
    x_sibling(1)
    x_hand_on(2)
    x_near(2, (3, 0))
    ag2_near(0, 3)
    x_far(2, (3, 1))
    ag2_near(1, 3)
    x_sibling(2)
    got(act.at[pl.ds(0, 4), pl.ds(0 * HALF, HALF), :], ag_r.at[0, 6])
    x_hand_on(3)
    got(act.at[pl.ds(0, 4), pl.ds(1 * HALF, HALF), :], ag_r.at[1, 6])
    loaded(gain, local_sem.at[3])
    acc[...] = jnp.zeros_like(acc)
    squares[...] = jnp.zeros_like(squares)

    @pl.loop(0, 16)
    def _(tt):
        rows = act[tt].astype(F32)
        power = rows * rows
        squares[...] += (power[:, :HD] + power[:, HD:2 * HD]) + (
            power[:, 2 * HD:3 * HD] + power[:, 3 * HD:]
        )
        scaled[tt] = (rows * gain[tt]).astype(BF)

    squares[:, :1] = lax.rsqrt(
        jnp.sum(squares[...], axis=1, keepdims=True) * (1.0 / (16 * WIDE)) + EPSILON
    )
    x_near(3, (4, 0))
    project(0, 0, WIDE + HD, range(8))
    project(1, 0, WIDE + HD, range(8))
    x_far(3, (4, 1))
    project(2, 0, WIDE + HD, range(8))
    x_sibling_near(3)
    project(3, 0, WIDE + HD, near_shards)
    x_hand_on(4)
    x_sibling_far(3)
    project(3, WIDE, HD, far_shards)
    loaded(cos, local_sem.at[4])
    loaded(sin, local_sem.at[5])

    @pl.loop(0, TAKEN, unroll=True)
    def _(n):
        rows = pl.ds(n * ITEM_LEN, ITEM_LEN)
        value = acc[rows, pl.ds(WIDE, HD)] * squares[rows, :1]
        kvown[rows, :] = jnp.where(parity == 0, rotated(value), value).astype(BF)

    put(kvown.at[pl.ds(0 * HALF, HALF), :], kvpart.at[pl.ds(0 * HALF, HALF), :], kv_s, kv_r.at[0], (me, t + 1 - 2 * parity))
    put(kvown.at[pl.ds(1 * HALF, HALF), :], kvpart.at[pl.ds(1 * HALF, HALF), :], kv_s, kv_r.at[1], (me, t + 1 - 2 * parity))
    project(3, 0, WIDE, far_shards)

    @pl.loop(0, TAKEN, unroll=True)
    def _(n):
        rows = pl.ds(n * ITEM_LEN, ITEM_LEN)
        inverse = squares[rows, :1]
        for h in range(4):
            value = acc[rows, pl.ds(h * HD, HD)] * inverse
            qs[n, pl.ds(h * ITEM_LEN, ITEM_LEN), :] = rotated(value).astype(BF)

    x_near(4, (5, 0))
    got(kvpart.at[pl.ds(0 * HALF, HALF), :], kv_r.at[0])

    @pl.loop(0, 3, unroll=True)
    def _(n):
        rows = pl.ds(n * ITEM_LEN, ITEM_LEN)
        mine, theirs = kvown[rows, :], kvpart[rows, :]
        keys = jnp.where(parity == 0, mine, theirs)
        values = jnp.where(parity == 0, theirs, mine)
        scores = lax.dot_general(
            qs[n], keys, (((1,), (1,)), ((), ())), preferred_element_type=F32
        ) * (HD ** -0.5)
        place = lax.broadcasted_iota(jnp.int32, scores.shape, 0) % ITEM_LEN
        scores = jnp.where(
            place >= lax.broadcasted_iota(jnp.int32, scores.shape, 1), scores, -1e30
        )
        raised = jnp.exp(scores - jnp.max(scores, axis=1, keepdims=True))
        probs = (raised * (1.0 / jnp.sum(raised, axis=1, keepdims=True))).astype(BF)
        context = jnp.dot(probs, values, preferred_element_type=F32).astype(BF)
        for h in range(4):
            ctx[rows, pl.ds(h * HD, HD)] = context[h * ITEM_LEN:(h + 1) * ITEM_LEN, :]

    got(kvpart.at[pl.ds(1 * HALF, HALF), :], kv_r.at[1])

    @pl.loop(3, 6, unroll=True)
    def _(n):
        rows = pl.ds(n * ITEM_LEN, ITEM_LEN)
        mine, theirs = kvown[rows, :], kvpart[rows, :]
        keys = jnp.where(parity == 0, mine, theirs)
        values = jnp.where(parity == 0, theirs, mine)
        scores = lax.dot_general(
            qs[n], keys, (((1,), (1,)), ((), ())), preferred_element_type=F32
        ) * (HD ** -0.5)
        place = lax.broadcasted_iota(jnp.int32, scores.shape, 0) % ITEM_LEN
        scores = jnp.where(
            place >= lax.broadcasted_iota(jnp.int32, scores.shape, 1), scores, -1e30
        )
        raised = jnp.exp(scores - jnp.max(scores, axis=1, keepdims=True))
        probs = (raised * (1.0 / jnp.sum(raised, axis=1, keepdims=True))).astype(BF)
        context = jnp.dot(probs, values, preferred_element_type=F32).astype(BF)
        for h in range(4):
            ctx[rows, pl.ds(h * HD, HD)] = context[h * ITEM_LEN:(h + 1) * ITEM_LEN, :]

    x_far(4, (5, 1))
    x_sibling_near(4)
    multiply(0, near_chips)
    x_sibling_far(4)
    multiply(0, far_chips)
    send_first(0)
    x_hand_on(5)
    x_near(5, (6, 0))
    add_first(0, 0)
    add_first(0, 1)
    x_far(5, (6, 1))
    x_sibling_near(5)
    multiply(1, near_chips)
    x_sibling_far(5)
    multiply(1, far_chips)
    send_first(1)
    x_hand_on(6)
    send_second(0, 0)
    send_second(0, 1)
    x_near(6, (7, 0))
    add_first(1, 0)
    add_first(1, 1)
    x_far(6, (7, 1))
    x_sibling_near(6)
    multiply(2, near_chips)
    add_second(0, 1)
    add_second(0, 0)
    x_sibling_far(6)
    multiply(2, far_chips)
    send_first(2)
    x_hand_on(7)
    send_second(1, 0)
    send_second(1, 1)
    finish(0, 0)
    finish(0, 1)
    x_near(7)
    add_first(2, 0)
    add_first(2, 1)
    x_far(7)
    x_sibling_near(7)
    multiply(3, near_chips)
    add_second(1, 1)
    add_second(1, 0)
    x_sibling_far(7)
    multiply(3, far_chips)
    send_first(3)
    finish(1, 0)
    finish(1, 1)
    add_first(3, 0)
    add_first(3, 1)
    send_second(2, 0)
    send_second(2, 1)
    send_second(3, 0)
    send_second(3, 1)
    add_second(2, 1)
    add_second(2, 0)
    finish(2, 0)
    finish(2, 1)
    finish(3, 0)
    finish(3, 1)

    sent(meta.at[pl.ds(0, 7)], meta_s)
    sent(outgoing.at[pl.ds(0, 7)], route_s)
    for r in range(8):
        sent(shares(r, 7), x_s.at[r])
    for half in range(2):
        sent(act.at[pl.ds(0, 15), pl.ds(half * HALF, HALF), :], ag_s.at[half])
    sent(kvown, kv_s)
    terms = part.reshape(64, ROWS, HD)
    for s in range(4):
        for half in range(2):
            sent(terms.at[pl.ds(16 * s, 15), pl.ds(0, HALF), :], rs_s.at[s, half])
    loaded(out, out_sem)


def shards(hidden, exited, destination, norm_gain, query_weight, keyvalue_weight, output_weight):
    cos, sin = tables()
    hbm = pl.BlockSpec(memory_space=pl.ANY)
    dma = pltpu.SemaphoreType.DMA
    return pl.pallas_call(
        kernel,
        out_shape=jax.ShapeDtypeStruct((ROWS, WIDE), BF),
        in_specs=[hbm, hbm, hbm, hbm, hbm, hbm, hbm, hbm, hbm],
        out_specs=hbm,
        scratch_shapes=[
            pltpu.SMEM((HERE,), jnp.int32),
            pltpu.SMEM((HERE,), jnp.int32),
            pltpu.VMEM((16, 1, WIDE), F32),
            pltpu.VMEM((ITEM_LEN, HD), F32),
            pltpu.VMEM((ITEM_LEN, HD), F32),
            pltpu.VMEM((ROWS, WIDE), BF),
            pltpu.VMEM((HERE, ITEM_LEN, WIDE), BF),
            pltpu.VMEM((8, 2, ITEM_LEN, WIDE), BF),
            pltpu.VMEM((8, 2, ITEM_LEN, WIDE), BF),
            pltpu.VMEM((8, 8, 128), jnp.int32),
            pltpu.SMEM((8, 8, 128), jnp.int32),
            pltpu.VMEM((16, ROWS, WIDE), BF),
            pltpu.VMEM((16, ROWS, WIDE), BF),
            pltpu.VMEM((8, DEPTH, WIDE + HD), BF),
            pltpu.VMEM((4, 8, WIDE, 2 * HD), BF),
            pltpu.VMEM((ROWS, WIDE + HD), F32),
            pltpu.VMEM((ROWS, HD), F32),
            pltpu.VMEM((TAKEN, 4 * ITEM_LEN, HD), BF),
            pltpu.VMEM((ROWS, HD), BF),
            pltpu.VMEM((ROWS, HD), BF),
            pltpu.VMEM((ROWS, WIDE), BF),
            pltpu.VMEM((4, 4, 4, ROWS, HD), BF),
            pltpu.VMEM((4, 2, 2, 4, QUARTER, HD), BF),
            pltpu.VMEM((4, 2, 2, 4, HALF, HD), BF),
            pltpu.VMEM((4, 2, 4, HALF, HD), BF),
            pltpu.VMEM((4, 2, 2, QUARTER, HD), BF),
            pltpu.VMEM((4, 2, 2, HALF, HD), BF),
            dma((9,)),
            dma(()),
            dma(()),
            dma(()),
            dma(()),
            dma(()),
            dma((8,)),
            dma((8, 5)),
            dma((2,)),
            dma((2, 7)),
            dma((4, 2)),
            dma((4, 2, 4)),
            dma(()),
            dma((2,)),
        ],
        compiler_params=pltpu.CompilerParams(
            collective_id=0, has_side_effects=True, vmem_limit_bytes=60 * 1024 * 1024
        ),
        cost_estimate=pl.CostEstimate(
            flops=2 * ROWS * 16 * WIDE * (2 * WIDE + HD),
            bytes_accessed=8 * 1024 * 1024,
            transcendentals=ROWS * 4 * ITEM_LEN,
        ),
    )(
        exited,
        destination,
        hidden.reshape(HERE, ITEM_LEN, WIDE),
        norm_gain.reshape(16, 1, WIDE),
        query_weight,
        keyvalue_weight,
        output_weight,
        jnp.asarray(cos),
        jnp.asarray(sin),
    )


def solution(mesh):
    placed = (
        P("dp", "tensor"),
        P("dp"),
        P("dp"),
        P(),
        P("dp", "tensor"),
        P("dp", "tensor"),
        P("tensor", "dp"),
    )
    return jax.shard_map(
        shards, mesh=mesh, in_specs=placed, out_specs=P("dp", "tensor"), check_vma=False
    )
```

```python
import functools

import jax
import jax.numpy as jnp
import numpy as np
from jax import lax
from jax.experimental import pallas as pl
from jax.experimental.pallas import tpu as pltpu
from jax.sharding import PartitionSpec as P

MESH = pl.DeviceIdType.MESH

HD = 128
ITEM_LEN = 64
HERE = 16
TAKEN = 6
ROWS = TAKEN * ITEM_LEN
WIDE = 512
DEPTH = 1024
EPSILON = 1e-05
THETA = 500000.0
BF = jnp.bfloat16
F32 = jnp.float32

PIECE = DEPTH // 4
HALF = ROWS // 2
QUARTER = ROWS // 4
DIRECT = (3,)


def tables():
    j = np.arange(HD // 2, dtype=np.float64)
    freq = (THETA ** (-2.0 * j / HD)).astype(np.float32)
    phase = (np.arange(ITEM_LEN, dtype=np.float32)[:, None] * freq).astype(np.float64)
    cos, sin = np.cos(phase), np.sin(phase)
    return (
        np.concatenate([cos, cos], axis=1).astype(np.float32),
        np.concatenate([-sin, sin], axis=1).astype(np.float32),
    )


def kernel(
    exited_in, destination_in, hidden, gain_in, wq, wkv, wo, cos_in, sin_in, result,
    exited, destination, gain, cos, sin, out,
    hid, outgoing, arrived, meta, meta_scalar, act, scaled, wbuf, obuf, acc, squares, qs, kvown, kvpart,
    ctx, part, r1, r2, s1, q1, q2,
    local_sem, out_sem, meta_s, meta_r, route_s, route_r, x_s, x_r, ag_s, ag_r, rs_s, rs_r, kv_s, kv_r,
):
    me = lax.axis_index("dp")
    t = lax.axis_index("tensor")
    x, c = me // 2, me % 2
    z, y = t // 4, t % 4
    left = ((x + 3) % 4) * 2 + c
    right = ((x + 1) % 4) * 2 + c
    far = ((x + 2) % 4) * 2 + c
    zp, zm, zf = (z + 1) % 4, (z + 3) % 4, (z + 2) % 4
    yp, ym, yf = (y + 1) % 4, (y + 3) % 4, (y + 2) % 4

    def sibling(i):
        return i + 1 - 2 * c

    sib = sibling(me)

    def put(src, dst, send, recv, device):
        copy = pltpu.make_async_remote_copy(
            src_ref=src, dst_ref=dst, send_sem=send, recv_sem=recv,
            device_id=device, device_id_type=MESH,
        )
        copy.start()

    def got(dst, recv):
        pltpu.make_async_remote_copy(
            src_ref=dst, dst_ref=dst, send_sem=recv, recv_sem=recv,
            device_id=(sib, t), device_id_type=MESH,
        ).wait_recv()

    def sent(src, send):
        pltpu.make_async_remote_copy(
            src_ref=src, dst_ref=src, send_sem=send, recv_sem=send,
            device_id=(sib, t), device_id_type=MESH,
        ).wait_send()

    def loaded(dst, sem):
        pltpu.make_async_copy(dst, dst, sem).wait()

    barrier = pltpu.get_barrier_semaphore()
    peers = [((me + k) % 8, t) for k in (4, 3, 5, 2, 6, 1, 7)]
    peers += [(me, zf * 4 + y), (me, z * 4 + yf)]
    peers += [(me, zp * 4 + y), (me, zm * 4 + y), (me, z * 4 + yp), (me, z * 4 + ym)]
    for peer in peers:
        pl.semaphore_signal(barrier, inc=1, device_id=peer, device_id_type=MESH)

    flags = [
        pltpu.make_async_copy(exited_in, exited, local_sem.at[7]),
        pltpu.make_async_copy(destination_in, destination, local_sem.at[8]),
    ]
    for flag in flags:
        flag.start()
    loads = [pltpu.make_async_copy(hidden, hid, local_sem.at[0])]
    loads.append(pltpu.make_async_copy(wq, wbuf.at[me, :, pl.ds(0, WIDE)], local_sem.at[1]))
    loads.append(pltpu.make_async_copy(wkv, wbuf.at[me, :, pl.ds(WIDE, HD)], local_sem.at[1]))
    for s in range(4):
        for h in range(2):
            loads.append(
                pltpu.make_async_copy(
                    wo.at[:, pl.ds(h * WIDE + s * HD, HD)],
                    obuf.at[s, me, :, pl.ds(h * HD, HD)],
                    local_sem.at[2],
                )
            )
    loads.append(pltpu.make_async_copy(gain_in, gain, local_sem.at[3]))
    loads.append(pltpu.make_async_copy(cos_in, cos, local_sem.at[4]))
    loads.append(pltpu.make_async_copy(sin_in, sin, local_sem.at[5]))
    for load in loads:
        load.start()

    def weights(r, i, low=0, count=None):
        if r < 4:
            return wbuf.at[i, pl.ds(r * PIECE + low, count or PIECE), :]
        return obuf.at[r - 4, i, pl.ds(low, count or WIDE), :]

    def half_of(r):
        return PIECE // 2 if r < 4 else WIDE // 2

    def x_put(r, k, view, device):
        put(view, view, x_s.at[r // 4], x_r.at[r, k], (device, t))

    def shares(r, count):
        if r < 4:
            return wbuf.at[pl.ds(0, count), pl.ds(r * PIECE, PIECE), :]
        return obuf.at[r - 4, pl.ds(0, count)]

    def x_own_sibling(r):
        x_put(r, 3, weights(r, me), sib)

    def x_own(r, which):
        n = half_of(r)
        x_put(r, which, weights(r, me, which * n, n), right)
        x_put(r, which, weights(r, me, n - which * n, n), left)

    def x_hand_on(r):
        n = half_of(r)
        got(shares(r, 1), x_r.at[r, 0])
        x_put(r, 2, weights(r, left, 0, n), right)
        x_put(r, 2, weights(r, right, n, n), left)

    def x_near(r, *after):
        got(shares(r, 1), x_r.at[r, 1])
        for piece in after:
            x_own(*piece)
        x_put(r, 3, weights(r, left), sib)
        x_put(r, 3, weights(r, right), sib)

    def x_far(r, *after):
        got(shares(r, 1), x_r.at[r, 2])
        for piece in after:
            x_own(*piece)
        x_put(r, 4, weights(r, far), sib)

    def x_sibling_near(r):
        got(shares(r, 3), x_r.at[r, 3])

    def x_sibling_far(r):
        got(shares(r, 1), x_r.at[r, 4])

    def x_sibling(r):
        x_sibling_near(r)
        x_sibling_far(r)

    for flag in flags:
        flag.wait()
    codes = [jnp.where(exited[k] == 0, destination[k], -1) for k in range(HERE)]
    lane = lax.broadcasted_iota(jnp.int32, (8, 128), 1)
    row = jnp.full((8, 128), -1, jnp.int32)
    for k in range(HERE):
        row = jnp.where(lane == k, codes[k], row)
    meta[me] = row
    loads[0].wait()
    for k in range(8):
        dest = (me + k) % 8 if k else me
        seen = jnp.int32(0)
        first = jnp.int32(0)
        second = jnp.int32(0)
        for item in range(HERE):
            hit = codes[item] == dest
            first = jnp.where(hit & (seen == 0), item, first)
            second = jnp.where(hit & (seen == 1), item, second)
            seen = seen + jnp.where(hit, 1, 0)
        if k:
            outgoing[dest, 0] = hid[first]
            outgoing[dest, 1] = hid[second]
        else:
            arrived[me, 0] = hid[first]
            arrived[me, 1] = hid[second]
    loaded(wbuf.at[me], local_sem.at[1])
    pl.semaphore_wait(barrier, len(peers))

    for k in range(1, 8):
        put(meta.at[me], meta.at[me], meta_s, meta_r, ((me + k) % 8, t))
    for k in (4, 2, 6, 3, 5, 1, 7):
        put(outgoing.at[(me + k) % 8], arrived.at[me], route_s, route_r, ((me + k) % 8, t))
    x_own(0, 0)
    x_own(0, 1)
    for r in range(4):
        x_own_sibling(r)
    loaded(obuf.at[pl.ds(0, 4), me], local_sem.at[2])
    for r in range(4, 8):
        x_own_sibling(r)

    got(meta.at[pl.ds(0, 7)], meta_r)
    to_scalar = pltpu.make_async_copy(meta, meta_scalar, local_sem.at[6])
    to_scalar.start()
    to_scalar.wait()
    picks = [jnp.int32(0)] * TAKEN
    rank = jnp.int32(0)
    for j in range(8):
        count = jnp.int32(0)
        for item in range(HERE):
            count = count + jnp.where(meta_scalar[j, 0, item] == me, 1, 0)
        for s in range(2):
            valid = count > s
            for r in range(TAKEN):
                picks[r] = jnp.where(valid & (rank == r), 2 * j + s, picks[r])
            rank = rank + jnp.where(valid, 1, 0)

    got(arrived.at[pl.ds(0, 7)], route_r)
    flat = arrived.reshape(16, ITEM_LEN, WIDE)
    for r in range(TAKEN):
        act[t, pl.ds(r * ITEM_LEN, ITEM_LEN), :] = flat[picks[r]]

    def line(half, phase):
        along_z = (half == 0) == (phase == 0)
        if along_z:
            return (z, zm, zp, zf), lambda a, b: a * 4 + b
        return (y, ym, yp, yf), lambda a, b: b * 4 + a

    def chunk(tt, half, low=0, count=HALF):
        return act.at[tt, pl.ds(half * HALF + low, count), :]

    def ag_put(half, k, view, device):
        put(view, view, ag_s, ag_r.at[half, k], (me, device))

    def other(half):
        return y if half == 0 else z

    def ag_send(half, phase, slot, tt, near):
        (own, minus, plus, opposite), at = line(half, phase)
        place = other(half) if phase == 0 else near
        ag_put(half, slot, chunk(tt, half), at(plus, place))
        ag_put(half, slot, chunk(tt, half), at(minus, place))

    def ag_near(half, phase, slot, far_slot, place):
        (own, minus, plus, opposite), at = line(half, phase)
        got(act.at[pl.ds(0, 2), pl.ds(half * HALF, HALF), :], ag_r.at[half, slot])
        q = HALF // 2
        here = other(half) if phase == 0 else (z if half == 0 else y)
        ag_put(half, far_slot, chunk(at(minus, place), half, 0, q), at(plus, here))
        ag_put(half, far_slot, chunk(at(plus, place), half, q, q), at(minus, here))

    def places(half):
        return (z, zm, zp, zf) if half == 0 else (y, ym, yp, yf)

    def first_at(half, a):
        return a * 4 + y if half == 0 else z * 4 + a

    def ag2_send(half, n):
        a = places(half)[n]
        ag_send(half, 1, 2 + n, first_at(half, a), places(half)[0])

    def ag2_near(half, n):
        ag_near(half, 1, 2 + n, 6, places(half)[n])

    def rotated(value):
        return value * cos[...] + pltpu.roll(value, HD // 2, 1) * sin[...]

    parity = t % 2

    near_chips, far_chips = [x, (x + 3) % 4, (x + 1) % 4], [(x + 2) % 4]
    near_shards = [2 * chip + b for chip in near_chips for b in range(2)]
    far_shards = [2 * chip + b for chip in far_chips for b in range(2)]

    def project(p, low, count, shards):
        term = None
        for i in shards:
            product = jnp.dot(
                scaled[2 * i + p // 2, :, pl.ds((p % 2) * PIECE, PIECE)],
                wbuf[i, pl.ds(p * PIECE, PIECE), pl.ds(low, count)],
                preferred_element_type=F32,
            )
            term = product if term is None else term + product
        acc[:, pl.ds(low, count)] += term

    def multiply(s, chips):
        for chip in chips:
            for b in range(2):
                term = jnp.dot(
                    ctx[...], obuf[s, 2 * chip + b], preferred_element_type=F32
                ).astype(BF)
                part[s, chip, 2 * b] = term[:, :HD]
                part[s, chip, 2 * b + 1] = term[:, HD:]

    def rs_put(s, half, k, src, dst, device):
        put(src, dst, rs_s, rs_r.at[s, half, k], (me, device))

    A = (0, QUARTER)
    B = (QUARTER, QUARTER)

    def block(s, half, a, rows):
        low, count = rows
        span = pl.ds(half * HALF + low, count)
        if half == 0:
            return part.at[s, a, :, span, :]
        return part.at[s, :, a, span, :]

    def devices(half, phase):
        if (half == 0) == (phase == 0):
            return zp * 4 + y, zm * 4 + y
        return z * 4 + yp, z * 4 + ym

    def ends(half, phase):
        if (half == 0) == (phase == 0):
            return z, zm, zp, zf
        return y, ym, yp, yf

    def span(rows):
        return pl.ds(rows[0], rows[1])

    def send_first(s):
        for half in range(2):
            own, minus, plus, opposite = ends(half, 0)
            up, down = devices(half, 0)
            rs_put(s, half, 0, block(s, half, opposite, A), r1.at[s, half, 0], up)
            rs_put(s, half, 0, block(s, half, opposite, B), r1.at[s, half, 1], down)
            rs_put(s, half, 1, block(s, half, plus, B), r2.at[s, half, 0, :, span(B), :], up)
            rs_put(s, half, 1, block(s, half, minus, A), r2.at[s, half, 1, :, span(A), :], down)

    def add_first(s, half):
        own, minus, plus, opposite = ends(half, 0)
        up, down = devices(half, 0)
        got(r1.at[s, half], rs_r.at[s, half, 0])
        for side, (a, rows, device) in enumerate(((plus, A, up), (minus, B, down))):
            view = block(s, half, a, rows)
            view[...] = (view[...].astype(F32) + r1[s, half, side].astype(F32)).astype(BF)
            rs_put(s, half, 1, view, r2.at[s, half, side, :, span(rows), :], device)

    def send_second(s, half):
        own, minus, plus, opposite = ends(half, 0)
        got(r2.at[s, half], rs_r.at[s, half, 1])
        view = block(s, half, own, (0, HALF))
        s1[s, half] = (
            view[...].astype(F32) + r2[s, half, 0].astype(F32) + r2[s, half, 1].astype(F32)
        ).astype(BF)
        own, minus, plus, opposite = ends(half, 1)
        up, down = devices(half, 1)
        to = lambda a, rows: s1.at[s, half, a, span(rows), :]
        if s in DIRECT:
            across = zf * 4 + y if half else z * 4 + yf
            rs_put(s, half, 2, to(opposite, A), q1.at[s, half, 0], across)
            rs_put(s, half, 2, to(opposite, B), q1.at[s, half, 1], across)
            rs_put(s, half, 3, to(plus, (0, HALF)), q2.at[s, half, 0], up)
            rs_put(s, half, 3, to(minus, (0, HALF)), q2.at[s, half, 1], down)
            return
        rs_put(s, half, 2, to(opposite, A), q1.at[s, half, 0], up)
        rs_put(s, half, 2, to(opposite, B), q1.at[s, half, 1], down)
        rs_put(s, half, 3, to(plus, B), q2.at[s, half, 0, span(B), :], up)
        rs_put(s, half, 3, to(minus, A), q2.at[s, half, 1, span(A), :], down)

    def add_second(s, half):
        own, minus, plus, opposite = ends(half, 1)
        up, down = devices(half, 1)
        got(q1.at[s, half], rs_r.at[s, half, 2])
        for side, (a, rows, device) in enumerate(((plus, A, up), (minus, B, down))):
            view = s1.at[s, half, a, span(rows), :]
            view[...] = (view[...].astype(F32) + q1[s, half, side].astype(F32)).astype(BF)
            rs_put(s, half, 3, view, q2.at[s, half, side, span(rows), :], device)

    def finish(s, half):
        own, minus, plus, opposite = ends(half, 1)
        got(q2.at[s, half], rs_r.at[s, half, 3])
        rows, cols = pl.ds(half * HALF, HALF), pl.ds(s * HD, HD)
        total = (
            act[t, rows, cols].astype(F32)
            + s1[s, half, own].astype(F32)
            + q2[s, half, 0].astype(F32)
            + q2[s, half, 1].astype(F32)
        )
        if s in DIRECT:
            got(q1.at[s, half], rs_r.at[s, half, 2])
            total = total + q1[s, half].reshape(HALF, HD).astype(F32)
        out[rows, cols] = total.astype(BF)
        pltpu.make_async_copy(out.at[rows, cols], result.at[rows, cols], out_sem).start()

    ag_send(0, 0, 0, t, None)
    ag_send(1, 0, 0, t, None)
    ag2_send(0, 0)
    ag2_send(1, 0)
    x_hand_on(0)
    x_near(0, (1, 0))
    ag_near(0, 0, 0, 1, other(0))
    ag2_send(0, 1)
    ag2_send(0, 2)
    ag_near(1, 0, 0, 1, other(1))
    ag2_send(1, 1)
    ag2_send(1, 2)
    x_far(0, (1, 1))
    ag2_near(1, 0)
    ag2_near(0, 0)
    x_sibling(0)
    got(act.at[0, pl.ds(0 * HALF, HALF), :], ag_r.at[0, 1])
    ag2_send(0, 3)
    x_hand_on(1)
    ag2_near(0, 1)
    x_near(1, (2, 0))
    ag2_near(1, 1)
    ag2_near(0, 2)
    x_far(1, (2, 1))
    ag2_near(1, 2)
    got(act.at[0, pl.ds(1 * HALF, HALF), :], ag_r.at[1, 1])
    ag2_send(1, 3)
    x_sibling(1)
    x_hand_on(2)
    x_near(2, (3, 0))
    ag2_near(0, 3)
    x_far(2, (3, 1))
    ag2_near(1, 3)
    x_sibling(2)
    got(act.at[pl.ds(0, 4), pl.ds(0 * HALF, HALF), :], ag_r.at[0, 6])
    x_hand_on(3)
    got(act.at[pl.ds(0, 4), pl.ds(1 * HALF, HALF), :], ag_r.at[1, 6])
    loaded(gain, local_sem.at[3])
    acc[...] = jnp.zeros_like(acc)
    squares[...] = jnp.zeros_like(squares)

    @pl.loop(0, 16)
    def _(tt):
        rows = act[tt].astype(F32)
        power = rows * rows
        squares[...] += (power[:, :HD] + power[:, HD:2 * HD]) + (
            power[:, 2 * HD:3 * HD] + power[:, 3 * HD:]
        )
        scaled[tt] = (rows * gain[tt]).astype(BF)

    squares[:, :1] = lax.rsqrt(
        jnp.sum(squares[...], axis=1, keepdims=True) * (1.0 / (16 * WIDE)) + EPSILON
    )
    x_near(3, (4, 0))
    project(0, 0, WIDE + HD, range(8))
    project(1, 0, WIDE + HD, range(8))
    x_far(3, (4, 1))
    project(2, 0, WIDE + HD, range(8))
    x_sibling_near(3)
    project(3, 0, WIDE + HD, near_shards)
    x_hand_on(4)
    x_sibling_far(3)
    project(3, WIDE, HD, far_shards)
    loaded(cos, local_sem.at[4])
    loaded(sin, local_sem.at[5])

    @pl.loop(0, TAKEN, unroll=True)
    def _(n):
        rows = pl.ds(n * ITEM_LEN, ITEM_LEN)
        value = acc[rows, pl.ds(WIDE, HD)] * squares[rows, :1]
        kvown[rows, :] = jnp.where(parity == 0, rotated(value), value).astype(BF)

    put(kvown.at[pl.ds(0 * HALF, HALF), :], kvpart.at[pl.ds(0 * HALF, HALF), :], kv_s, kv_r.at[0], (me, t + 1 - 2 * parity))
    put(kvown.at[pl.ds(1 * HALF, HALF), :], kvpart.at[pl.ds(1 * HALF, HALF), :], kv_s, kv_r.at[1], (me, t + 1 - 2 * parity))
    project(3, 0, WIDE, far_shards)

    @pl.loop(0, TAKEN, unroll=True)
    def _(n):
        rows = pl.ds(n * ITEM_LEN, ITEM_LEN)
        inverse = squares[rows, :1]
        for h in range(4):
            value = acc[rows, pl.ds(h * HD, HD)] * inverse
            qs[n, pl.ds(h * ITEM_LEN, ITEM_LEN), :] = rotated(value).astype(BF)

    x_near(4, (5, 0))
    got(kvpart.at[pl.ds(0 * HALF, HALF), :], kv_r.at[0])

    @pl.loop(0, 3, unroll=True)
    def _(n):
        rows = pl.ds(n * ITEM_LEN, ITEM_LEN)
        mine, theirs = kvown[rows, :], kvpart[rows, :]
        keys = jnp.where(parity == 0, mine, theirs)
        values = jnp.where(parity == 0, theirs, mine)
        scores = lax.dot_general(
            qs[n], keys, (((1,), (1,)), ((), ())), preferred_element_type=F32
        ) * (HD ** -0.5)
        place = lax.broadcasted_iota(jnp.int32, scores.shape, 0) % ITEM_LEN
        scores = jnp.where(
            place >= lax.broadcasted_iota(jnp.int32, scores.shape, 1), scores, -1e30
        )
        raised = jnp.exp(scores - jnp.max(scores, axis=1, keepdims=True))
        probs = (raised * (1.0 / jnp.sum(raised, axis=1, keepdims=True))).astype(BF)
        context = jnp.dot(probs, values, preferred_element_type=F32).astype(BF)
        for h in range(4):
            ctx[rows, pl.ds(h * HD, HD)] = context[h * ITEM_LEN:(h + 1) * ITEM_LEN, :]

    got(kvpart.at[pl.ds(1 * HALF, HALF), :], kv_r.at[1])

    @pl.loop(3, 6, unroll=True)
    def _(n):
        rows = pl.ds(n * ITEM_LEN, ITEM_LEN)
        mine, theirs = kvown[rows, :], kvpart[rows, :]
        keys = jnp.where(parity == 0, mine, theirs)
        values = jnp.where(parity == 0, theirs, mine)
        scores = lax.dot_general(
            qs[n], keys, (((1,), (1,)), ((), ())), preferred_element_type=F32
        ) * (HD ** -0.5)
        place = lax.broadcasted_iota(jnp.int32, scores.shape, 0) % ITEM_LEN
        scores = jnp.where(
            place >= lax.broadcasted_iota(jnp.int32, scores.shape, 1), scores, -1e30
        )
        raised = jnp.exp(scores - jnp.max(scores, axis=1, keepdims=True))
        probs = (raised * (1.0 / jnp.sum(raised, axis=1, keepdims=True))).astype(BF)
        context = jnp.dot(probs, values, preferred_element_type=F32).astype(BF)
        for h in range(4):
            ctx[rows, pl.ds(h * HD, HD)] = context[h * ITEM_LEN:(h + 1) * ITEM_LEN, :]

    x_far(4, (5, 1))
    x_sibling_near(4)
    multiply(0, near_chips)
    x_sibling_far(4)
    multiply(0, far_chips)
    send_first(0)
    x_hand_on(5)
    x_near(5, (6, 0))
    add_first(0, 0)
    add_first(0, 1)
    x_far(5, (6, 1))
    x_sibling_near(5)
    multiply(1, near_chips)
    x_sibling_far(5)
    multiply(1, far_chips)
    send_first(1)
    x_hand_on(6)
    send_second(0, 0)
    send_second(0, 1)
    x_near(6, (7, 0))
    add_first(1, 0)
    add_first(1, 1)
    x_far(6, (7, 1))
    x_sibling_near(6)
    multiply(2, near_chips)
    add_second(0, 1)
    add_second(0, 0)
    x_sibling_far(6)
    multiply(2, far_chips)
    send_first(2)
    x_hand_on(7)
    send_second(1, 0)
    send_second(1, 1)
    finish(0, 0)
    finish(0, 1)
    x_near(7)
    add_first(2, 0)
    add_first(2, 1)
    x_far(7)
    x_sibling_near(7)
    multiply(3, near_chips)
    add_second(1, 1)
    add_second(1, 0)
    x_sibling_far(7)
    multiply(3, far_chips)
    send_first(3)
    finish(1, 0)
    finish(1, 1)
    add_first(3, 0)
    add_first(3, 1)
    send_second(2, 0)
    send_second(2, 1)
    send_second(3, 0)
    send_second(3, 1)
    add_second(2, 1)
    add_second(2, 0)
    finish(2, 0)
    finish(2, 1)
    finish(3, 0)
    finish(3, 1)

    sent(meta.at[pl.ds(0, 7)], meta_s)
    sent(outgoing.at[pl.ds(0, 7)], route_s)
    sent(wbuf.at[pl.ds(0, 7)], x_s.at[0])
    sent(obuf.at[:, pl.ds(0, 7)], x_s.at[1])
    sent(act.at[pl.ds(0, 15)], ag_s)
    sent(kvown, kv_s)
    sent(part.reshape(64, ROWS, HD).at[pl.ds(0, 60)], rs_s)
    loaded(out, out_sem)


def shards(hidden, exited, destination, norm_gain, query_weight, keyvalue_weight, output_weight):
    cos, sin = tables()
    hbm = pl.BlockSpec(memory_space=pl.ANY)
    dma = pltpu.SemaphoreType.DMA
    return pl.pallas_call(
        kernel,
        out_shape=jax.ShapeDtypeStruct((ROWS, WIDE), BF),
        in_specs=[hbm, hbm, hbm, hbm, hbm, hbm, hbm, hbm, hbm],
        out_specs=hbm,
        scratch_shapes=[
            pltpu.SMEM((HERE,), jnp.int32),
            pltpu.SMEM((HERE,), jnp.int32),
            pltpu.VMEM((16, 1, WIDE), F32),
            pltpu.VMEM((ITEM_LEN, HD), F32),
            pltpu.VMEM((ITEM_LEN, HD), F32),
            pltpu.VMEM((ROWS, WIDE), BF),
            pltpu.VMEM((HERE, ITEM_LEN, WIDE), BF),
            pltpu.VMEM((8, 2, ITEM_LEN, WIDE), BF),
            pltpu.VMEM((8, 2, ITEM_LEN, WIDE), BF),
            pltpu.VMEM((8, 8, 128), jnp.int32),
            pltpu.SMEM((8, 8, 128), jnp.int32),
            pltpu.VMEM((16, ROWS, WIDE), BF),
            pltpu.VMEM((16, ROWS, WIDE), BF),
            pltpu.VMEM((8, DEPTH, WIDE + HD), BF),
            pltpu.VMEM((4, 8, WIDE, 2 * HD), BF),
            pltpu.VMEM((ROWS, WIDE + HD), F32),
            pltpu.VMEM((ROWS, HD), F32),
            pltpu.VMEM((TAKEN, 4 * ITEM_LEN, HD), BF),
            pltpu.VMEM((ROWS, HD), BF),
            pltpu.VMEM((ROWS, HD), BF),
            pltpu.VMEM((ROWS, WIDE), BF),
            pltpu.VMEM((4, 4, 4, ROWS, HD), BF),
            pltpu.VMEM((4, 2, 2, 4, QUARTER, HD), BF),
            pltpu.VMEM((4, 2, 2, 4, HALF, HD), BF),
            pltpu.VMEM((4, 2, 4, HALF, HD), BF),
            pltpu.VMEM((4, 2, 2, QUARTER, HD), BF),
            pltpu.VMEM((4, 2, 2, HALF, HD), BF),
            dma((9,)),
            dma(()),
            dma(()),
            dma(()),
            dma(()),
            dma(()),
            dma((2,)),
            dma((8, 5)),
            dma(()),
            dma((2, 7)),
            dma(()),
            dma((4, 2, 4)),
            dma(()),
            dma((2,)),
        ],
        compiler_params=pltpu.CompilerParams(
            collective_id=0, has_side_effects=True, vmem_limit_bytes=60 * 1024 * 1024
        ),
        cost_estimate=pl.CostEstimate(
            flops=2 * ROWS * 16 * WIDE * (2 * WIDE + HD),
            bytes_accessed=8 * 1024 * 1024,
            transcendentals=ROWS * 4 * ITEM_LEN,
        ),
    )(
        exited,
        destination,
        hidden.reshape(HERE, ITEM_LEN, WIDE),
        norm_gain.reshape(16, 1, WIDE),
        query_weight,
        keyvalue_weight,
        output_weight,
        jnp.asarray(cos),
        jnp.asarray(sin),
    )


def solution(mesh):
    placed = (
        P("dp", "tensor"),
        P("dp"),
        P("dp"),
        P(),
        P("dp", "tensor"),
        P("dp", "tensor"),
        P("tensor", "dp"),
    )
    return jax.shard_map(
        shards, mesh=mesh, in_specs=placed, out_specs=P("dp", "tensor"), check_vma=False
    )
```

```python
import functools

import jax
import jax.numpy as jnp
import numpy as np
from jax import lax
from jax.experimental import pallas as pl
from jax.experimental.pallas import tpu as pltpu
from jax.sharding import PartitionSpec as P

MESH = pl.DeviceIdType.MESH

HD = 128
ITEM_LEN = 64
HERE = 16
TAKEN = 6
ROWS = TAKEN * ITEM_LEN
WIDE = 512
DEPTH = 1024
EPSILON = 1e-05
THETA = 500000.0
BF = jnp.bfloat16
F32 = jnp.float32

PIECE = DEPTH // 4
HALF = ROWS // 2
QUARTER = ROWS // 4
DIRECT = (3,)


def tables():
    j = np.arange(HD // 2, dtype=np.float64)
    freq = (THETA ** (-2.0 * j / HD)).astype(np.float32)
    phase = (np.arange(ITEM_LEN, dtype=np.float32)[:, None] * freq).astype(np.float64)
    cos, sin = np.cos(phase), np.sin(phase)
    return (
        np.concatenate([cos, cos], axis=1).astype(np.float32),
        np.concatenate([-sin, sin], axis=1).astype(np.float32),
    )


def kernel(
    exited_in, destination_in, hidden, gain_in, wq, wkv, wo, cos_in, sin_in, result,
    exited, destination, gain, cos, sin, out,
    hid, outgoing, arrived, meta, meta_scalar, act, scaled, wbuf, obuf, acc, squares, qs, kvown, kvpart,
    ctx, part, r1, r2, s1, q1, q2,
    local_sem, out_sem, meta_s, meta_r, route_s, route_r, x_s, x_r, ag_s, ag_r, rs_s, rs_r, kv_s, kv_r,
):
    me = lax.axis_index("dp")
    t = lax.axis_index("tensor")
    x, c = me // 2, me % 2
    z, y = t // 4, t % 4
    left = ((x + 3) % 4) * 2 + c
    right = ((x + 1) % 4) * 2 + c
    far = ((x + 2) % 4) * 2 + c
    zp, zm, zf = (z + 1) % 4, (z + 3) % 4, (z + 2) % 4
    yp, ym, yf = (y + 1) % 4, (y + 3) % 4, (y + 2) % 4

    def sibling(i):
        return i + 1 - 2 * c

    sib = sibling(me)

    def put(src, dst, send, recv, device):
        copy = pltpu.make_async_remote_copy(
            src_ref=src, dst_ref=dst, send_sem=send, recv_sem=recv,
            device_id=device, device_id_type=MESH,
        )
        copy.start()

    def got(dst, recv):
        pltpu.make_async_remote_copy(
            src_ref=dst, dst_ref=dst, send_sem=recv, recv_sem=recv,
            device_id=(sib, t), device_id_type=MESH,
        ).wait_recv()

    def sent(src, send):
        pltpu.make_async_remote_copy(
            src_ref=src, dst_ref=src, send_sem=send, recv_sem=send,
            device_id=(sib, t), device_id_type=MESH,
        ).wait_send()

    def loaded(dst, sem):
        pltpu.make_async_copy(dst, dst, sem).wait()

    barrier = pltpu.get_barrier_semaphore()
    peers = [((me + k) % 8, t) for k in (4, 3, 5, 2, 6, 1, 7)]
    peers += [(me, zf * 4 + y), (me, z * 4 + yf)]
    peers += [(me, zp * 4 + y), (me, zm * 4 + y), (me, z * 4 + yp), (me, z * 4 + ym)]
    for peer in peers:
        pl.semaphore_signal(barrier, inc=1, device_id=peer, device_id_type=MESH)

    flags = [
        pltpu.make_async_copy(exited_in, exited, local_sem.at[7]),
        pltpu.make_async_copy(destination_in, destination, local_sem.at[8]),
    ]
    for flag in flags:
        flag.start()
    loads = [pltpu.make_async_copy(hidden, hid, local_sem.at[0])]
    loads.append(pltpu.make_async_copy(wq, wbuf.at[me, :, pl.ds(0, WIDE)], local_sem.at[1]))
    loads.append(pltpu.make_async_copy(wkv, wbuf.at[me, :, pl.ds(WIDE, HD)], local_sem.at[1]))
    for s in range(4):
        for h in range(2):
            loads.append(
                pltpu.make_async_copy(
                    wo.at[:, pl.ds(h * WIDE + s * HD, HD)],
                    obuf.at[s, me, :, pl.ds(h * HD, HD)],
                    local_sem.at[2],
                )
            )
    loads.append(pltpu.make_async_copy(gain_in, gain, local_sem.at[3]))
    loads.append(pltpu.make_async_copy(cos_in, cos, local_sem.at[4]))
    loads.append(pltpu.make_async_copy(sin_in, sin, local_sem.at[5]))
    for load in loads:
        load.start()

    def weights(r, i, low=0, count=None):
        if r < 4:
            return wbuf.at[i, pl.ds(r * PIECE + low, count or PIECE), :]
        return obuf.at[r - 4, i, pl.ds(low, count or WIDE), :]

    def half_of(r):
        return PIECE // 2 if r < 4 else WIDE // 2

    def x_put(r, k, view, device):
        put(view, view, x_s.at[r], x_r.at[r, k], (device, t))

    def shares(r, count):
        if r < 4:
            return wbuf.at[pl.ds(0, count), pl.ds(r * PIECE, PIECE), :]
        return obuf.at[r - 4, pl.ds(0, count)]

    def x_own_sibling(r):
        x_put(r, 3, weights(r, me), sib)

    def x_own(r, which):
        n = half_of(r)
        x_put(r, which, weights(r, me, which * n, n), right)
        x_put(r, which, weights(r, me, n - which * n, n), left)

    def x_hand_on(r):
        n = half_of(r)
        got(shares(r, 1), x_r.at[r, 0])
        x_put(r, 2, weights(r, left, 0, n), right)
        x_put(r, 2, weights(r, right, n, n), left)

    def x_near(r, *after):
        got(shares(r, 1), x_r.at[r, 1])
        for piece in after:
            x_own(*piece)
        x_put(r, 3, weights(r, left), sib)
        x_put(r, 3, weights(r, right), sib)

    def x_far(r, *after):
        got(shares(r, 1), x_r.at[r, 2])
        for piece in after:
            x_own(*piece)
        x_put(r, 4, weights(r, far), sib)

    def x_sibling_near(r):
        got(shares(r, 3), x_r.at[r, 3])

    def x_sibling_far(r):
        got(shares(r, 1), x_r.at[r, 4])

    def x_sibling(r):
        x_sibling_near(r)
        x_sibling_far(r)

    for flag in flags:
        flag.wait()
    codes = [jnp.where(exited[k] == 0, destination[k], -1) for k in range(HERE)]
    lane = lax.broadcasted_iota(jnp.int32, (8, 128), 1)
    row = jnp.full((8, 128), -1, jnp.int32)
    for k in range(HERE):
        row = jnp.where(lane == k, codes[k], row)
    meta[me] = row
    loads[0].wait()
    for k in range(8):
        dest = (me + k) % 8 if k else me
        seen = jnp.int32(0)
        first = jnp.int32(0)
        second = jnp.int32(0)
        for item in range(HERE):
            hit = codes[item] == dest
            first = jnp.where(hit & (seen == 0), item, first)
            second = jnp.where(hit & (seen == 1), item, second)
            seen = seen + jnp.where(hit, 1, 0)
        if k:
            outgoing[dest, 0] = hid[first]
            outgoing[dest, 1] = hid[second]
        else:
            arrived[me, 0] = hid[first]
            arrived[me, 1] = hid[second]
    loaded(wbuf.at[me], local_sem.at[1])
    pl.semaphore_wait(barrier, len(peers))

    for k in range(1, 8):
        put(meta.at[me], meta.at[me], meta_s, meta_r, ((me + k) % 8, t))
    for k in (4, 2, 6, 3, 5, 1, 7):
        put(outgoing.at[(me + k) % 8], arrived.at[me], route_s, route_r, ((me + k) % 8, t))
    x_own(0, 0)
    x_own(0, 1)
    for r in range(4):
        x_own_sibling(r)
    loaded(obuf.at[pl.ds(0, 4), me], local_sem.at[2])
    for r in range(4, 8):
        x_own_sibling(r)

    got(meta.at[pl.ds(0, 7)], meta_r)
    to_scalar = pltpu.make_async_copy(meta, meta_scalar, local_sem.at[6])
    to_scalar.start()
    to_scalar.wait()
    picks = [jnp.int32(0)] * TAKEN
    rank = jnp.int32(0)
    for j in range(8):
        count = jnp.int32(0)
        for item in range(HERE):
            count = count + jnp.where(meta_scalar[j, 0, item] == me, 1, 0)
        for s in range(2):
            valid = count > s
            for r in range(TAKEN):
                picks[r] = jnp.where(valid & (rank == r), 2 * j + s, picks[r])
            rank = rank + jnp.where(valid, 1, 0)

    got(arrived.at[pl.ds(0, 7)], route_r)
    flat = arrived.reshape(16, ITEM_LEN, WIDE)
    for r in range(TAKEN):
        act[t, pl.ds(r * ITEM_LEN, ITEM_LEN), :] = flat[picks[r]]

    def line(half, phase):
        along_z = (half == 0) == (phase == 0)
        if along_z:
            return (z, zm, zp, zf), lambda a, b: a * 4 + b
        return (y, ym, yp, yf), lambda a, b: b * 4 + a

    def chunk(tt, half, low=0, count=HALF):
        return act.at[tt, pl.ds(half * HALF + low, count), :]

    def ag_put(half, k, view, device):
        put(view, view, ag_s.at[half], ag_r.at[half, k], (me, device))

    def other(half):
        return y if half == 0 else z

    def ag_send(half, phase, slot, tt, near):
        (own, minus, plus, opposite), at = line(half, phase)
        place = other(half) if phase == 0 else near
        ag_put(half, slot, chunk(tt, half), at(plus, place))
        ag_put(half, slot, chunk(tt, half), at(minus, place))

    def ag_near(half, phase, slot, far_slot, place):
        (own, minus, plus, opposite), at = line(half, phase)
        got(act.at[pl.ds(0, 2), pl.ds(half * HALF, HALF), :], ag_r.at[half, slot])
        q = HALF // 2
        here = other(half) if phase == 0 else (z if half == 0 else y)
        ag_put(half, far_slot, chunk(at(minus, place), half, 0, q), at(plus, here))
        ag_put(half, far_slot, chunk(at(plus, place), half, q, q), at(minus, here))

    def places(half):
        return (z, zm, zp, zf) if half == 0 else (y, ym, yp, yf)

    def first_at(half, a):
        return a * 4 + y if half == 0 else z * 4 + a

    def ag2_send(half, n):
        a = places(half)[n]
        ag_send(half, 1, 2 + n, first_at(half, a), places(half)[0])

    def ag2_near(half, n):
        ag_near(half, 1, 2 + n, 6, places(half)[n])

    def rotated(value):
        return value * cos[...] + pltpu.roll(value, HD // 2, 1) * sin[...]

    parity = t % 2

    near_chips, far_chips = [x, (x + 3) % 4, (x + 1) % 4], [(x + 2) % 4]
    near_shards = [2 * chip + b for chip in near_chips for b in range(2)]
    far_shards = [2 * chip + b for chip in far_chips for b in range(2)]

    def project(p, low, count, shards):
        term = None
        for i in shards:
            product = jnp.dot(
                scaled[2 * i + p // 2, :, pl.ds((p % 2) * PIECE, PIECE)],
                wbuf[i, pl.ds(p * PIECE, PIECE), pl.ds(low, count)],
                preferred_element_type=F32,
            )
            term = product if term is None else term + product
        acc[:, pl.ds(low, count)] += term

    def multiply(s, chips):
        for chip in chips:
            for b in range(2):
                term = jnp.dot(
                    ctx[...], obuf[s, 2 * chip + b], preferred_element_type=F32
                ).astype(BF)
                part[s, chip, 2 * b] = term[:, :HD]
                part[s, chip, 2 * b + 1] = term[:, HD:]

    def rs_put(s, half, k, src, dst, device):
        put(src, dst, rs_s.at[s, half], rs_r.at[s, half, k], (me, device))

    A = (0, QUARTER)
    B = (QUARTER, QUARTER)

    def block(s, half, a, rows):
        low, count = rows
        span = pl.ds(half * HALF + low, count)
        if half == 0:
            return part.at[s, a, :, span, :]
        return part.at[s, :, a, span, :]

    def devices(half, phase):
        if (half == 0) == (phase == 0):
            return zp * 4 + y, zm * 4 + y
        return z * 4 + yp, z * 4 + ym

    def ends(half, phase):
        if (half == 0) == (phase == 0):
            return z, zm, zp, zf
        return y, ym, yp, yf

    def span(rows):
        return pl.ds(rows[0], rows[1])

    def send_first(s):
        for half in range(2):
            own, minus, plus, opposite = ends(half, 0)
            up, down = devices(half, 0)
            rs_put(s, half, 0, block(s, half, opposite, A), r1.at[s, half, 0], up)
            rs_put(s, half, 0, block(s, half, opposite, B), r1.at[s, half, 1], down)
        for half in range(2):
            own, minus, plus, opposite = ends(half, 0)
            up, down = devices(half, 0)
            rs_put(s, half, 1, block(s, half, plus, B), r2.at[s, half, 0, :, span(B), :], up)
            rs_put(s, half, 1, block(s, half, minus, A), r2.at[s, half, 1, :, span(A), :], down)

    def add_first(s, half):
        own, minus, plus, opposite = ends(half, 0)
        up, down = devices(half, 0)
        got(r1.at[s, half], rs_r.at[s, half, 0])
        for side, (a, rows, device) in enumerate(((plus, A, up), (minus, B, down))):
            view = block(s, half, a, rows)
            view[...] = (view[...].astype(F32) + r1[s, half, side].astype(F32)).astype(BF)
            rs_put(s, half, 1, view, r2.at[s, half, side, :, span(rows), :], device)

    def send_second(s, half):
        own, minus, plus, opposite = ends(half, 0)
        got(r2.at[s, half], rs_r.at[s, half, 1])
        view = block(s, half, own, (0, HALF))
        s1[s, half] = (
            view[...].astype(F32) + r2[s, half, 0].astype(F32) + r2[s, half, 1].astype(F32)
        ).astype(BF)
        own, minus, plus, opposite = ends(half, 1)
        up, down = devices(half, 1)
        to = lambda a, rows: s1.at[s, half, a, span(rows), :]
        if s in DIRECT:
            across = zf * 4 + y if half else z * 4 + yf
            rs_put(s, half, 2, to(opposite, A), q1.at[s, half, 0], across)
            rs_put(s, half, 2, to(opposite, B), q1.at[s, half, 1], across)
            rs_put(s, half, 3, to(plus, (0, HALF)), q2.at[s, half, 0], up)
            rs_put(s, half, 3, to(minus, (0, HALF)), q2.at[s, half, 1], down)
            return
        rs_put(s, half, 2, to(opposite, A), q1.at[s, half, 0], up)
        rs_put(s, half, 2, to(opposite, B), q1.at[s, half, 1], down)
        rs_put(s, half, 3, to(plus, B), q2.at[s, half, 0, span(B), :], up)
        rs_put(s, half, 3, to(minus, A), q2.at[s, half, 1, span(A), :], down)

    def add_second(s, half):
        own, minus, plus, opposite = ends(half, 1)
        up, down = devices(half, 1)
        got(q1.at[s, half], rs_r.at[s, half, 2])
        for side, (a, rows, device) in enumerate(((plus, A, up), (minus, B, down))):
            view = s1.at[s, half, a, span(rows), :]
            view[...] = (view[...].astype(F32) + q1[s, half, side].astype(F32)).astype(BF)
            rs_put(s, half, 3, view, q2.at[s, half, side, span(rows), :], device)

    def finish(s, half):
        own, minus, plus, opposite = ends(half, 1)
        got(q2.at[s, half], rs_r.at[s, half, 3])
        rows, cols = pl.ds(half * HALF, HALF), pl.ds(s * HD, HD)
        total = (
            act[t, rows, cols].astype(F32)
            + s1[s, half, own].astype(F32)
            + q2[s, half, 0].astype(F32)
            + q2[s, half, 1].astype(F32)
        )
        if s in DIRECT:
            got(q1.at[s, half], rs_r.at[s, half, 2])
            total = total + q1[s, half].reshape(HALF, HD).astype(F32)
        out[rows, cols] = total.astype(BF)
        pltpu.make_async_copy(out.at[rows, cols], result.at[rows, cols], out_sem).start()

    ag_send(0, 0, 0, t, None)
    ag_send(1, 0, 0, t, None)
    ag2_send(0, 0)
    ag2_send(1, 0)
    x_hand_on(0)
    x_near(0, (1, 0))
    ag_near(0, 0, 0, 1, other(0))
    ag2_send(0, 1)
    ag2_send(0, 2)
    ag_near(1, 0, 0, 1, other(1))
    ag2_send(1, 1)
    ag2_send(1, 2)
    x_far(0, (1, 1))
    ag2_near(1, 0)
    ag2_near(0, 0)
    x_sibling(0)
    got(act.at[0, pl.ds(0 * HALF, HALF), :], ag_r.at[0, 1])
    ag2_send(0, 3)
    x_hand_on(1)
    ag2_near(0, 1)
    x_near(1, (2, 0))
    ag2_near(1, 1)
    ag2_near(0, 2)
    x_far(1, (2, 1))
    ag2_near(1, 2)
    got(act.at[0, pl.ds(1 * HALF, HALF), :], ag_r.at[1, 1])
    ag2_send(1, 3)
    x_sibling(1)
    x_hand_on(2)
    x_near(2, (3, 0))
    ag2_near(0, 3)
    x_far(2, (3, 1))
    ag2_near(1, 3)
    x_sibling(2)
    got(act.at[pl.ds(0, 4), pl.ds(0 * HALF, HALF), :], ag_r.at[0, 6])
    x_hand_on(3)
    got(act.at[pl.ds(0, 4), pl.ds(1 * HALF, HALF), :], ag_r.at[1, 6])
    loaded(gain, local_sem.at[3])
    acc[...] = jnp.zeros_like(acc)
    squares[...] = jnp.zeros_like(squares)

    @pl.loop(0, 16)
    def _(tt):
        rows = act[tt].astype(F32)
        power = rows * rows
        squares[...] += (power[:, :HD] + power[:, HD:2 * HD]) + (
            power[:, 2 * HD:3 * HD] + power[:, 3 * HD:]
        )
        scaled[tt] = (rows * gain[tt]).astype(BF)

    squares[:, :1] = lax.rsqrt(
        jnp.sum(squares[...], axis=1, keepdims=True) * (1.0 / (16 * WIDE)) + EPSILON
    )
    x_near(3, (4, 0))
    project(0, 0, WIDE + HD, range(8))
    project(1, 0, WIDE + HD, range(8))
    x_far(3, (4, 1))
    project(2, 0, WIDE + HD, range(8))
    x_sibling_near(3)
    project(3, 0, WIDE + HD, near_shards)
    x_hand_on(4)
    x_sibling_far(3)
    project(3, WIDE, HD, far_shards)
    loaded(cos, local_sem.at[4])
    loaded(sin, local_sem.at[5])

    @pl.loop(0, TAKEN, unroll=True)
    def _(n):
        rows = pl.ds(n * ITEM_LEN, ITEM_LEN)
        value = acc[rows, pl.ds(WIDE, HD)] * squares[rows, :1]
        kvown[rows, :] = jnp.where(parity == 0, rotated(value), value).astype(BF)

    put(kvown.at[pl.ds(0 * HALF, HALF), :], kvpart.at[pl.ds(0 * HALF, HALF), :], kv_s, kv_r.at[0], (me, t + 1 - 2 * parity))
    put(kvown.at[pl.ds(1 * HALF, HALF), :], kvpart.at[pl.ds(1 * HALF, HALF), :], kv_s, kv_r.at[1], (me, t + 1 - 2 * parity))
    project(3, 0, WIDE, far_shards)

    @pl.loop(0, TAKEN, unroll=True)
    def _(n):
        rows = pl.ds(n * ITEM_LEN, ITEM_LEN)
        inverse = squares[rows, :1]
        for h in range(4):
            value = acc[rows, pl.ds(h * HD, HD)] * inverse
            qs[n, pl.ds(h * ITEM_LEN, ITEM_LEN), :] = rotated(value).astype(BF)

    x_near(4, (5, 0))
    got(kvpart.at[pl.ds(0 * HALF, HALF), :], kv_r.at[0])

    @pl.loop(0, 3, unroll=True)
    def _(n):
        rows = pl.ds(n * ITEM_LEN, ITEM_LEN)
        mine, theirs = kvown[rows, :], kvpart[rows, :]
        keys = jnp.where(parity == 0, mine, theirs)
        values = jnp.where(parity == 0, theirs, mine)
        scores = lax.dot_general(
            qs[n], keys, (((1,), (1,)), ((), ())), preferred_element_type=F32
        ) * (HD ** -0.5)
        place = lax.broadcasted_iota(jnp.int32, scores.shape, 0) % ITEM_LEN
        scores = jnp.where(
            place >= lax.broadcasted_iota(jnp.int32, scores.shape, 1), scores, -1e30
        )
        raised = jnp.exp(scores - jnp.max(scores, axis=1, keepdims=True))
        probs = (raised * (1.0 / jnp.sum(raised, axis=1, keepdims=True))).astype(BF)
        context = jnp.dot(probs, values, preferred_element_type=F32).astype(BF)
        for h in range(4):
            ctx[rows, pl.ds(h * HD, HD)] = context[h * ITEM_LEN:(h + 1) * ITEM_LEN, :]

    got(kvpart.at[pl.ds(1 * HALF, HALF), :], kv_r.at[1])

    @pl.loop(3, 6, unroll=True)
    def _(n):
        rows = pl.ds(n * ITEM_LEN, ITEM_LEN)
        mine, theirs = kvown[rows, :], kvpart[rows, :]
        keys = jnp.where(parity == 0, mine, theirs)
        values = jnp.where(parity == 0, theirs, mine)
        scores = lax.dot_general(
            qs[n], keys, (((1,), (1,)), ((), ())), preferred_element_type=F32
        ) * (HD ** -0.5)
        place = lax.broadcasted_iota(jnp.int32, scores.shape, 0) % ITEM_LEN
        scores = jnp.where(
            place >= lax.broadcasted_iota(jnp.int32, scores.shape, 1), scores, -1e30
        )
        raised = jnp.exp(scores - jnp.max(scores, axis=1, keepdims=True))
        probs = (raised * (1.0 / jnp.sum(raised, axis=1, keepdims=True))).astype(BF)
        context = jnp.dot(probs, values, preferred_element_type=F32).astype(BF)
        for h in range(4):
            ctx[rows, pl.ds(h * HD, HD)] = context[h * ITEM_LEN:(h + 1) * ITEM_LEN, :]

    x_far(4, (5, 1))
    x_sibling_near(4)
    multiply(0, near_chips)
    x_sibling_far(4)
    multiply(0, far_chips)
    send_first(0)
    x_hand_on(5)
    x_near(5, (6, 0))
    add_first(0, 0)
    add_first(0, 1)
    x_far(5, (6, 1))
    x_sibling_near(5)
    multiply(1, near_chips)
    x_sibling_far(5)
    multiply(1, far_chips)
    send_first(1)
    x_hand_on(6)
    send_second(0, 0)
    send_second(0, 1)
    x_near(6, (7, 0))
    add_first(1, 0)
    add_first(1, 1)
    x_far(6, (7, 1))
    x_sibling_near(6)
    multiply(2, near_chips)
    add_second(0, 1)
    add_second(0, 0)
    x_sibling_far(6)
    multiply(2, far_chips)
    send_first(2)
    x_hand_on(7)
    send_second(1, 0)
    send_second(1, 1)
    finish(0, 0)
    finish(0, 1)
    x_near(7)
    add_first(2, 0)
    add_first(2, 1)
    x_far(7)
    x_sibling_near(7)
    multiply(3, near_chips)
    add_second(1, 1)
    add_second(1, 0)
    x_sibling_far(7)
    multiply(3, far_chips)
    send_first(3)
    finish(1, 0)
    finish(1, 1)
    add_first(3, 0)
    add_first(3, 1)
    send_second(2, 0)
    send_second(2, 1)
    send_second(3, 0)
    send_second(3, 1)
    add_second(2, 1)
    add_second(2, 0)
    finish(2, 0)
    finish(2, 1)
    finish(3, 0)
    finish(3, 1)

    sent(meta.at[pl.ds(0, 7)], meta_s)
    sent(outgoing.at[pl.ds(0, 7)], route_s)
    for r in range(8):
        sent(shares(r, 7), x_s.at[r])
    for half in range(2):
        sent(act.at[pl.ds(0, 15), pl.ds(half * HALF, HALF), :], ag_s.at[half])
    sent(kvown, kv_s)
    terms = part.reshape(64, ROWS, HD)
    for s in range(4):
        for half in range(2):
            sent(terms.at[pl.ds(16 * s, 15), pl.ds(0, HALF), :], rs_s.at[s, half])
    loaded(out, out_sem)


def shards(hidden, exited, destination, norm_gain, query_weight, keyvalue_weight, output_weight):
    cos, sin = tables()
    hbm = pl.BlockSpec(memory_space=pl.ANY)
    dma = pltpu.SemaphoreType.DMA
    return pl.pallas_call(
        kernel,
        out_shape=jax.ShapeDtypeStruct((ROWS, WIDE), BF),
        in_specs=[hbm, hbm, hbm, hbm, hbm, hbm, hbm, hbm, hbm],
        out_specs=hbm,
        scratch_shapes=[
            pltpu.SMEM((HERE,), jnp.int32),
            pltpu.SMEM((HERE,), jnp.int32),
            pltpu.VMEM((16, 1, WIDE), F32),
            pltpu.VMEM((ITEM_LEN, HD), F32),
            pltpu.VMEM((ITEM_LEN, HD), F32),
            pltpu.VMEM((ROWS, WIDE), BF),
            pltpu.VMEM((HERE, ITEM_LEN, WIDE), BF),
            pltpu.VMEM((8, 2, ITEM_LEN, WIDE), BF),
            pltpu.VMEM((8, 2, ITEM_LEN, WIDE), BF),
            pltpu.VMEM((8, 8, 128), jnp.int32),
            pltpu.SMEM((8, 8, 128), jnp.int32),
            pltpu.VMEM((16, ROWS, WIDE), BF),
            pltpu.VMEM((16, ROWS, WIDE), BF),
            pltpu.VMEM((8, DEPTH, WIDE + HD), BF),
            pltpu.VMEM((4, 8, WIDE, 2 * HD), BF),
            pltpu.VMEM((ROWS, WIDE + HD), F32),
            pltpu.VMEM((ROWS, HD), F32),
            pltpu.VMEM((TAKEN, 4 * ITEM_LEN, HD), BF),
            pltpu.VMEM((ROWS, HD), BF),
            pltpu.VMEM((ROWS, HD), BF),
            pltpu.VMEM((ROWS, WIDE), BF),
            pltpu.VMEM((4, 4, 4, ROWS, HD), BF),
            pltpu.VMEM((4, 2, 2, 4, QUARTER, HD), BF),
            pltpu.VMEM((4, 2, 2, 4, HALF, HD), BF),
            pltpu.VMEM((4, 2, 4, HALF, HD), BF),
            pltpu.VMEM((4, 2, 2, QUARTER, HD), BF),
            pltpu.VMEM((4, 2, 2, HALF, HD), BF),
            dma((9,)),
            dma(()),
            dma(()),
            dma(()),
            dma(()),
            dma(()),
            dma((8,)),
            dma((8, 5)),
            dma((2,)),
            dma((2, 7)),
            dma((4, 2)),
            dma((4, 2, 4)),
            dma(()),
            dma((2,)),
        ],
        compiler_params=pltpu.CompilerParams(
            collective_id=0, has_side_effects=True, vmem_limit_bytes=60 * 1024 * 1024
        ),
        cost_estimate=pl.CostEstimate(
            flops=2 * ROWS * 16 * WIDE * (2 * WIDE + HD),
            bytes_accessed=8 * 1024 * 1024,
            transcendentals=ROWS * 4 * ITEM_LEN,
        ),
    )(
        exited,
        destination,
        hidden.reshape(HERE, ITEM_LEN, WIDE),
        norm_gain.reshape(16, 1, WIDE),
        query_weight,
        keyvalue_weight,
        output_weight,
        jnp.asarray(cos),
        jnp.asarray(sin),
    )


def solution(mesh):
    placed = (
        P("dp", "tensor"),
        P("dp"),
        P("dp"),
        P(),
        P("dp", "tensor"),
        P("dp", "tensor"),
        P("tensor", "dp"),
    )
    return jax.shard_map(
        shards, mesh=mesh, in_specs=placed, out_specs=P("dp", "tensor"), check_vma=False
    )
```
